256 devices in a mesh: dp: 64 (over z, y, core), mp: 4 (over x).
Axes of the slice: x: 4, y: 4, z: 8, core: 2. Of those that a mesh axis runs over, the one named last changes fastest.
Arguments:
- texts: bfloat16 [1024, 35, 768], P('dp'), may hold values from -6 to 6
- query_weight: bfloat16 [768, 768], P('mp'), may hold values from -0.21875 to 0.21875
- patch_key_value: bfloat16 [256, 12, 577, 128], P('dp', 'mp'), may hold values from -300 to 300
- grad_out: bfloat16 [1024, 4, 35, 768], P('dp'), may hold values from -6 to 6
- negatives: int32 [1024, 3], P('dp'), may hold values from 0 to 255, as said below
Outputs:
- text_grad: bfloat16 [1024, 35, 768], P(('dp', 'mp'))
- weight_grad: float32 [768, 768], P('mp')
- key_value_grad: bfloat16 [256, 12, 577, 128], P('dp', 'mp')
The draws below stay inside these ranges and needn't reach their ends.
Inputs may be any that keep to these rules, and one draw needn't show every extreme that they name: Never an image whose index // 4 equals the text's index // 16. Among the negatives of the texts of one index of dp, at most 2 name images of any one index; some pair of indices reaches 2.
All inputs are finite; a program needn't handle non-finite values.
Results may differ from the reference program's by a relative error of at most 0.03.
The reference program's roundings to bfloat16 on the way (of `query`, `probs`, `dscores` and `dquery`) count: a program that leaves them out, or rounds other values in their place, can miss the bound.
Values may be sent and summed in bfloat16 or wider, within the bound.
No kernel may reach another device: no remote copies, remote signals or barrier semaphores. Data moves between devices by JAX's collectives and lax.ppermute only.
A program may use at most 192 MiB of HBM per device.

```python
import jax
import jax.numpy as jnp
from jax import lax

D = 768
HEAD_SIZE = 64
HEADS = 12
PATCHES = 577
TEXT_LEN = 35
NEG = 3
CAPS = 4
IMG_DEV = 4
TXT_DEV = 16
SLOTS = 4
CAP = 2
TEXTS = 1024
IMAGES = 256
N_DP = 64


def draw_negatives(key, part):
    key = jax.random.fold_in(key, 7)
    k_rank, k_noise, k_first, k_second, k_order = jax.random.split(key, 5)
    owning_devices = N_DP
    width = owning_devices * CAP
    wanted = NEG * TXT_DEV
    image_frequency = jax.random.permutation(k_rank, owning_devices).astype(jnp.int32)
    extra_score = (owning_devices - image_frequency) * 16 + jnp.where(image_frequency == 0, 1 << 20, 0)
    random_perturb = jax.random.randint(k_noise, (owning_devices, owning_devices, CAP), 0, 1024, dtype=jnp.int32)
    match_score = random_perturb + extra_score[None, :, None]
    sender = jnp.arange(owning_devices, dtype=jnp.int32)
    match_score = jnp.where((sender[:, None] == sender[None, :])[:, :, None], -1, match_score)
    match_score = match_score.reshape(owning_devices, width) * width + jnp.arange(width, dtype=jnp.int32)[None, :]
    _, picked = lax.top_k(match_score, wanted)
    owner = picked.astype(jnp.int32) // CAP
    first = jax.random.randint(k_first, (owning_devices, wanted), 0, IMG_DEV, dtype=jnp.int32)
    second = jax.random.randint(k_second, (owning_devices, wanted), 0, IMG_DEV, dtype=jnp.int32)
    image = owner * IMG_DEV + jnp.minimum(first, second)
    order_keys = jax.random.split(k_order, owning_devices)
    orders = jax.vmap(lambda k: jax.random.permutation(k, wanted))(order_keys).astype(jnp.int32)
    image = jnp.take_along_axis(image, orders, axis=1)
    return image.reshape(owning_devices * TXT_DEV, NEG).astype(jnp.int32)


def draw_patch_key_value(key, part):
    key = jax.random.fold_in(key, 3)
    k_base = jax.random.fold_in(key, 0)
    k_values = jax.random.fold_in(key, 4)
    base = jnp.clip(jax.random.normal(k_base, (IMAGES, PATCHES, D), jnp.float32), -6.0, 6.0)
    keys = base.reshape(IMAGES, PATCHES, HEADS, HEAD_SIZE).transpose(0, 2, 1, 3)
    values = jnp.clip(jax.random.normal(k_values, (IMAGES, HEADS, PATCHES, HEAD_SIZE), jnp.float32), -6.0, 6.0)
    return jnp.concatenate([keys, values], axis=-1).astype(jnp.bfloat16)


def level_of(key, shape, shards, low, top_value):
    loudness = 1.0
    for position, shards_of in shards:
        draws = jax.random.uniform(jax.random.fold_in(jax.random.fold_in(key, 6), position), (shards_of,), jnp.float32, low / len(shards), top_value / len(shards))
        loudness = loudness * jnp.repeat(jnp.exp(draws), shape[position] // shards_of).reshape((-1,) + (1,) * (len(shape) - 1 - position))
    return loudness


def noise(own_key, extent, deviation, limit, cuts=(), held_as=jnp.bfloat16):
    level = level_of(own_key, extent, cuts, -0.22, 0.18) if cuts else 1.0
    drawn = jax.random.normal(own_key, extent, jnp.float32) * deviation * level
    return jnp.minimum(jnp.maximum(drawn, -limit), limit).astype(held_as)


def setup_inputs(seed: int = 0) -> dict:
    seeds = jax.random.split(jax.random.key(seed), 6)
    return {
        "texts": noise(seeds[0], (TEXTS, TEXT_LEN, D), 1.0, 6.0, ((0, 64),)),
        "query_weight": noise(seeds[1], (D, D), D ** -0.5, 0.21875, ((0, 4),)),
        "patch_key_value": draw_patch_key_value(jax.random.fold_in(seeds[5], 71), 0),
        "grad_out": noise(seeds[3], (TEXTS, SLOTS, TEXT_LEN, D), 1.0, 6.0, ((0, 64),)),
        "negatives": draw_negatives(jax.random.fold_in(seeds[5], 71), 0),
    }


def pair_grads(query, cotangent, memory):
    scale = HEAD_SIZE ** -0.5
    q4 = query.reshape(query.shape[:-1] + (-1, HEAD_SIZE)).astype(jnp.float32)
    g4 = cotangent.reshape(cotangent.shape[:-1] + (-1, HEAD_SIZE)).astype(jnp.float32)
    mem = memory.astype(jnp.float32)
    k4 = mem[..., :HEAD_SIZE]
    v4 = mem[..., HEAD_SIZE:]
    scores = jnp.einsum('blhd,bhkd->bhlk', q4, k4) * scale
    probs_f = jax.nn.softmax(scores, axis=-1)
    probs = probs_f.astype(jnp.bfloat16).astype(jnp.float32)
    dprobs = jnp.einsum('blhd,bhkd->bhlk', g4, v4)
    center = jnp.sum(probs_f * dprobs, axis=-1, keepdims=True)
    dscores = (probs_f * (dprobs - center) * scale).astype(jnp.bfloat16).astype(jnp.float32)
    pair_dv = jnp.einsum('bhlk,blhd->bhkd', probs, g4)
    pair_dq = jnp.einsum('bhlk,bhkd->blhd', dscores, k4)
    pair_dk = jnp.einsum('bhlk,blhd->bhkd', dscores, q4)
    pair_dq = pair_dq.reshape(pair_dq.shape[:2] + (-1,))
    return pair_dq, jnp.concatenate([pair_dk, pair_dv], axis=-1)


def reference(texts, query_weight, patch_key_value, grad_out, negatives):
    flat_text = texts.reshape(-1, D)
    query = jnp.dot(flat_text, query_weight.T, preferred_element_type=jnp.float32).astype(jnp.bfloat16)
    query = query.reshape(TEXTS, TEXT_LEN, D)
    own = (jnp.arange(TEXTS, dtype=jnp.int32) // CAPS).astype(jnp.int32)
    chosen = jnp.concatenate([own[:, None], negatives.astype(jnp.int32)], axis=1)
    block = TEXTS // N_DP
    query_blocks = query.reshape(N_DP, block, TEXT_LEN, D)
    grad_blocks = grad_out.reshape(N_DP, block, SLOTS, TEXT_LEN, D)
    image_blocks = chosen.reshape(N_DP, block * SLOTS)

    def visit(memory_acc, item):
        query_tile, g_block, ids = item
        q_rep = jnp.repeat(query_tile, SLOTS, axis=0)
        g_flat = g_block.reshape(block * SLOTS, TEXT_LEN, D)
        memory = jnp.take(patch_key_value, ids, axis=0)
        pair_dq, pair_dkv = pair_grads(q_rep, g_flat, memory)
        memory_acc = memory_acc.at[ids].add(pair_dkv)
        dquery = jnp.sum(pair_dq.reshape(block, SLOTS, TEXT_LEN, D), axis=1)
        return memory_acc, dquery

    start = jnp.zeros((IMAGES, HEADS, PATCHES, 2 * HEAD_SIZE), jnp.float32)
    memory_acc, dquery = lax.scan(visit, start, (query_blocks, grad_blocks, image_blocks))
    dquery = dquery.reshape(-1, D).astype(jnp.bfloat16)
    weight_grad = jnp.dot(dquery.T, flat_text, preferred_element_type=jnp.float32)
    text_grad = jnp.dot(dquery, query_weight, preferred_element_type=jnp.float32).astype(jnp.bfloat16)
    return (text_grad.reshape(TEXTS, TEXT_LEN, D), weight_grad, memory_acc.astype(jnp.bfloat16))
```

```python
import functools

import jax
import jax.numpy as jnp
from jax import lax
from jax.experimental import pallas as pl
from jax.experimental.pallas import tpu as pltpu
from jax.sharding import PartitionSpec as P

HEAD_SIZE = 64
NEG = 3
LANES = 128
TILE = 256
VMEM_LIMIT = 48 * 1024 * 1024


def cdiv(a, b):
    return -(-a // b)


def lower_half(shape):
    return lax.broadcasted_iota(jnp.int32, shape, len(shape) - 1) < HEAD_SIZE


def request_slots(neg_ref, rank_ref, owners, images_here, wanted):
    def clear(o, carry):
        rank_ref[wanted + o] = 0
        return carry

    lax.fori_loop(0, owners, clear, 0)

    def count(k, carry):
        o = neg_ref[k] // images_here
        c = rank_ref[wanted + o]
        rank_ref[k] = c
        rank_ref[wanted + o] = c + 1
        return carry

    lax.fori_loop(0, wanted, count, 0)


def pack_kernel(
    heads, length, images_here, mp_ref, neg_ref, text_ref, weight_ref, grad_ref, *rest
):
    wires = rest[:heads]
    own_ref, q_scr, wire_scr, own_scr, rank_ref = rest[heads:]
    texts_here, slots = grad_ref.shape[0], grad_ref.shape[1]
    owners = wires[0].shape[0]
    wire_rows = wires[0].shape[1]
    captions = texts_here // images_here
    wanted = neg_ref.shape[0]
    request_slots(neg_ref, rank_ref, owners, images_here, wanted)
    for h in range(heads):
        w = weight_ref[h * LANES : (h + 1) * LANES, :]
        q = lax.dot_general(
            text_ref[...], w, (((1,), (1,)), ((), ())), preferred_element_type=jnp.float32
        )
        q_scr[h] = q.astype(jnp.bfloat16).astype(jnp.float32)
    low = lower_half((length, LANES))
    first = mp_ref[0] * heads

    def joined(t, s, h, q):
        head = first + h
        col = pl.multiple_of((head // 2) * LANES, LANES)
        g = grad_ref[t, s, :, pl.ds(col, LANES)].astype(jnp.float32)
        g = jnp.where(lax.rem(head, 2) == 1, g, pltpu.roll(g, HEAD_SIZE, 1))
        return jnp.where(low, q, g)

    def one_text(t, carry):
        for h in range(heads):
            q = q_scr[h, pl.ds(t * length, length), :]
            for j in range(slots - 1):
                k = t * (slots - 1) + j
                o = neg_ref[k] // images_here
                row = o * wire_rows + rank_ref[k] * length
                wire_scr[h, pl.ds(row, length), :] = joined(t, j + 1, h, q)
        return carry

    lax.fori_loop(0, texts_here, one_text, 0)
    for h in range(heads):
        wires[h][...] = (
            wire_scr[h].reshape(owners, wire_rows, LANES).astype(jnp.bfloat16)
        )
    for i in range(images_here):
        for h in range(heads):
            own_scr[...] = jnp.zeros(own_scr.shape, jnp.float32)
            for c in range(captions):
                t = i * captions + c
                q = q_scr[h, t * length : (t + 1) * length, :]
                own_scr[c * length : (c + 1) * length, :] = joined(t, 0, h, q)
            own_ref[i, h] = own_scr[...].astype(jnp.bfloat16)


def load_memory(kv, keys, kv_scr, kkt_scr, padded):
    whole = keys // 16 * 16
    low = lower_half((whole, LANES))
    body, tail = kv[:whole], kv[whole:]
    extra = padded - whole
    tail = jnp.concatenate(
        [tail, jnp.zeros((extra - (keys - whole), LANES), jnp.float32)], axis=0
    )
    full = jnp.concatenate([body, tail], axis=0)
    low = lower_half(full.shape)
    k_only = jnp.where(low, full, 0.0)
    kv_scr[:padded, :] = k_only.astype(jnp.bfloat16)
    kv_scr[padded:, :] = jnp.where(low, 0.0, full).astype(jnp.bfloat16)
    twice = k_only + pltpu.roll(k_only, HEAD_SIZE, 1)
    kkt_scr[...] = twice.T.astype(jnp.bfloat16)


def tile_grads(qg, keys, padded, kv_scr, kkt_scr, s_scr, pd_scr):
    tile = qg.shape[0]
    low = lower_half(qg.shape)
    zero = jnp.zeros_like(qg)
    s_scr[...] = lax.dot_general(
        kv_scr[...], qg, (((1,), (1,)), ((), ())), preferred_element_type=jnp.float32
    )
    bounds = list(range(0, padded, 64)) + [padded]
    chunks = list(zip(bounds[:-1], bounds[1:]))
    top = jnp.full((8, tile), -jnp.inf, jnp.float32)
    for a, b in chunks:
        s = s_scr[a:b, :]
        if b > keys:
            row = lax.broadcasted_iota(jnp.int32, s.shape, 0) + a
            s = jnp.where(row < keys, s, -jnp.inf)
            s_scr[a:b, :] = s
        top = jnp.maximum(top, jnp.max(s.reshape((b - a) // 8, 8, tile), axis=0))
    top = jnp.max(top, axis=0, keepdims=True)
    total = jnp.zeros((8, tile), jnp.float32)
    center = jnp.zeros((8, tile), jnp.float32)
    for a, b in chunks:
        e = jnp.exp(s_scr[a:b, :] - top)
        s_scr[a:b, :] = e
        total = total + jnp.sum(e.reshape((b - a) // 8, 8, tile), axis=0)
        d = e * s_scr[padded + a : padded + b, :]
        center = center + jnp.sum(d.reshape((b - a) // 8, 8, tile), axis=0)
    inverse = 1.0 / jnp.sum(total, axis=0, keepdims=True)
    center = jnp.sum(center, axis=0, keepdims=True) * inverse
    for a, b in chunks:
        p = s_scr[a:b, :] * inverse
        pd_scr[a:b, tile:] = p.astype(jnp.bfloat16)
        ds = p * (s_scr[padded + a : padded + b, :] - center)
        pd_scr[a:b, :tile] = ds.astype(jnp.bfloat16)
    both = jnp.concatenate([jnp.where(low, qg, zero), jnp.where(low, zero, qg)], axis=0)
    dkv = jnp.dot(pd_scr[...], both, preferred_element_type=jnp.float32)
    dqt = jnp.dot(kkt_scr[...], pd_scr[:, :tile], preferred_element_type=jnp.float32)
    return dqt.T * (HEAD_SIZE**-0.5), dkv


def own_kernel(keys, padded, qg_ref, kv_ref, acc_ref, dq_ref, kv_scr, kkt_scr, s_scr, pd_scr):
    load_memory(kv_ref[0, 0].astype(jnp.float32), keys, kv_scr, kkt_scr, padded)
    dq, dkv = tile_grads(qg_ref[0, 0], keys, padded, kv_scr, kkt_scr, s_scr, pd_scr)
    acc_ref[0, 0] = dkv
    dq_ref[0, 0] = dq


def far_kernel(
    keys,
    padded,
    length,
    images_here,
    plan_ref,
    wire_ref,
    kv_ref,
    own_ref,
    dkv_in,
    dkv_ref,
    back_ref,
    rows_scr,
    acc_scr,
    kv_scr,
    kkt_scr,
    s_scr,
    pd_scr,
):
    image = pl.program_id(0)
    senders = wire_ref.shape[0]
    slots = 2 * senders

    @pl.when(image == 0)
    def _():
        for i in range(images_here):
            n = plan_ref[slots + images_here + i]

            @pl.when(n > 0)
            def _():
                start = pl.multiple_of(plan_ref[slots + i] + (n - 1) * TILE, TILE)
                rows_scr[pl.ds(start, TILE), :] = jnp.zeros((TILE, LANES), jnp.float32)

        def place(s, carry):
            block = wire_ref[s].astype(jnp.float32)
            for r in range(2):
                pos = plan_ref[2 * s + r]

                @pl.when(pos >= 0)
                def _():
                    rows_scr[pl.ds(pos, length), :] = block[r * length : (r + 1) * length]

            return carry

        lax.fori_loop(0, senders, place, 0)

    load_memory(kv_ref[0, 0].astype(jnp.float32), keys, kv_scr, kkt_scr, padded)
    acc_scr[...] = own_ref[0, 0]
    base = plan_ref[slots + image]

    def step(n, carry):
        start = pl.multiple_of(base + n * TILE, TILE)
        qg = rows_scr[pl.ds(start, TILE), :].astype(jnp.bfloat16)
        dq, dkv = tile_grads(qg, keys, padded, kv_scr, kkt_scr, s_scr, pd_scr)
        acc_scr[...] += dkv
        rows_scr[pl.ds(start, TILE), :] = dq
        return carry

    lax.fori_loop(0, plan_ref[slots + images_here + image], step, 0)
    dkv_ref[0, 0] = acc_scr[:keys, :].astype(jnp.bfloat16)

    @pl.when(image == images_here - 1)
    def _():
        rows = back_ref.shape[1]
        low = lower_half((rows, LANES))

        def give(s, carry):
            p0 = jnp.maximum(plan_ref[2 * s], 0)
            p1 = jnp.maximum(plan_ref[2 * s + 1], 0)
            x0 = rows_scr[pl.ds(p0, rows), :]
            x1 = rows_scr[pl.ds(p1, rows), :]
            back_ref[s] = jnp.where(low, x0, x1).astype(jnp.bfloat16)
            return carry

        lax.fori_loop(0, senders, give, 0)


def gather_kernel(heads, length, images_here, neg_ref, text_ref, own_ref, *rest):
    backs = rest[:heads]
    dq_ref, weight_ref, sum_scr, rank_ref = rest[heads:]
    owners = backs[0].shape[0]
    wanted = neg_ref.shape[0]
    block = own_ref.shape[2]
    count = sum_scr.shape[1]
    per_image = count // images_here
    request_slots(neg_ref, rank_ref, owners, images_here, wanted)
    for h in range(heads):
        for i in range(images_here):
            sum_scr[h, i * per_image : (i + 1) * per_image, :] = own_ref[i, h][:per_image]

    def one(t, carry):
        at = pl.ds(t * length, length)
        for h in range(heads):
            total = sum_scr[h, at, :]
            for j in range(NEG):
                k = t * NEG + j
                o = neg_ref[k] // images_here
                x = backs[h][o].astype(jnp.float32)[:length]
                x = jnp.where(rank_ref[k] == 1, pltpu.roll(x, HEAD_SIZE, 1), x)
                total = total + x
            sum_scr[h, at, :] = total
        return carry

    lax.fori_loop(0, count // length, one, 0)
    text = text_ref[...]
    for h in range(heads):
        dq = sum_scr[h].astype(jnp.bfloat16)
        dq_ref[h] = dq
        full = lax.dot_general(
            dq, text, (((0,), (0,)), ((), ())), preferred_element_type=jnp.float32
        )
        weight_ref[h * HEAD_SIZE : (h + 1) * HEAD_SIZE, :] = full[:HEAD_SIZE].astype(
            jnp.bfloat16
        )


def params():
    return pltpu.CompilerParams(vmem_limit_bytes=VMEM_LIMIT)


SMEM = pl.BlockSpec(memory_space=pltpu.SMEM)
VMEM = pl.BlockSpec(memory_space=pltpu.VMEM)


def per_device(texts, query_weight, patch_key_value, grad_out, negatives):
    owners = lax.axis_size("dp")
    members = lax.axis_size("mp")
    texts_here, length, depth = texts.shape
    images_here, heads, keys, _ = patch_key_value.shape
    width = query_weight.shape[0]
    padded = cdiv(keys, 16) * 16
    count = texts_here * length
    wanted = NEG * texts_here
    slots = 2 * owners
    wire_rows = cdiv(2 * length, 8) * 8
    back_rows = cdiv(length, 8) * 8
    bf16, f32, i32 = jnp.bfloat16, jnp.float32, jnp.int32

    flat_text = texts.reshape(count, depth)
    flat_neg = negatives.reshape(-1)
    scaled = query_weight * jnp.asarray(HEAD_SIZE**-0.5, bf16)
    spread = jnp.pad(
        scaled.reshape(heads, HEAD_SIZE, depth), ((0, 0), (0, LANES - HEAD_SIZE), (0, 0))
    ).reshape(heads * LANES, depth)
    all_weight = lax.all_gather(query_weight, "mp", axis=0, tiled=True)

    packed = pl.pallas_call(
        functools.partial(pack_kernel, heads, length, images_here),
        in_specs=[SMEM, SMEM, VMEM, VMEM, VMEM],
        out_specs=[VMEM] * (heads + 1),
        out_shape=[jax.ShapeDtypeStruct((owners, wire_rows, LANES), bf16)] * heads
        + [jax.ShapeDtypeStruct((images_here, heads, TILE, LANES), bf16)],
        scratch_shapes=[
            pltpu.VMEM((heads, count, LANES), f32),
            pltpu.VMEM((heads, owners * wire_rows, LANES), f32),
            pltpu.VMEM((TILE, LANES), f32),
            pltpu.SMEM((wanted + owners,), i32),
        ],
        compiler_params=params(),
        name="pack",
    )(
        lax.axis_index("mp").reshape(1).astype(i32),
        flat_neg,
        flat_text,
        spread,
        grad_out,
    )
    wires, own_rows = packed[:heads], packed[heads]

    owner = flat_neg // images_here
    order = jnp.arange(wanted, dtype=i32)
    rank = jnp.sum(
        (owner[:, None] == owner[None, :]) & (order[None, :] < order[:, None]), axis=1
    ).astype(i32)
    slot = owner * 2 + rank
    placed = slot[None, :] == jnp.arange(slots, dtype=i32)[:, None]
    send_id = jnp.sum(jnp.where(placed, flat_neg[None, :] % images_here + 1, 0), axis=1) - 1
    got_id = lax.all_to_all(
        send_id.astype(i32).reshape(owners, 2), "dp", split_axis=0, concat_axis=0, tiled=True
    ).reshape(-1)
    got_wires = [lax.all_to_all(w, "dp", split_axis=0, concat_axis=0, tiled=True) for w in wires]

    here = jnp.arange(images_here, dtype=i32)
    all_slots = jnp.arange(slots, dtype=i32)
    ahead = jnp.sum(
        (got_id[:, None] == got_id[None, :]) & (all_slots[None, :] < all_slots[:, None]), axis=1
    ).astype(i32)
    number = jnp.sum(got_id[:, None] == here[None, :], axis=0).astype(i32)
    tiles = (number * length + TILE - 1) // TILE
    base = jnp.sum(jnp.where(here[None, :] < here[:, None], tiles[None, :], 0), axis=1) * TILE
    start = jnp.sum(jnp.where(got_id[:, None] == here[None, :], base[None, :], 0), axis=1)
    pos = jnp.where(got_id >= 0, start + ahead * length, -1)
    plan = jnp.concatenate([pos, base, tiles]).astype(i32)

    math_scratch = [
        pltpu.VMEM((2 * padded, LANES), bf16),
        pltpu.VMEM((LANES, padded), bf16),
        pltpu.VMEM((2 * padded, TILE), f32),
        pltpu.VMEM((padded, 2 * TILE), bf16),
    ]
    own_acc, own_dq = pl.pallas_call(
        functools.partial(own_kernel, keys, padded),
        grid=(images_here, heads),
        in_specs=[
            pl.BlockSpec((1, 1, TILE, LANES), lambda i, h: (i, h, 0, 0)),
            pl.BlockSpec((1, 1, keys, LANES), lambda i, h: (i, h, 0, 0)),
        ],
        out_specs=[
            pl.BlockSpec((1, 1, padded, LANES), lambda i, h: (i, h, 0, 0)),
            pl.BlockSpec((1, 1, TILE, LANES), lambda i, h: (i, h, 0, 0)),
        ],
        out_shape=[
            jax.ShapeDtypeStruct((images_here, heads, padded, LANES), f32),
            jax.ShapeDtypeStruct((images_here, heads, TILE, LANES), f32),
        ],
        scratch_shapes=math_scratch,
        compiler_params=params(),
        name="own",
    )(own_rows, patch_key_value)

    most = (2 * owners * length) // TILE + images_here
    dkv = jnp.zeros(patch_key_value.shape, bf16)
    backs = []
    for h in range(heads):
        dkv, back = pl.pallas_call(
            functools.partial(far_kernel, keys, padded, length, images_here),
            grid=(images_here,),
            in_specs=[
                SMEM,
                pl.BlockSpec((owners, wire_rows, LANES), lambda i: (0, 0, 0)),
                pl.BlockSpec((1, 1, keys, LANES), lambda i, h=h: (i, h, 0, 0)),
                pl.BlockSpec((1, 1, padded, LANES), lambda i, h=h: (i, h, 0, 0)),
                pl.BlockSpec(memory_space=pl.ANY),
            ],
            out_specs=[
                pl.BlockSpec((1, 1, keys, LANES), lambda i, h=h: (i, h, 0, 0)),
                pl.BlockSpec((owners, back_rows, LANES), lambda i: (0, 0, 0)),
            ],
            out_shape=[
                jax.ShapeDtypeStruct(patch_key_value.shape, bf16),
                jax.ShapeDtypeStruct((owners, back_rows, LANES), bf16),
            ],
            scratch_shapes=[
                pltpu.VMEM((most * TILE + 64, LANES), f32),
                pltpu.VMEM((padded, LANES), f32),
            ]
            + math_scratch,
            input_output_aliases={4: 0},
            compiler_params=params(),
            name="far" + str(h),
        )(plan, got_wires[h], patch_key_value, own_acc, dkv)
        backs.append(lax.all_to_all(back, "dp", split_axis=0, concat_axis=0, tiled=True))

    dquery, weight_local = pl.pallas_call(
        functools.partial(gather_kernel, heads, length, images_here),
        in_specs=[SMEM] + [VMEM] * (2 + heads),
        out_specs=[VMEM, VMEM],
        out_shape=[
            jax.ShapeDtypeStruct((heads, count, LANES), bf16),
            jax.ShapeDtypeStruct((width, depth), bf16),
        ],
        scratch_shapes=[
            pltpu.VMEM((heads, count, LANES), f32),
            pltpu.SMEM((wanted + owners,), i32),
        ],
        compiler_params=params(),
        name="gather",
    )(flat_neg, flat_text, own_dq, *backs)

    share = width // owners
    parts = lax.all_to_all(
        weight_local.reshape(owners, share, depth), "dp", split_axis=0, concat_axis=0, tiled=True
    )
    rows = jnp.sum(parts.astype(f32), axis=0).astype(bf16)
    weight_grad = lax.all_to_all(
        jnp.broadcast_to(rows[None], (owners, share, depth)),
        "dp",
        split_axis=0,
        concat_axis=0,
        tiled=True,
    )
    weight_grad = weight_grad.reshape(width, depth).astype(f32)

    mine = count // members
    flat_dq = dquery[:, :, :HEAD_SIZE].transpose(1, 0, 2).reshape(members, mine, width)
    flat_dq = lax.all_to_all(flat_dq, "mp", split_axis=0, concat_axis=0, tiled=True)
    flat_dq = flat_dq.transpose(1, 0, 2).reshape(mine, members * width)
    text_grad = jnp.dot(flat_dq, all_weight, preferred_element_type=f32).astype(bf16)
    text_grad = text_grad.reshape(texts_here // members, length, depth)
    return (text_grad, weight_grad, dkv)


def solution(mesh):
    in_specs = (
        P("dp", None, None),
        P("mp", None),
        P("dp", "mp", None, None),
        P("dp", None, None, None),
        P("dp", None),
    )
    out_specs = (P(("dp", "mp"), None, None), P("mp", None), P("dp", "mp", None, None))
    return jax.shard_map(
        per_device, mesh=mesh, in_specs=in_specs, out_specs=out_specs, check_vma=False
    )
```

```python
import functools

import jax
import jax.numpy as jnp
from jax import lax
from jax.experimental import pallas as pl
from jax.experimental.pallas import tpu as pltpu
from jax.sharding import PartitionSpec as P

HEAD_SIZE = 64
NEG = 3
LANES = 128
TILE = 256
WAYS = 4
VMEM_LIMIT = 60 * 1024 * 1024


def cdiv(a, b):
    return -(-a // b)


def lower_half(shape):
    return lax.broadcasted_iota(jnp.int32, shape, len(shape) - 1) < HEAD_SIZE


def request_slots(neg_ref, rank_ref, seen_ref, owners, images_here):
    negatives, texts_here = neg_ref.shape

    def clear(o, carry):
        seen_ref[o] = 0
        return carry

    lax.fori_loop(0, owners, clear, 0)

    def count(t, carry):
        for j in range(negatives):
            o = neg_ref[j, t] // images_here
            c = seen_ref[o]
            rank_ref[j, t] = c
            seen_ref[o] = c + 1
        return carry

    lax.fori_loop(0, texts_here, count, 0)


def joined(g, odd, q):
    g = g.astype(jnp.float32)
    g = jnp.where(odd == 1, g, pltpu.roll(g, HEAD_SIZE, 1))
    return jnp.where(lower_half(g.shape), q, g)


def project(text_ref, weight_ref, query_ref):
    q = lax.dot_general(
        text_ref[...], weight_ref[...], (((1,), (1,)), ((), ())), preferred_element_type=jnp.float32
    )
    q = q.astype(jnp.bfloat16).astype(jnp.float32) * HEAD_SIZE**-0.5
    for h in range(query_ref.shape[0]):
        if h % 2:
            a = (h - 1) * HEAD_SIZE
            query_ref[h] = pltpu.roll(q[:, a : a + LANES], HEAD_SIZE, 1)
        elif (h + 2) * HEAD_SIZE <= q.shape[1]:
            query_ref[h] = q[:, h * HEAD_SIZE : (h + 2) * HEAD_SIZE]
        else:
            query_ref[h, :, :HEAD_SIZE] = q[:, h * HEAD_SIZE :]
            query_ref[h, :, HEAD_SIZE:] = jnp.zeros((q.shape[0], HEAD_SIZE), jnp.float32)


def pack_rows(first, heads, images_here, odd_ref, neg_ref, rank_ref, query_ref, grad_ref, wire_ref, scr):
    texts_here, slots, length, _ = grad_ref.shape
    wire_rows = wire_ref.shape[1]
    tells = wire_rows >= 2 * heads * length + 2
    if tells:
        scr[...] = jnp.full(scr.shape, -1.0, jnp.float32)

    def one_text(t, carry):
        for h in range(heads):
            q = query_ref[first + h, pl.ds(t, length, stride=texts_here), :]
            place = odd_ref[0] + first + h
            col = pl.multiple_of((place // 2) * LANES, LANES)
            for j in range(slots - 1):
                n = neg_ref[j, t]
                r = rank_ref[j, t]
                o = n // images_here
                row = o * wire_rows + (r * heads + h) * length
                g = grad_ref[t, j + 1, :, pl.ds(col, LANES)]
                scr[pl.ds(row, length), :] = joined(g, lax.rem(place, 2), q)
                if h == 0 and tells:
                    tell = o * wire_rows + 2 * heads * length + r
                    image = (n - o * images_here).astype(jnp.float32)
                    scr[pl.ds(tell, 1), :] = jnp.full((1, LANES), image, jnp.float32)
        return carry

    lax.fori_loop(0, texts_here, one_text, 0)
    wire_ref[...] = scr[...].reshape(wire_ref.shape).astype(jnp.bfloat16)


def pack_first_kernel(
    heads, images_here, odd_ref, neg_ref, text_ref, weight_ref, grad_ref, wire_ref, query_ref, rank_ref, scr, seen_ref
):
    request_slots(neg_ref, rank_ref, seen_ref, wire_ref.shape[0], images_here)
    project(text_ref, weight_ref, query_ref)
    pack_rows(0, heads, images_here, odd_ref, neg_ref, rank_ref, query_ref, grad_ref, wire_ref, scr)


def pack_later_kernel(
    first, heads, images_here, odd_ref, neg_ref, rank_ref, query_ref, grad_ref, after_ref, wire_ref, scr
):
    pack_rows(first, heads, images_here, odd_ref, neg_ref, rank_ref, query_ref, grad_ref, wire_ref, scr)


def load_memory(kv, keys, kv_ref, kkt_ref, padded):
    full = jnp.concatenate([kv, jnp.zeros((padded - keys, LANES), jnp.float32)], axis=0)
    low = lower_half(full.shape)
    k_only = jnp.where(low, full, 0.0)
    kv_ref[:padded, :] = k_only.astype(jnp.bfloat16)
    kv_ref[padded:, :] = jnp.where(low, 0.0, full).astype(jnp.bfloat16)
    twice = k_only + pltpu.roll(k_only, HEAD_SIZE, 1)
    kkt_ref[...] = twice.T.astype(jnp.bfloat16)


def tile_scores(qg, kv, s_scr):
    s_scr[...] = lax.dot_general(
        kv, qg, (((1,), (1,)), ((), ())), preferred_element_type=jnp.float32
    )


def tile_softmax(keys, padded, s_scr, pd_scr):
    tile = s_scr.shape[1]
    bounds = list(range(0, padded, 64)) + [padded]
    chunks = list(zip(bounds[:-1], bounds[1:]))
    top = jnp.full((8, tile), -jnp.inf, jnp.float32)
    for a, b in chunks:
        s = s_scr[a:b, :]
        if b > keys:
            row = lax.broadcasted_iota(jnp.int32, s.shape, 0) + a
            s = jnp.where(row < keys, s, -jnp.inf)
            s_scr[a:b, :] = s
        top = jnp.maximum(top, jnp.max(s.reshape((b - a) // 8, 8, tile), axis=0))
    top = jnp.max(top, axis=0, keepdims=True)
    total = jnp.zeros((8, tile), jnp.float32)
    center = jnp.zeros((8, tile), jnp.float32)
    for a, b in chunks:
        e = jnp.exp(s_scr[a:b, :] - top)
        s_scr[a:b, :] = e
        total = total + jnp.sum(e.reshape((b - a) // 8, 8, tile), axis=0)
        d = e * s_scr[padded + a : padded + b, :]
        center = center + jnp.sum(d.reshape((b - a) // 8, 8, tile), axis=0)
    inverse = 1.0 / jnp.sum(total, axis=0, keepdims=True)
    center = jnp.sum(center, axis=0, keepdims=True) * inverse
    for a, b in chunks:
        p = s_scr[a:b, :] * inverse
        pd_scr[a:b, tile:] = p.astype(jnp.bfloat16)
        ds = p * (s_scr[padded + a : padded + b, :] - center)
        pd_scr[a:b, :tile] = ds.astype(jnp.bfloat16)


def tile_outputs(qg, kkt, pd_scr):
    tile = qg.shape[0]
    low = lower_half(qg.shape)
    zero = jnp.zeros_like(qg)
    both = jnp.concatenate([jnp.where(low, qg, zero), jnp.where(low, zero, qg)], axis=0)
    dkv = jnp.dot(pd_scr[...], both, preferred_element_type=jnp.float32)
    dqt = jnp.dot(kkt, pd_scr[:, :tile], preferred_element_type=jnp.float32)
    return dqt.T * (HEAD_SIZE**-0.5), dkv


def own_kernel(
    keys, padded, texts_here, odd_ref, query_ref, grad_ref, kv_ref, acc_ref, dq_ref, both_ref, kkt_ref, own_scr, s_scr, pd_scr
):
    image, h = pl.program_id(0), pl.program_id(1)
    captions, _, length, _ = grad_ref.shape
    load_memory(kv_ref[0, 0].astype(jnp.float32), keys, both_ref.at[0, 0], kkt_ref.at[0, 0], padded)
    place = odd_ref[0] + h
    col = pl.multiple_of((place // 2) * LANES, LANES)
    own_scr[captions * length :, :] = jnp.zeros((TILE - captions * length, LANES), jnp.float32)
    for c in range(captions):
        q = query_ref[0, pl.ds(image * captions + c, length, stride=texts_here), :]
        g = grad_ref[c, 0, :, pl.ds(col, LANES)]
        own_scr[c * length : (c + 1) * length, :] = joined(g, lax.rem(place, 2), q)
    qg = own_scr[...].astype(jnp.bfloat16)
    tile_scores(qg, both_ref[0, 0], s_scr)
    tile_softmax(keys, padded, s_scr, pd_scr)
    dq, dkv = tile_outputs(qg, kkt_ref[0, 0], pd_scr)
    acc_ref[0, 0] = dkv
    dq_ref[0, 0] = dq


def far_kernel(
    keys,
    padded,
    length,
    heads,
    plan_ref,
    wire_ref,
    both_ref,
    kkt_ref,
    own_ref,
    dkv_in,
    dkv_ref,
    back_ref,
    rows_scr,
    acc_scr,
    *pairs,
):
    h = pl.program_id(0)
    images = both_ref.shape[0]
    senders = wire_ref.shape[0]
    slots = 2 * senders
    ways = len(pairs) // 2
    s_scrs, pd_scrs = pairs[:ways], pairs[ways:]

    @pl.when(h == 0)
    def _():
        def clear(start):
            for g in range(heads):
                rows_scr[g, pl.ds(pl.multiple_of(start, TILE), TILE), :] = jnp.zeros(
                    (TILE, LANES), jnp.float32
                )

        for i in range(images):
            n = plan_ref[slots + images + i]

            @pl.when(n > 0)
            def _():
                clear(plan_ref[slots + i] + (n - 1) * TILE)

        end = plan_ref[slots + images - 1] + plan_ref[slots + 2 * images - 1] * TILE
        for w in range(ways - 1):
            clear(end + w * TILE)

        def place(s, carry):
            block = wire_ref[s].astype(jnp.float32)
            for r in range(2):
                pos = plan_ref[2 * s + r]

                @pl.when(pos >= 0)
                def _():
                    for g in range(heads):
                        a = (r * heads + g) * length
                        rows_scr[g, pl.ds(pos, length), :] = block[a : a + length]

            return carry

        lax.fori_loop(0, senders, place, 0)

    for i in range(images):
        acc_scr[i] = own_ref[i, 0]
    edges = [plan_ref[slots + i] // TILE for i in range(1, images)]
    tiles = plan_ref[slots + images - 1] // TILE + plan_ref[slots + 2 * images - 1]

    def step(k, carry):
        starts, images_of, rows = [], [], []
        for w in range(ways):
            n = k * ways + w
            image = jnp.int32(0)
            for e in edges:
                image = image + (n >= e).astype(jnp.int32)
            start = pl.multiple_of(n * TILE, TILE)
            qg = rows_scr[h, pl.ds(start, TILE), :].astype(jnp.bfloat16)
            starts.append(start)
            images_of.append(image)
            rows.append(qg)
            tile_scores(qg, both_ref[image, 0], s_scrs[w])
        for w in range(ways):
            tile_softmax(keys, padded, s_scrs[w], pd_scrs[w])
            dq, dkv = tile_outputs(rows[w], kkt_ref[images_of[w], 0], pd_scrs[w])
            acc_scr[images_of[w]] += dkv
            rows_scr[h, pl.ds(starts[w], TILE), :] = dq
        return carry

    lax.fori_loop(0, (tiles + ways - 1) // ways, step, 0)
    for i in range(images):
        dkv_ref[i, 0] = acc_scr[i, :keys, :].astype(jnp.bfloat16)

    @pl.when(h == heads - 1)
    def _():
        rows = back_ref.shape[1]
        low = lower_half((length, LANES))
        spare = rows - heads * length

        def give(s, carry):
            p0 = jnp.maximum(plan_ref[2 * s], 0)
            p1 = jnp.maximum(plan_ref[2 * s + 1], 0)
            parts = []
            for g in range(heads):
                x0 = rows_scr[g, pl.ds(p0, length), :]
                x1 = rows_scr[g, pl.ds(p1, length), :]
                parts.append(jnp.where(low, x0, x1))
            if spare:
                parts.append(jnp.zeros((spare, LANES), jnp.float32))
            back_ref[s] = jnp.concatenate(parts, axis=0).astype(jnp.bfloat16)
            return carry

        lax.fori_loop(0, senders, give, 0)


def sum_requests(heads, length, images_here, neg_ref, rank_ref, own_ref, back_ref, sum_scr):
    texts_here = sum_scr.shape[1] // length
    captions = texts_here // images_here

    def one(t, carry):
        image = t // captions
        totals = [
            own_ref[image, h, pl.ds((t - image * captions) * length, length), :]
            for h in range(heads)
        ]
        for j in range(NEG):
            block = back_ref[neg_ref[j, t] // images_here].astype(jnp.float32)
            block = jnp.where(rank_ref[j, t] == 1, pltpu.roll(block, HEAD_SIZE, 1), block)
            for h in range(heads):
                totals[h] = totals[h] + block[h * length : (h + 1) * length]
        for h in range(heads):
            sum_scr[h, pl.ds(t, length, stride=texts_here), :] = totals[h]
        return carry

    lax.fori_loop(0, texts_here, one, 0)


def gather_two_kernel(
    length, images_here, neg_ref, rank_ref, text_ref, own_ref, back_ref, dq_ref, weight_ref, sum_scr
):
    sum_requests(2, length, images_here, neg_ref, rank_ref, own_ref, back_ref, sum_scr)
    pair = jnp.where(
        lower_half(sum_scr.shape[1:]), sum_scr[0], pltpu.roll(sum_scr[1], HEAD_SIZE, 1)
    )
    dq = pair.astype(jnp.bfloat16)
    dq_ref[...] = dq
    weight_ref[...] = lax.dot_general(
        dq, text_ref[...], (((0,), (0,)), ((), ())), preferred_element_type=jnp.float32
    )


def gather_last_kernel(
    length, images_here, neg_ref, rank_ref, text_ref, own_ref, back_ref, head_ref, dq_ref, weight_ref, sum_scr
):
    sum_requests(1, length, images_here, neg_ref, rank_ref, own_ref, back_ref, sum_scr)
    dq = sum_scr[0].astype(jnp.bfloat16)
    dq_ref[...] = dq
    last = lax.dot_general(
        dq, text_ref[...], (((0,), (0,)), ((), ())), preferred_element_type=jnp.float32
    )
    half = weight_ref.shape[2]
    before = head_ref.shape[0] // 8
    for b in range(before + HEAD_SIZE // 8):
        rows = head_ref[b * 8 : b * 8 + 8, :] if b < before else last[(b - before) * 8 : (b - before) * 8 + 8]
        for side in range(2):
            weight_ref[2 * b + side] = rows[:, side * half : (side + 1) * half].astype(jnp.bfloat16)


def total_kernel(parts_ref, out_ref):
    total = parts_ref[0].astype(jnp.float32)
    for d in range(1, parts_ref.shape[0]):
        total = total + parts_ref[d].astype(jnp.float32)
    total = total.astype(jnp.bfloat16)
    for d in range(out_ref.shape[0]):
        out_ref[d] = total


def unfold_kernel(pieces_ref, out_ref):
    half = pieces_ref.shape[2]
    for b in range(out_ref.shape[0] // 8):
        for side in range(2):
            out_ref[b * 8 : b * 8 + 8, side * half : (side + 1) * half] = pieces_ref[
                2 * b + side
            ].astype(jnp.float32)


def params():
    return pltpu.CompilerParams(vmem_limit_bytes=VMEM_LIMIT)


def cost(us):
    return pl.CostEstimate(
        flops=int(us * 1e6 * 1150 / 2), bytes_accessed=int(us * 1e-6 * 3.6e12), transcendentals=0
    )


SMEM = pl.BlockSpec(memory_space=pltpu.SMEM)
VMEM = pl.BlockSpec(memory_space=pltpu.VMEM)
ANY = pl.BlockSpec(memory_space=pl.ANY)


def math_scratch(padded, ways):
    return [pltpu.VMEM((2 * padded, TILE), jnp.float32)] * ways + [
        pltpu.VMEM((padded, 2 * TILE), jnp.bfloat16)
    ] * ways


def far_call(plan, wire, first, many, both, kkt, own_acc, dkv, us, length):
    owners, rows, _ = wire.shape
    images, _, keys, _ = dkv.shape
    padded = own_acc.shape[2]
    back_rows = cdiv(many * length, 8) * 8
    most = (2 * owners * length) // TILE + images + WAYS - 1
    return pl.pallas_call(
        functools.partial(far_kernel, keys, padded, length, many),
        grid=(many,),
        in_specs=[
            SMEM,
            pl.BlockSpec((owners, rows, LANES), lambda h: (0, 0, 0)),
            pl.BlockSpec((images, 1, 2 * padded, LANES), lambda h: (0, first + h, 0, 0)),
            pl.BlockSpec((images, 1, LANES, padded), lambda h: (0, first + h, 0, 0)),
            pl.BlockSpec((images, 1, padded, LANES), lambda h: (0, first + h, 0, 0)),
            ANY,
        ],
        out_specs=[
            pl.BlockSpec((images, 1, keys, LANES), lambda h: (0, first + h, 0, 0)),
            pl.BlockSpec((owners, back_rows, LANES), lambda h: (0, 0, 0)),
        ],
        out_shape=[
            jax.ShapeDtypeStruct(dkv.shape, jnp.bfloat16),
            jax.ShapeDtypeStruct((owners, back_rows, LANES), jnp.bfloat16),
        ],
        scratch_shapes=[
            pltpu.VMEM((many, most * TILE + 64, LANES), jnp.float32),
            pltpu.VMEM((images, padded, LANES), jnp.float32),
        ]
        + math_scratch(padded, WAYS),
        input_output_aliases={5: 0},
        compiler_params=params(),
        cost_estimate=cost(us),
        name="far" + str(first),
    )(plan, wire, both, kkt, own_acc, dkv)


def exchange(x):
    return lax.all_to_all(x, "dp", split_axis=0, concat_axis=0, tiled=True)


def per_device(texts, query_weight, patch_key_value, grad_out, negatives):
    owners = lax.axis_size("dp")
    members = lax.axis_size("mp")
    member = lax.axis_index("mp")
    texts_here, length, depth = texts.shape
    images_here, heads, keys, _ = patch_key_value.shape
    width = query_weight.shape[0]
    captions = texts_here // images_here
    padded = cdiv(keys, 16) * 16
    count = texts_here * length
    slots = 2 * owners
    bf16, f32, i32 = jnp.bfloat16, jnp.float32, jnp.int32
    early = heads - 1
    first_rows = cdiv(2 * early * length + 2, 8) * 8
    later_rows = cdiv(2 * length, 8) * 8

    flat_text = texts.transpose(1, 0, 2).reshape(count, depth)
    neg = negatives.T
    all_weight = lax.all_gather(query_weight, "mp", axis=0, tiled=True)
    start_col = member * width // LANES * LANES
    odd = ((member * width - start_col) // HEAD_SIZE).reshape(1).astype(i32)
    window = lax.dynamic_slice_in_dim(grad_out, start_col, 2 * LANES, 3)

    wire_first, query, rank = pl.pallas_call(
        functools.partial(pack_first_kernel, early, images_here),
        in_specs=[SMEM, SMEM, VMEM, VMEM, VMEM],
        out_specs=[VMEM, VMEM, SMEM],
        out_shape=[
            jax.ShapeDtypeStruct((owners, first_rows, LANES), bf16),
            jax.ShapeDtypeStruct((heads, count, LANES), f32),
            jax.ShapeDtypeStruct(neg.shape, i32),
        ],
        scratch_shapes=[
            pltpu.VMEM((owners * first_rows, LANES), f32),
            pltpu.SMEM((owners,), i32),
        ],
        compiler_params=params(),
        cost_estimate=cost(5),
        name="pack_first",
    )(odd, neg, flat_text, query_weight, window)
    got_first = exchange(wire_first)

    own_acc, own_dq, both, kkt = pl.pallas_call(
        functools.partial(own_kernel, keys, padded, texts_here),
        grid=(images_here, heads),
        in_specs=[
            SMEM,
            pl.BlockSpec((1, count, LANES), lambda i, h: (h, 0, 0)),
            pl.BlockSpec((captions, 1, length, 2 * LANES), lambda i, h: (i, 0, 0, 0)),
            pl.BlockSpec((1, 1, keys, LANES), lambda i, h: (i, h, 0, 0)),
        ],
        out_specs=[
            pl.BlockSpec((1, 1, padded, LANES), lambda i, h: (i, h, 0, 0)),
            pl.BlockSpec((1, 1, TILE, LANES), lambda i, h: (i, h, 0, 0)),
            pl.BlockSpec((1, 1, 2 * padded, LANES), lambda i, h: (i, h, 0, 0)),
            pl.BlockSpec((1, 1, LANES, padded), lambda i, h: (i, h, 0, 0)),
        ],
        out_shape=[
            jax.ShapeDtypeStruct((images_here, heads, padded, LANES), f32),
            jax.ShapeDtypeStruct((images_here, heads, TILE, LANES), f32),
            jax.ShapeDtypeStruct((images_here, heads, 2 * padded, LANES), bf16),
            jax.ShapeDtypeStruct((images_here, heads, LANES, padded), bf16),
        ],
        scratch_shapes=[pltpu.VMEM((TILE, LANES), f32)] + math_scratch(padded, 1),
        compiler_params=params(),
        cost_estimate=cost(13),
        name="own",
    )(odd, query, window, patch_key_value)

    wire_later = pl.pallas_call(
        functools.partial(pack_later_kernel, early, heads - early, images_here),
        in_specs=[SMEM, SMEM, SMEM, VMEM, VMEM, ANY],
        out_specs=VMEM,
        out_shape=jax.ShapeDtypeStruct((owners, later_rows, LANES), bf16),
        scratch_shapes=[pltpu.VMEM((owners * later_rows, LANES), f32)],
        compiler_params=params(),
        cost_estimate=cost(4),
        name="pack_later",
    )(odd, neg, rank, query, window, own_acc)
    got_later = exchange(wire_later)

    tell = 2 * early * length
    got_id = got_first[:, tell : tell + 2, 0].astype(i32).reshape(-1)
    here = jnp.arange(images_here, dtype=i32)
    all_slots = jnp.arange(slots, dtype=i32)
    ahead = jnp.sum(
        (got_id[:, None] == got_id[None, :]) & (all_slots[None, :] < all_slots[:, None]), axis=1
    ).astype(i32)
    number = jnp.sum(got_id[:, None] == here[None, :], axis=0).astype(i32)
    tiles = (number * length + TILE - 1) // TILE
    base = jnp.sum(jnp.where(here[None, :] < here[:, None], tiles[None, :], 0), axis=1) * TILE
    start = jnp.sum(jnp.where(got_id[:, None] == here[None, :], base[None, :], 0), axis=1)
    pos = jnp.where(got_id >= 0, start + ahead * length, -1)
    plan = jnp.concatenate([pos, base, tiles]).astype(i32)

    dkv = jnp.zeros(patch_key_value.shape, bf16)
    dkv, back_first = far_call(
        plan, got_first, 0, early, both, kkt, own_acc, dkv, 22, length
    )
    home_first = exchange(back_first)
    dkv, back_later = far_call(
        plan, got_later, early, heads - early, both, kkt, own_acc, dkv, 12, length
    )
    home_later = exchange(back_later)

    half = depth // 2
    dq_first, weight_first = pl.pallas_call(
        functools.partial(gather_two_kernel, length, images_here),
        grid=(1,),
        in_specs=[
            SMEM,
            SMEM,
            VMEM,
            pl.BlockSpec((images_here, early, TILE, LANES), lambda n: (0, 0, 0, 0)),
            VMEM,
        ],
        out_specs=[VMEM, VMEM],
        out_shape=[
            jax.ShapeDtypeStruct((count, LANES), bf16),
            jax.ShapeDtypeStruct((early * HEAD_SIZE, depth), f32),
        ],
        scratch_shapes=[pltpu.VMEM((early, count, LANES), f32)],
        compiler_params=params(),
        cost_estimate=cost(4),
        name="gather_two",
    )(neg, rank, flat_text, own_dq, home_first)
    dq_later, weight_local = pl.pallas_call(
        functools.partial(gather_last_kernel, length, images_here),
        grid=(1,),
        in_specs=[
            SMEM,
            SMEM,
            VMEM,
            pl.BlockSpec((images_here, 1, TILE, LANES), lambda n: (0, early, 0, 0)),
            VMEM,
            VMEM,
        ],
        out_specs=[VMEM, VMEM],
        out_shape=[
            jax.ShapeDtypeStruct((count, LANES), bf16),
            jax.ShapeDtypeStruct((owners, 8, half), bf16),
        ],
        scratch_shapes=[pltpu.VMEM((1, count, LANES), f32)],
        compiler_params=params(),
        cost_estimate=cost(3),
        name="gather_last",
    )(neg, rank, flat_text, own_dq, home_later, weight_first)

    parts = exchange(weight_local)
    piece = pl.pallas_call(
        total_kernel,
        in_specs=[VMEM],
        out_specs=VMEM,
        out_shape=jax.ShapeDtypeStruct(parts.shape, bf16),
        compiler_params=params(),
        name="total",
    )(parts)
    weight_grad = pl.pallas_call(
        unfold_kernel,
        in_specs=[VMEM],
        out_specs=VMEM,
        out_shape=jax.ShapeDtypeStruct((width, depth), f32),
        compiler_params=params(),
        name="unfold",
    )(exchange(piece))

    mine = texts_here // members
    dq = jnp.concatenate([dq_first, dq_later[:, :HEAD_SIZE]], axis=1)
    dq = dq.reshape(length, texts_here, width)
    text_grad = jnp.zeros((length * mine, depth), f32)
    for r in range(members):
        to = lax.rem(member + r, members)
        block = lax.dynamic_slice_in_dim(dq, to * mine, mine, 1)
        if r:
            block = lax.ppermute(block, "mp", [(i, (i + r) % members) for i in range(members)])
        source = lax.rem(member + members - r, members)
        weight = lax.dynamic_slice_in_dim(all_weight, source * width, width, 0)
        text_grad = text_grad + jnp.dot(
            block.reshape(length * mine, width), weight, preferred_element_type=f32
        )
    text_grad = text_grad.astype(bf16).reshape(length, mine, depth).transpose(1, 0, 2)
    return (text_grad, weight_grad, dkv)


def solution(mesh):
    in_specs = (
        P("dp", None, None),
        P("mp", None),
        P("dp", "mp", None, None),
        P("dp", None, None, None),
        P("dp", None),
    )
    out_specs = (P(("dp", "mp"), None, None), P("mp", None), P("dp", "mp", None, None))
    return jax.shard_map(
        per_device, mesh=mesh, in_specs=in_specs, out_specs=out_specs, check_vma=False
    )
```

```python
import functools

import jax
import jax.numpy as jnp
from jax import lax
from jax.experimental import pallas as pl
from jax.experimental.pallas import tpu as pltpu
from jax.sharding import PartitionSpec as P

HEAD_SIZE = 64
NEG = 3
LANES = 128
TILE = 256
WAYS = 4
PARTS = 4
VMEM_LIMIT = 60 * 1024 * 1024


def cdiv(a, b):
    return -(-a // b)


def lower_half(shape):
    return lax.broadcasted_iota(jnp.int32, shape, len(shape) - 1) < HEAD_SIZE


def request_slots(neg_ref, rank_ref, seen_ref, owners, images_here):
    negatives, texts_here = neg_ref.shape

    def clear(o, carry):
        seen_ref[o] = 0
        return carry

    lax.fori_loop(0, owners, clear, 0)

    def count(t, carry):
        for j in range(negatives):
            o = neg_ref[j, t] // images_here
            c = seen_ref[o]
            rank_ref[j, t] = c
            seen_ref[o] = c + 1
        return carry

    lax.fori_loop(0, texts_here, count, 0)


def joined(g, odd, q):
    g = g.astype(jnp.float32)
    g = jnp.where(odd == 1, g, pltpu.roll(g, HEAD_SIZE, 1))
    return jnp.where(lower_half(g.shape), q, g)


def project(text_ref, weight_ref, query_ref):
    q = lax.dot_general(
        text_ref[...], weight_ref[...], (((1,), (1,)), ((), ())), preferred_element_type=jnp.float32
    )
    q = q.astype(jnp.bfloat16).astype(jnp.float32) * HEAD_SIZE**-0.5
    for h in range(query_ref.shape[0]):
        if h % 2:
            a = (h - 1) * HEAD_SIZE
            query_ref[h] = pltpu.roll(q[:, a : a + LANES], HEAD_SIZE, 1)
        elif (h + 2) * HEAD_SIZE <= q.shape[1]:
            query_ref[h] = q[:, h * HEAD_SIZE : (h + 2) * HEAD_SIZE]
        else:
            query_ref[h, :, :HEAD_SIZE] = q[:, h * HEAD_SIZE :]
            query_ref[h, :, HEAD_SIZE:] = jnp.zeros((q.shape[0], HEAD_SIZE), jnp.float32)


def place_rows(
    first, heads, images_here, odd_ref, neg_ref, rank_ref, query_ref, grad_ref, wire_rows, scr
):
    texts_here, slots, length, _ = grad_ref.shape
    tells = wire_rows >= 2 * heads * length + 2
    if tells:
        scr[...] = jnp.full(scr.shape, -1.0, jnp.float32)

    def one_text(t, carry):
        for h in range(heads):
            q = query_ref[first + h, pl.ds(t, length, stride=texts_here), :]
            place = odd_ref[0] + first + h
            col = pl.multiple_of((place // 2) * LANES, LANES)
            for j in range(slots - 1):
                n = neg_ref[j, t]
                r = rank_ref[j, t]
                o = n // images_here
                row = o * wire_rows + (r * heads + h) * length
                g = grad_ref[t, j + 1, :, pl.ds(col, LANES)]
                scr[pl.ds(row, length), :] = joined(g, lax.rem(place, 2), q)
                if h == 0 and tells:
                    tell = o * wire_rows + 2 * heads * length + r
                    image = (n - o * images_here).astype(jnp.float32)
                    scr[pl.ds(tell, 1), :] = jnp.full((1, LANES), image, jnp.float32)
        return carry

    lax.fori_loop(0, texts_here, one_text, 0)


def pack_first_kernel(
    heads,
    images_here,
    odd_ref,
    neg_ref,
    text_ref,
    weight_ref,
    grad_hbm,
    wire_hbm,
    query_hbm,
    rank_ref,
    scr,
    grad_scr,
    query_scr,
    wire_scr,
    seen_ref,
    sems,
):
    load = pltpu.make_async_copy(grad_hbm, grad_scr, sems.at[0])
    load.start()
    request_slots(neg_ref, rank_ref, seen_ref, wire_scr.shape[0], images_here)
    project(text_ref, weight_ref, query_scr)
    keep = pltpu.make_async_copy(query_scr, query_hbm, sems.at[1])
    keep.start()
    load.wait()
    place_rows(
        0, heads, images_here, odd_ref, neg_ref, rank_ref, query_scr, grad_scr, wire_scr.shape[1], scr
    )
    owners, rows, _ = wire_scr.shape
    part = owners // PARTS
    sends = []
    for p in range(PARTS):
        block = scr[p * part * rows : (p + 1) * part * rows, :]
        wire_scr[p * part : (p + 1) * part] = block.reshape(part, rows, LANES).astype(jnp.bfloat16)
        send = pltpu.make_async_copy(
            wire_scr.at[pl.ds(p * part, part)], wire_hbm.at[pl.ds(p * part, part)], sems.at[2 + p]
        )
        send.start()
        sends.append(send)
    keep.wait()
    for send in sends:
        send.wait()


def pack_later_kernel(
    first, heads, images_here, odd_ref, neg_ref, rank_ref, query_ref, grad_ref, after_ref, wire_ref, scr
):
    place_rows(
        first, heads, images_here, odd_ref, neg_ref, rank_ref, query_ref, grad_ref, wire_ref.shape[1], scr
    )
    wire_ref[...] = scr[...].reshape(wire_ref.shape).astype(jnp.bfloat16)


def load_memory(kv, keys, kv_ref, kkt_ref, padded):
    full = jnp.concatenate([kv, jnp.zeros((padded - keys, LANES), jnp.float32)], axis=0)
    low = lower_half(full.shape)
    k_only = jnp.where(low, full, 0.0)
    kv_ref[:padded, :] = k_only.astype(jnp.bfloat16)
    kv_ref[padded:, :] = jnp.where(low, 0.0, full).astype(jnp.bfloat16)
    twice = k_only + pltpu.roll(k_only, HEAD_SIZE, 1)
    kkt_ref[...] = twice.T.astype(jnp.bfloat16)


def tile_scores(qg, kv, s_scr):
    s_scr[...] = lax.dot_general(
        kv, qg, (((1,), (1,)), ((), ())), preferred_element_type=jnp.float32
    )


def tile_softmax(keys, padded, s_scr, pd_scr):
    tile = s_scr.shape[1]
    bounds = list(range(0, padded, 64)) + [padded]
    chunks = list(zip(bounds[:-1], bounds[1:]))
    top = jnp.full((8, tile), -jnp.inf, jnp.float32)
    for a, b in chunks:
        s = s_scr[a:b, :]
        if b > keys:
            row = lax.broadcasted_iota(jnp.int32, s.shape, 0) + a
            s = jnp.where(row < keys, s, -jnp.inf)
            s_scr[a:b, :] = s
        top = jnp.maximum(top, jnp.max(s.reshape((b - a) // 8, 8, tile), axis=0))
    top = jnp.max(top, axis=0, keepdims=True)
    total = jnp.zeros((8, tile), jnp.float32)
    center = jnp.zeros((8, tile), jnp.float32)
    for a, b in chunks:
        e = jnp.exp(s_scr[a:b, :] - top)
        s_scr[a:b, :] = e
        total = total + jnp.sum(e.reshape((b - a) // 8, 8, tile), axis=0)
        d = e * s_scr[padded + a : padded + b, :]
        center = center + jnp.sum(d.reshape((b - a) // 8, 8, tile), axis=0)
    inverse = 1.0 / jnp.sum(total, axis=0, keepdims=True)
    center = jnp.sum(center, axis=0, keepdims=True) * inverse
    for a, b in chunks:
        p = s_scr[a:b, :] * inverse
        pd_scr[a:b, tile:] = p.astype(jnp.bfloat16)
        ds = p * (s_scr[padded + a : padded + b, :] - center)
        pd_scr[a:b, :tile] = ds.astype(jnp.bfloat16)


def tile_outputs(qg, kkt, pd_scr):
    tile = qg.shape[0]
    low = lower_half(qg.shape)
    zero = jnp.zeros_like(qg)
    both = jnp.concatenate([jnp.where(low, qg, zero), jnp.where(low, zero, qg)], axis=0)
    dkv = jnp.dot(pd_scr[...], both, preferred_element_type=jnp.float32)
    dqt = jnp.dot(kkt, pd_scr[:, :tile], preferred_element_type=jnp.float32)
    return dqt.T * (HEAD_SIZE**-0.5), dkv


def own_kernel(
    keys, padded, texts_here, odd_ref, query_ref, grad_ref, kv_ref, acc_ref, dq_ref, both_ref, kkt_ref, own_scr, s_scr, pd_scr
):
    image, h = pl.program_id(0), pl.program_id(1)
    captions, _, length, _ = grad_ref.shape
    load_memory(kv_ref[0, 0].astype(jnp.float32), keys, both_ref.at[0, 0], kkt_ref.at[0, 0], padded)
    place = odd_ref[0] + h
    col = pl.multiple_of((place // 2) * LANES, LANES)
    own_scr[captions * length :, :] = jnp.zeros((TILE - captions * length, LANES), jnp.float32)
    for c in range(captions):
        q = query_ref[0, pl.ds(image * captions + c, length, stride=texts_here), :]
        g = grad_ref[c, 0, :, pl.ds(col, LANES)]
        own_scr[c * length : (c + 1) * length, :] = joined(g, lax.rem(place, 2), q)
    qg = own_scr[...].astype(jnp.bfloat16)
    tile_scores(qg, both_ref[0, 0], s_scr)
    tile_softmax(keys, padded, s_scr, pd_scr)
    dq, dkv = tile_outputs(qg, kkt_ref[0, 0], pd_scr)
    acc_ref[0, 0] = dkv
    dq_ref[0, 0] = dq


def plan_kernel(length, images, tell, wire_hbm, plan_ref, tail_scr, sem):
    senders, rows, _ = tail_scr.shape
    first = tell // 16 * 16
    copy = pltpu.make_async_copy(wire_hbm.at[:, pl.ds(first, rows), :], tail_scr, sem)
    copy.start()
    copy.wait()
    tail = tail_scr[...].astype(jnp.float32)
    id0, id1 = tail[:, tell - first, :], tail[:, tell - first + 1, :]
    lane = lax.broadcasted_iota(jnp.int32, (senders, LANES), 1)
    image = lane.astype(jnp.float32)
    hot0 = jnp.where(id0 == image, 1.0, 0.0)
    hot1 = jnp.where(id1 == image, 1.0, 0.0)
    both = hot0 + hot1
    row = lax.broadcasted_iota(jnp.int32, (senders, senders), 0)
    col = lax.broadcasted_iota(jnp.int32, (senders, senders), 1)
    before = jnp.where(col < row, 1.0, 0.0).astype(jnp.bfloat16)
    ahead = jnp.dot(before, both.astype(jnp.bfloat16), preferred_element_type=jnp.float32)
    number = jnp.sum(both, axis=0, keepdims=True).astype(jnp.int32)
    tiles = (number * length + (TILE - 1)) // TILE
    tiles = jnp.broadcast_to(tiles, (8, LANES))
    row = lax.broadcasted_iota(jnp.int32, (LANES, LANES), 0)
    col = lax.broadcasted_iota(jnp.int32, (LANES, LANES), 1)
    before = jnp.where(row < col, 1.0, 0.0).astype(jnp.bfloat16)
    first_tile = jnp.dot(
        tiles.astype(jnp.float32).astype(jnp.bfloat16), before, preferred_element_type=jnp.float32
    )
    at = first_tile[0:1] * TILE + ahead * length
    pos0 = jnp.sum(hot0 * at, axis=1, keepdims=True)
    pos1 = jnp.sum(hot1 * (at + hot0 * length), axis=1, keepdims=True)
    pos0 = jnp.where(id0 >= 0, pos0, -1.0)
    pos1 = jnp.where(id1 >= 0, pos1, -1.0)
    plan_ref[:senders, :] = jnp.where(lane == 0, pos0, pos1).astype(jnp.int32)
    low = lax.broadcasted_iota(jnp.int32, (8, LANES), 0)
    plan_ref[senders:, :] = jnp.where(low == 0, first_tile.astype(jnp.int32), tiles)


def far_kernel(
    keys,
    padded,
    length,
    heads,
    plan_ref,
    wire_ref,
    both_ref,
    kkt_ref,
    own_ref,
    *rest,
):
    h = pl.program_id(0)
    images = both_ref.shape[0]
    senders = wire_ref.shape[0]
    dkv_ref, back_ref, rows_scr, acc_scr = rest[-4 - 2 * WAYS : -2 * WAYS]
    pairs = rest[-2 * WAYS :]
    ways = WAYS
    s_scrs, pd_scrs = pairs[:ways], pairs[ways:]

    @pl.when(h == 0)
    def _():
        def clear(start):
            for g in range(heads):
                rows_scr[g, pl.ds(pl.multiple_of(start, TILE), TILE), :] = jnp.zeros(
                    (TILE, LANES), jnp.float32
                )

        for i in range(images):
            n = plan_ref[senders + 1, i]

            @pl.when(n > 0)
            def _():
                clear((plan_ref[senders, i] + n - 1) * TILE)

        end = plan_ref[senders, images - 1] + plan_ref[senders + 1, images - 1]
        for w in range(ways - 1):
            clear((end + w) * TILE)

        def place(s, carry):
            block = wire_ref[s].astype(jnp.float32)
            for r in range(2):
                pos = plan_ref[s, r]

                @pl.when(pos >= 0)
                def _():
                    for g in range(heads):
                        a = (r * heads + g) * length
                        rows_scr[g, pl.ds(pos, length), :] = block[a : a + length]

            return carry

        lax.fori_loop(0, senders, place, 0)

    for i in range(images):
        acc_scr[i] = own_ref[i, 0]
    edges = [plan_ref[senders, i] for i in range(1, images)]
    tiles = plan_ref[senders, images - 1] + plan_ref[senders + 1, images - 1]

    def step(k, carry):
        starts, images_of, rows = [], [], []
        for w in range(ways):
            n = k * ways + w
            image = jnp.int32(0)
            for e in edges:
                image = image + (n >= e).astype(jnp.int32)
            start = pl.multiple_of(n * TILE, TILE)
            qg = rows_scr[h, pl.ds(start, TILE), :].astype(jnp.bfloat16)
            starts.append(start)
            images_of.append(image)
            rows.append(qg)
            tile_scores(qg, both_ref[image, 0], s_scrs[w])
        for w in range(ways):
            tile_softmax(keys, padded, s_scrs[w], pd_scrs[w])
            dq, dkv = tile_outputs(rows[w], kkt_ref[images_of[w], 0], pd_scrs[w])
            acc_scr[images_of[w]] += dkv
            rows_scr[h, pl.ds(starts[w], TILE), :] = dq
        return carry

    lax.fori_loop(0, (tiles + ways - 1) // ways, step, 0)
    for i in range(images):
        dkv_ref[i, 0] = acc_scr[i, :keys, :].astype(jnp.bfloat16)

    @pl.when(h == heads - 1)
    def _():
        rows = back_ref.shape[1]
        low = lower_half((length, LANES))
        spare = rows - heads * length

        def give(s, carry):
            p0 = jnp.maximum(plan_ref[s, 0], 0)
            p1 = jnp.maximum(plan_ref[s, 1], 0)
            parts = []
            for g in range(heads):
                x0 = rows_scr[g, pl.ds(p0, length), :]
                x1 = rows_scr[g, pl.ds(p1, length), :]
                parts.append(jnp.where(low, x0, x1))
            if spare:
                parts.append(jnp.zeros((spare, LANES), jnp.float32))
            back_ref[s] = jnp.concatenate(parts, axis=0).astype(jnp.bfloat16)
            return carry

        lax.fori_loop(0, senders, give, 0)


def sum_requests(heads, length, images_here, neg_ref, rank_ref, own_ref, back_ref, sum_scr, text_scr):
    texts_here = sum_scr.shape[1] // length
    captions = texts_here // images_here

    def one(t, carry):
        image = t // captions
        totals = [
            own_ref[image, h, pl.ds((t - image * captions) * length, length), :]
            for h in range(heads)
        ]
        for j in range(NEG):
            block = back_ref[neg_ref[j, t] // images_here].astype(jnp.float32)
            block = jnp.where(rank_ref[j, t] == 1, pltpu.roll(block, HEAD_SIZE, 1), block)
            for h in range(heads):
                totals[h] = totals[h] + block[h * length : (h + 1) * length]
        for h in range(heads):
            sum_scr[h, pl.ds(t, length, stride=texts_here), :] = totals[h]
            text_scr[h, pl.ds(t * length, length), :] = totals[h]
        return carry

    lax.fori_loop(0, texts_here, one, 0)


def gather_two_kernel(
    length, images_here, neg_ref, rank_ref, text_ref, own_ref, back_ref, dq_ref, weight_ref, sum_scr, text_scr
):
    sum_requests(2, length, images_here, neg_ref, rank_ref, own_ref, back_ref, sum_scr, text_scr)
    members, mine, _ = dq_ref.shape

    def paired(x0, x1):
        x = jnp.where(lower_half(x0.shape), x0, pltpu.roll(x1, HEAD_SIZE, 1))
        return x.astype(jnp.bfloat16)

    for m in range(members):
        at = slice(m * mine, (m + 1) * mine)
        dq_ref[m] = paired(text_scr[0, at, :], text_scr[1, at, :])
    dq = paired(sum_scr[0], sum_scr[1])
    weight_ref[...] = lax.dot_general(
        dq, text_ref[...], (((0,), (0,)), ((), ())), preferred_element_type=jnp.float32
    )


def gather_last_kernel(
    length, images_here, neg_ref, rank_ref, text_ref, own_ref, back_ref, head_ref, after_ref, dq_ref, weight_ref, sum_scr, text_scr
):
    sum_requests(1, length, images_here, neg_ref, rank_ref, own_ref, back_ref, sum_scr, text_scr)
    members, mine, _ = dq_ref.shape
    for m in range(members):
        dq_ref[m] = text_scr[0, m * mine : (m + 1) * mine, :].astype(jnp.bfloat16)
    dq = sum_scr[0].astype(jnp.bfloat16)
    last = lax.dot_general(
        dq, text_ref[...], (((0,), (0,)), ((), ())), preferred_element_type=jnp.float32
    )
    half = weight_ref.shape[2]
    before = head_ref.shape[0] // 8
    for b in range(before + HEAD_SIZE // 8):
        rows = head_ref[b * 8 : b * 8 + 8, :] if b < before else last[(b - before) * 8 : (b - before) * 8 + 8]
        for side in range(2):
            weight_ref[2 * b + side] = rows[:, side * half : (side + 1) * half].astype(jnp.bfloat16)


def total_kernel(parts_ref, out_ref):
    total = parts_ref[0].astype(jnp.float32)
    for d in range(1, parts_ref.shape[0]):
        total = total + parts_ref[d].astype(jnp.float32)
    total = total.astype(jnp.bfloat16)
    for d in range(out_ref.shape[0]):
        out_ref[d] = total


def unfold_kernel(pieces_ref, out_ref):
    half = pieces_ref.shape[2]
    for b in range(out_ref.shape[0] // 8):
        for side in range(2):
            out_ref[b * 8 : b * 8 + 8, side * half : (side + 1) * half] = pieces_ref[
                2 * b + side
            ].astype(jnp.float32)


def params():
    return pltpu.CompilerParams(vmem_limit_bytes=VMEM_LIMIT)


def cost(us):
    return pl.CostEstimate(
        flops=int(us * 1e6 * 1150 / 2), bytes_accessed=int(us * 1e-6 * 3.6e12), transcendentals=0
    )


SMEM = pl.BlockSpec(memory_space=pltpu.SMEM)
VMEM = pl.BlockSpec(memory_space=pltpu.VMEM)
ANY = pl.BlockSpec(memory_space=pl.ANY)


def math_scratch(padded, ways):
    return [pltpu.VMEM((2 * padded, TILE), jnp.float32)] * ways + [
        pltpu.VMEM((padded, 2 * TILE), jnp.bfloat16)
    ] * ways


def far_call(plan, wire, first, many, both, kkt, own_acc, dkv, keys, us, length):
    owners, rows, _ = wire.shape
    images, all_heads, padded, _ = own_acc.shape
    more = () if dkv is None else (dkv,)
    back_rows = cdiv(many * length, 8) * 8
    most = (2 * owners * length) // TILE + images + WAYS - 1
    return pl.pallas_call(
        functools.partial(far_kernel, keys, padded, length, many),
        grid=(many,),
        in_specs=[
            SMEM,
            pl.BlockSpec((owners, rows, LANES), lambda h: (0, 0, 0)),
            pl.BlockSpec((images, 1, 2 * padded, LANES), lambda h: (0, first + h, 0, 0)),
            pl.BlockSpec((images, 1, LANES, padded), lambda h: (0, first + h, 0, 0)),
            pl.BlockSpec((images, 1, padded, LANES), lambda h: (0, first + h, 0, 0)),
        ]
        + [ANY] * len(more),
        out_specs=[
            pl.BlockSpec((images, 1, keys, LANES), lambda h: (0, first + h, 0, 0)),
            pl.BlockSpec((owners, back_rows, LANES), lambda h: (0, 0, 0)),
        ],
        out_shape=[
            jax.ShapeDtypeStruct((images, all_heads, keys, LANES), jnp.bfloat16),
            jax.ShapeDtypeStruct((owners, back_rows, LANES), jnp.bfloat16),
        ],
        scratch_shapes=[
            pltpu.VMEM((many, most * TILE + 64, LANES), jnp.float32),
            pltpu.VMEM((images, padded, LANES), jnp.float32),
        ]
        + math_scratch(padded, WAYS),
        input_output_aliases={5: 0} if more else {},
        compiler_params=params(),
        cost_estimate=cost(us),
        name="far" + str(first),
    )(plan, wire, both, kkt, own_acc, *more)


def exchange(x):
    return lax.all_to_all(x, "dp", split_axis=0, concat_axis=0, tiled=True)


def per_device(texts, query_weight, patch_key_value, grad_out, negatives):
    owners = lax.axis_size("dp")
    members = lax.axis_size("mp")
    member = lax.axis_index("mp")
    texts_here, length, depth = texts.shape
    images_here, heads, keys, _ = patch_key_value.shape
    width = query_weight.shape[0]
    captions = texts_here // images_here
    padded = cdiv(keys, 16) * 16
    count = texts_here * length
    bf16, f32, i32 = jnp.bfloat16, jnp.float32, jnp.int32
    early = heads - 1
    first_rows = cdiv(2 * early * length + 2, 8) * 8
    later_rows = cdiv(2 * length, 8) * 8

    flat_text = texts.transpose(1, 0, 2).reshape(count, depth)
    neg = negatives.T
    all_weight = lax.all_gather(query_weight, "mp", axis=0, tiled=True)
    start_col = member * width // LANES * LANES
    odd = ((member * width - start_col) // HEAD_SIZE).reshape(1).astype(i32)
    window = lax.dynamic_slice_in_dim(grad_out, start_col, 2 * LANES, 3)

    wire_first, query, rank = pl.pallas_call(
        functools.partial(pack_first_kernel, early, images_here),
        in_specs=[SMEM, SMEM, VMEM, VMEM, ANY],
        out_specs=[ANY, ANY, SMEM],
        out_shape=[
            jax.ShapeDtypeStruct((owners, first_rows, LANES), bf16),
            jax.ShapeDtypeStruct((heads, count, LANES), f32),
            jax.ShapeDtypeStruct(neg.shape, i32),
        ],
        scratch_shapes=[
            pltpu.VMEM((owners * first_rows, LANES), f32),
            pltpu.VMEM(window.shape, bf16),
            pltpu.VMEM((heads, count, LANES), f32),
            pltpu.VMEM((owners, first_rows, LANES), bf16),
            pltpu.SMEM((owners,), i32),
            pltpu.SemaphoreType.DMA((2 + PARTS,)),
        ],
        compiler_params=params(),
        cost_estimate=cost(5),
        name="pack_first",
    )(odd, neg, flat_text, query_weight, window)
    got_first = exchange(wire_first)

    own_acc, own_dq, both, kkt = pl.pallas_call(
        functools.partial(own_kernel, keys, padded, texts_here),
        grid=(images_here, heads),
        in_specs=[
            SMEM,
            pl.BlockSpec((1, count, LANES), lambda i, h: (h, 0, 0)),
            pl.BlockSpec((captions, 1, length, 2 * LANES), lambda i, h: (i, 0, 0, 0)),
            pl.BlockSpec((1, 1, keys, LANES), lambda i, h: (i, h, 0, 0)),
        ],
        out_specs=[
            pl.BlockSpec((1, 1, padded, LANES), lambda i, h: (i, h, 0, 0)),
            pl.BlockSpec((1, 1, TILE, LANES), lambda i, h: (i, h, 0, 0)),
            pl.BlockSpec((1, 1, 2 * padded, LANES), lambda i, h: (i, h, 0, 0)),
            pl.BlockSpec((1, 1, LANES, padded), lambda i, h: (i, h, 0, 0)),
        ],
        out_shape=[
            jax.ShapeDtypeStruct((images_here, heads, padded, LANES), f32),
            jax.ShapeDtypeStruct((images_here, heads, TILE, LANES), f32),
            jax.ShapeDtypeStruct((images_here, heads, 2 * padded, LANES), bf16),
            jax.ShapeDtypeStruct((images_here, heads, LANES, padded), bf16),
        ],
        scratch_shapes=[pltpu.VMEM((TILE, LANES), f32)] + math_scratch(padded, 1),
        compiler_params=params(),
        cost_estimate=cost(13),
        name="own",
    )(odd, query, window, patch_key_value)

    wire_later = pl.pallas_call(
        functools.partial(pack_later_kernel, early, heads - early, images_here),
        in_specs=[SMEM, SMEM, SMEM, VMEM, VMEM, ANY],
        out_specs=VMEM,
        out_shape=jax.ShapeDtypeStruct((owners, later_rows, LANES), bf16),
        scratch_shapes=[pltpu.VMEM((owners * later_rows, LANES), f32)],
        compiler_params=params(),
        cost_estimate=cost(4),
        name="pack_later",
    )(odd, neg, rank, query, window, own_acc)
    got_later = exchange(wire_later)

    tell = 2 * early * length
    plan = pl.pallas_call(
        functools.partial(plan_kernel, length, images_here, tell),
        in_specs=[ANY],
        out_specs=VMEM,
        out_shape=jax.ShapeDtypeStruct((owners + 8, LANES), i32),
        scratch_shapes=[
            pltpu.VMEM((owners, first_rows - tell // 16 * 16, LANES), bf16),
            pltpu.SemaphoreType.DMA,
        ],
        compiler_params=params(),
        cost_estimate=cost(2),
        name="plan",
    )(got_first)

    dkv, back_first = far_call(
        plan, got_first, 0, early, both, kkt, own_acc, None, keys, 22, length
    )
    home_first = exchange(back_first)
    dkv, back_later = far_call(
        plan, got_later, early, heads - early, both, kkt, own_acc, dkv, keys, 12, length
    )
    home_later = exchange(back_later)

    half = depth // 2
    dq_first, weight_first = pl.pallas_call(
        functools.partial(gather_two_kernel, length, images_here),
        grid=(1,),
        in_specs=[
            SMEM,
            SMEM,
            VMEM,
            pl.BlockSpec((images_here, early, TILE, LANES), lambda n: (0, 0, 0, 0)),
            VMEM,
        ],
        out_specs=[VMEM, VMEM],
        out_shape=[
            jax.ShapeDtypeStruct((members, count // members, LANES), bf16),
            jax.ShapeDtypeStruct((early * HEAD_SIZE, depth), f32),
        ],
        scratch_shapes=[pltpu.VMEM((early, count, LANES), f32)] * 2,
        compiler_params=params(),
        cost_estimate=cost(4),
        name="gather_two",
    )(neg, rank, flat_text, own_dq, home_first)
    def swap(dq):
        rows = []
        for r in range(members):
            block = lax.dynamic_index_in_dim(dq, lax.rem(member + r, members), 0, False)
            if r:
                block = lax.ppermute(block, "mp", [(i, (i + r) % members) for i in range(members)])
            rows.append(block)
        return rows

    def text_part(rows, skip, wide):
        total = None
        for r in range(members):
            source = lax.rem(member + members - r, members)
            weight = lax.dynamic_slice_in_dim(all_weight, source * width + skip, wide, 0)
            part = jnp.dot(rows[r][:, :wide], weight, preferred_element_type=f32)
            total = part if total is None else total + part
        return total

    rows_first = swap(dq_first)
    dq_later, weight_local = pl.pallas_call(
        functools.partial(gather_last_kernel, length, images_here),
        grid=(1,),
        in_specs=[
            SMEM,
            SMEM,
            VMEM,
            pl.BlockSpec((images_here, 1, TILE, LANES), lambda n: (0, early, 0, 0)),
            VMEM,
            VMEM,
            ANY,
        ],
        out_specs=[VMEM, VMEM],
        out_shape=[
            jax.ShapeDtypeStruct((members, count // members, LANES), bf16),
            jax.ShapeDtypeStruct((owners, 8, half), bf16),
        ],
        scratch_shapes=[pltpu.VMEM((1, count, LANES), f32)] * 2,
        compiler_params=params(),
        cost_estimate=cost(3),
        name="gather_last",
    )(neg, rank, flat_text, own_dq, home_later, weight_first, rows_first[-1])

    parts = exchange(weight_local)
    piece = pl.pallas_call(
        total_kernel,
        in_specs=[VMEM],
        out_specs=VMEM,
        out_shape=jax.ShapeDtypeStruct(parts.shape, bf16),
        compiler_params=params(),
        name="total",
    )(parts)
    weight_grad = pl.pallas_call(
        unfold_kernel,
        in_specs=[VMEM],
        out_specs=VMEM,
        out_shape=jax.ShapeDtypeStruct((width, depth), f32),
        compiler_params=params(),
        name="unfold",
    )(exchange(piece))

    rows_later = swap(dq_later)
    text_grad = text_part(rows_first, 0, early * HEAD_SIZE)
    text_grad = text_grad + text_part(rows_later, early * HEAD_SIZE, (heads - early) * HEAD_SIZE)
    text_grad = text_grad.astype(bf16).reshape(texts_here // members, length, depth)
    return (text_grad, weight_grad, dkv)


def solution(mesh):
    in_specs = (
        P("dp", None, None),
        P("mp", None),
        P("dp", "mp", None, None),
        P("dp", None, None, None),
        P("dp", None),
    )
    out_specs = (P(("dp", "mp"), None, None), P("mp", None), P("dp", "mp", None, None))
    return jax.shard_map(
        per_device, mesh=mesh, in_specs=in_specs, out_specs=out_specs, check_vma=False
    )
```

```python
import functools

import jax
import jax.numpy as jnp
from jax import lax
from jax.experimental import pallas as pl
from jax.experimental.pallas import tpu as pltpu
from jax.sharding import PartitionSpec as P

HEAD_SIZE = 64
NEG = 3
LANES = 128
TILE = 256
WAYS = 4
PARTS = 4
VMEM_LIMIT = 60 * 1024 * 1024


def cdiv(a, b):
    return -(-a // b)


def lower_half(shape):
    return lax.broadcasted_iota(jnp.int32, shape, len(shape) - 1) < HEAD_SIZE


def request_slots(neg_ref, rank_ref, seen_ref, owners, images_here):
    negatives, texts_here = neg_ref.shape

    def clear(o, carry):
        seen_ref[o] = 0
        return carry

    lax.fori_loop(0, owners, clear, 0)

    def count(t, carry):
        for j in range(negatives):
            o = neg_ref[j, t] // images_here
            c = seen_ref[o]
            rank_ref[j, t] = c
            seen_ref[o] = c + 1
        return carry

    lax.fori_loop(0, texts_here, count, 0)


def joined(g, odd, q):
    g = g.astype(jnp.float32)
    g = jnp.where(odd == 1, g, pltpu.roll(g, HEAD_SIZE, 1))
    return jnp.where(lower_half(g.shape), q, g)


def project(text_ref, weight_ref, query_ref):
    q = lax.dot_general(
        text_ref[...], weight_ref[...], (((1,), (1,)), ((), ())), preferred_element_type=jnp.float32
    )
    q = q.astype(jnp.bfloat16).astype(jnp.float32) * HEAD_SIZE**-0.5
    for h in range(query_ref.shape[0]):
        if h % 2:
            a = (h - 1) * HEAD_SIZE
            query_ref[h] = pltpu.roll(q[:, a : a + LANES], HEAD_SIZE, 1)
        elif (h + 2) * HEAD_SIZE <= q.shape[1]:
            query_ref[h] = q[:, h * HEAD_SIZE : (h + 2) * HEAD_SIZE]
        else:
            query_ref[h, :, :HEAD_SIZE] = q[:, h * HEAD_SIZE :]
            query_ref[h, :, HEAD_SIZE:] = jnp.zeros((q.shape[0], HEAD_SIZE), jnp.float32)


def place_rows(
    first, heads, images_here, odd_ref, neg_ref, rank_ref, query_ref, grad_ref, wire_rows, scr
):
    texts_here, slots, length, _ = grad_ref.shape
    tells = wire_rows >= 2 * heads * length + 2
    if tells:
        scr[...] = jnp.full(scr.shape, -1.0, jnp.float32)

    def one_text(t, carry):
        for h in range(heads):
            q = query_ref[first + h, pl.ds(t, length, stride=texts_here), :]
            place = odd_ref[0] + first + h
            col = pl.multiple_of((place // 2) * LANES, LANES)
            for j in range(slots - 1):
                n = neg_ref[j, t]
                r = rank_ref[j, t]
                o = n // images_here
                row = o * wire_rows + (r * heads + h) * length
                g = grad_ref[t, j + 1, :, pl.ds(col, LANES)]
                scr[pl.ds(row, length), :] = joined(g, lax.rem(place, 2), q)
                if h == 0 and tells:
                    tell = o * wire_rows + 2 * heads * length + r
                    image = (n - o * images_here).astype(jnp.float32)
                    scr[pl.ds(tell, 1), :] = jnp.full((1, LANES), image, jnp.float32)
        return carry

    lax.fori_loop(0, texts_here, one_text, 0, unroll=2)


def pack_first_kernel(
    heads,
    images_here,
    odd_ref,
    neg_ref,
    text_ref,
    weight_ref,
    grad_hbm,
    wire_hbm,
    query_hbm,
    rank_ref,
    scr,
    grad_scr,
    query_scr,
    wire_scr,
    seen_ref,
    sems,
):
    load = pltpu.make_async_copy(grad_hbm, grad_scr, sems.at[0])
    load.start()
    request_slots(neg_ref, rank_ref, seen_ref, wire_scr.shape[0], images_here)
    project(text_ref, weight_ref, query_scr)
    keep = pltpu.make_async_copy(query_scr, query_hbm, sems.at[1])
    keep.start()
    load.wait()
    place_rows(
        0, heads, images_here, odd_ref, neg_ref, rank_ref, query_scr, grad_scr, wire_scr.shape[1], scr
    )
    owners, rows, _ = wire_scr.shape
    part = owners // PARTS
    sends = []
    for p in range(PARTS):
        block = scr[p * part * rows : (p + 1) * part * rows, :]
        wire_scr[p * part : (p + 1) * part] = block.reshape(part, rows, LANES).astype(jnp.bfloat16)
        send = pltpu.make_async_copy(
            wire_scr.at[pl.ds(p * part, part)], wire_hbm.at[pl.ds(p * part, part)], sems.at[2 + p]
        )
        send.start()
        sends.append(send)
    keep.wait()
    for send in sends:
        send.wait()


def pack_later_kernel(
    first, heads, images_here, odd_ref, neg_ref, rank_ref, query_ref, grad_ref, after_ref, wire_ref, scr
):
    place_rows(
        first, heads, images_here, odd_ref, neg_ref, rank_ref, query_ref, grad_ref, wire_ref.shape[1], scr
    )
    wire_ref[...] = scr[...].reshape(wire_ref.shape).astype(jnp.bfloat16)


def load_memory(kv, keys, kv_ref, kkt_ref, padded):
    full = jnp.concatenate([kv, jnp.zeros((padded - keys, LANES), jnp.float32)], axis=0)
    low = lower_half(full.shape)
    k_only = jnp.where(low, full, 0.0)
    kv_ref[:padded, :] = k_only.astype(jnp.bfloat16)
    kv_ref[padded:, :] = jnp.where(low, 0.0, full).astype(jnp.bfloat16)
    twice = k_only + pltpu.roll(k_only, HEAD_SIZE, 1)
    kkt_ref[...] = twice.T.astype(jnp.bfloat16)


def tile_scores(qg, kv, s_scr):
    s_scr[...] = lax.dot_general(
        kv, qg, (((1,), (1,)), ((), ())), preferred_element_type=jnp.float32
    )


def tile_softmax(keys, padded, s_scr, pd_scr):
    tile = s_scr.shape[1]
    bounds = list(range(0, padded, 64)) + [padded]
    chunks = list(zip(bounds[:-1], bounds[1:]))
    top = jnp.full((8, tile), -jnp.inf, jnp.float32)
    for a, b in chunks:
        s = s_scr[a:b, :]
        if b > keys:
            row = lax.broadcasted_iota(jnp.int32, s.shape, 0) + a
            s = jnp.where(row < keys, s, -jnp.inf)
            s_scr[a:b, :] = s
        top = jnp.maximum(top, jnp.max(s.reshape((b - a) // 8, 8, tile), axis=0))
    top = jnp.max(top, axis=0, keepdims=True)
    total = jnp.zeros((8, tile), jnp.float32)
    center = jnp.zeros((8, tile), jnp.float32)
    for a, b in chunks:
        e = jnp.exp(s_scr[a:b, :] - top)
        s_scr[a:b, :] = e
        total = total + jnp.sum(e.reshape((b - a) // 8, 8, tile), axis=0)
        d = e * s_scr[padded + a : padded + b, :]
        center = center + jnp.sum(d.reshape((b - a) // 8, 8, tile), axis=0)
    inverse = 1.0 / jnp.sum(total, axis=0, keepdims=True)
    center = jnp.sum(center, axis=0, keepdims=True) * inverse
    for a, b in chunks:
        p = s_scr[a:b, :] * inverse
        pd_scr[a:b, tile:] = p.astype(jnp.bfloat16)
        ds = p * (s_scr[padded + a : padded + b, :] - center)
        pd_scr[a:b, :tile] = ds.astype(jnp.bfloat16)


def tile_outputs(qg, kkt, pd_scr):
    tile = qg.shape[0]
    low = lower_half(qg.shape)
    zero = jnp.zeros_like(qg)
    both = jnp.concatenate([jnp.where(low, qg, zero), jnp.where(low, zero, qg)], axis=0)
    dkv = jnp.dot(pd_scr[...], both, preferred_element_type=jnp.float32)
    dqt = jnp.dot(kkt, pd_scr[:, :tile], preferred_element_type=jnp.float32)
    return dqt.T * (HEAD_SIZE**-0.5), dkv


def own_kernel(
    keys, padded, texts_here, odd_ref, query_ref, grad_ref, kv_ref, acc_ref, dq_ref, both_ref, kkt_ref, own_scr, s_scr, pd_scr
):
    image, h = pl.program_id(0), pl.program_id(1)
    captions, _, length, _ = grad_ref.shape
    load_memory(kv_ref[0, 0].astype(jnp.float32), keys, both_ref.at[0, 0], kkt_ref.at[0, 0], padded)
    place = odd_ref[0] + h
    col = pl.multiple_of((place // 2) * LANES, LANES)
    own_scr[captions * length :, :] = jnp.zeros((TILE - captions * length, LANES), jnp.float32)
    for c in range(captions):
        q = query_ref[0, pl.ds(image * captions + c, length, stride=texts_here), :]
        g = grad_ref[c, 0, :, pl.ds(col, LANES)]
        own_scr[c * length : (c + 1) * length, :] = joined(g, lax.rem(place, 2), q)
    qg = own_scr[...].astype(jnp.bfloat16)
    tile_scores(qg, both_ref[0, 0], s_scr)
    tile_softmax(keys, padded, s_scr, pd_scr)
    dq, dkv = tile_outputs(qg, kkt_ref[0, 0], pd_scr)
    acc_ref[0, 0] = dkv
    dq_ref[0, 0] = dq


def plan_kernel(length, images, tell, wire_hbm, plan_ref, tail_scr, sem):
    senders, rows, _ = tail_scr.shape
    first = tell // 16 * 16
    copy = pltpu.make_async_copy(wire_hbm.at[:, pl.ds(first, rows), :], tail_scr, sem)
    copy.start()
    copy.wait()
    tail = tail_scr[...].astype(jnp.float32)
    id0, id1 = tail[:, tell - first, :], tail[:, tell - first + 1, :]
    lane = lax.broadcasted_iota(jnp.int32, (senders, LANES), 1)
    image = lane.astype(jnp.float32)
    hot0 = jnp.where(id0 == image, 1.0, 0.0)
    hot1 = jnp.where(id1 == image, 1.0, 0.0)
    both = hot0 + hot1
    row = lax.broadcasted_iota(jnp.int32, (senders, senders), 0)
    col = lax.broadcasted_iota(jnp.int32, (senders, senders), 1)
    before = jnp.where(col < row, 1.0, 0.0).astype(jnp.bfloat16)
    ahead = jnp.dot(before, both.astype(jnp.bfloat16), preferred_element_type=jnp.float32)
    number = jnp.sum(both, axis=0, keepdims=True).astype(jnp.int32)
    tiles = (number * length + (TILE - 1)) // TILE
    tiles = jnp.broadcast_to(tiles, (8, LANES))
    row = lax.broadcasted_iota(jnp.int32, (LANES, LANES), 0)
    col = lax.broadcasted_iota(jnp.int32, (LANES, LANES), 1)
    before = jnp.where(row < col, 1.0, 0.0).astype(jnp.bfloat16)
    first_tile = jnp.dot(
        tiles.astype(jnp.float32).astype(jnp.bfloat16), before, preferred_element_type=jnp.float32
    )
    at = first_tile[0:1] * TILE + ahead * length
    pos0 = jnp.sum(hot0 * at, axis=1, keepdims=True)
    pos1 = jnp.sum(hot1 * (at + hot0 * length), axis=1, keepdims=True)
    pos0 = jnp.where(id0 >= 0, pos0, -1.0)
    pos1 = jnp.where(id1 >= 0, pos1, -1.0)
    plan_ref[:senders, :] = jnp.where(lane == 0, pos0, pos1).astype(jnp.int32)
    low = lax.broadcasted_iota(jnp.int32, (8, LANES), 0)
    plan_ref[senders:, :] = jnp.where(low == 0, first_tile.astype(jnp.int32), tiles)


def far_kernel(
    keys,
    padded,
    length,
    heads,
    plan_ref,
    wire_ref,
    both_ref,
    kkt_ref,
    own_ref,
    *rest,
):
    h = pl.program_id(0)
    images = both_ref.shape[0]
    senders = wire_ref.shape[0]
    dkv_ref, back_ref, rows_scr, acc_scr = rest[-4 - 2 * WAYS : -2 * WAYS]
    pairs = rest[-2 * WAYS :]
    ways = WAYS
    s_scrs, pd_scrs = pairs[:ways], pairs[ways:]

    @pl.when(h == 0)
    def _():
        def clear(start):
            for g in range(heads):
                rows_scr[g, pl.ds(pl.multiple_of(start, TILE), TILE), :] = jnp.zeros(
                    (TILE, LANES), jnp.float32
                )

        for i in range(images):
            n = plan_ref[senders + 1, i]

            @pl.when(n > 0)
            def _():
                clear((plan_ref[senders, i] + n - 1) * TILE)

        end = plan_ref[senders, images - 1] + plan_ref[senders + 1, images - 1]
        for w in range(ways - 1):
            clear((end + w) * TILE)

        def place(s, carry):
            block = wire_ref[s].astype(jnp.float32)
            for r in range(2):
                pos = plan_ref[s, r]

                @pl.when(pos >= 0)
                def _():
                    for g in range(heads):
                        a = (r * heads + g) * length
                        rows_scr[g, pl.ds(pos, length), :] = block[a : a + length]

            return carry

        lax.fori_loop(0, senders, place, 0, unroll=4)

    for i in range(images):
        acc_scr[i] = own_ref[i, 0]
    edges = [plan_ref[senders, i] for i in range(1, images)]
    tiles = plan_ref[senders, images - 1] + plan_ref[senders + 1, images - 1]

    def step(k, carry):
        starts, images_of, rows = [], [], []
        for w in range(ways):
            n = k * ways + w
            image = jnp.int32(0)
            for e in edges:
                image = image + (n >= e).astype(jnp.int32)
            start = pl.multiple_of(n * TILE, TILE)
            qg = rows_scr[h, pl.ds(start, TILE), :].astype(jnp.bfloat16)
            starts.append(start)
            images_of.append(image)
            rows.append(qg)
            tile_scores(qg, both_ref[image, 0], s_scrs[w])
        for w in range(ways):
            tile_softmax(keys, padded, s_scrs[w], pd_scrs[w])
            dq, dkv = tile_outputs(rows[w], kkt_ref[images_of[w], 0], pd_scrs[w])
            acc_scr[images_of[w]] += dkv
            rows_scr[h, pl.ds(starts[w], TILE), :] = dq
        return carry

    lax.fori_loop(0, (tiles + ways - 1) // ways, step, 0)
    for i in range(images):
        dkv_ref[i, 0] = acc_scr[i, :keys, :].astype(jnp.bfloat16)

    @pl.when(h == heads - 1)
    def _():
        rows = back_ref.shape[1]
        low = lower_half((length, LANES))
        spare = rows - heads * length

        def give(s, carry):
            p0 = jnp.maximum(plan_ref[s, 0], 0)
            p1 = jnp.maximum(plan_ref[s, 1], 0)
            parts = []
            for g in range(heads):
                x0 = rows_scr[g, pl.ds(p0, length), :]
                x1 = rows_scr[g, pl.ds(p1, length), :]
                parts.append(jnp.where(low, x0, x1))
            if spare:
                parts.append(jnp.zeros((spare, LANES), jnp.float32))
            back_ref[s] = jnp.concatenate(parts, axis=0).astype(jnp.bfloat16)
            return carry

        lax.fori_loop(0, senders, give, 0, unroll=4)


def sum_requests(heads, length, images_here, neg_ref, rank_ref, own_ref, back_ref, sum_scr, text_scr):
    texts_here = sum_scr.shape[1] // length
    captions = texts_here // images_here

    def one(t, carry):
        image = t // captions
        totals = [
            own_ref[image, h, pl.ds((t - image * captions) * length, length), :]
            for h in range(heads)
        ]
        for j in range(NEG):
            block = back_ref[neg_ref[j, t] // images_here].astype(jnp.float32)
            block = jnp.where(rank_ref[j, t] == 1, pltpu.roll(block, HEAD_SIZE, 1), block)
            for h in range(heads):
                totals[h] = totals[h] + block[h * length : (h + 1) * length]
        for h in range(heads):
            sum_scr[h, pl.ds(t, length, stride=texts_here), :] = totals[h]
            text_scr[h, pl.ds(t * length, length), :] = totals[h]
        return carry

    lax.fori_loop(0, texts_here, one, 0, unroll=2)


def gather_two_kernel(
    length, images_here, neg_ref, rank_ref, text_ref, own_ref, back_ref, dq_ref, weight_ref, sum_scr, text_scr
):
    sum_requests(2, length, images_here, neg_ref, rank_ref, own_ref, back_ref, sum_scr, text_scr)
    members, mine, _ = dq_ref.shape

    def paired(x0, x1):
        x = jnp.where(lower_half(x0.shape), x0, pltpu.roll(x1, HEAD_SIZE, 1))
        return x.astype(jnp.bfloat16)

    for m in range(members):
        at = slice(m * mine, (m + 1) * mine)
        dq_ref[m] = paired(text_scr[0, at, :], text_scr[1, at, :])
    dq = paired(sum_scr[0], sum_scr[1])
    weight_ref[...] = lax.dot_general(
        dq, text_ref[...], (((0,), (0,)), ((), ())), preferred_element_type=jnp.float32
    )


def gather_last_kernel(
    length,
    images_here,
    core_ref,
    neg_ref,
    rank_ref,
    text_ref,
    own_ref,
    back_ref,
    head_ref,
    after_ref,
    dq_ref,
    keep_ref,
    give_ref,
    sum_scr,
    text_scr,
    cut_scr,
):
    sum_requests(1, length, images_here, neg_ref, rank_ref, own_ref, back_ref, sum_scr, text_scr)
    members, mine, _ = dq_ref.shape
    for m in range(members):
        dq_ref[m] = text_scr[0, m * mine : (m + 1) * mine, :].astype(jnp.bfloat16)
    dq = sum_scr[0].astype(jnp.bfloat16)
    last = lax.dot_general(
        dq, text_ref[...], (((0,), (0,)), ((), ())), preferred_element_type=jnp.float32
    )
    half = cut_scr.shape[3]
    before = head_ref.shape[0] // 8
    blocks = before + HEAD_SIZE // 8
    for b in range(blocks):
        rows = head_ref[b * 8 : b * 8 + 8, :] if b < before else last[(b - before) * 8 : (b - before) * 8 + 8]
        for side in range(2):
            cut_scr[2 * b // blocks, 2 * b % blocks + side] = rows[:, side * half : (side + 1) * half]
    core = core_ref[0]
    keep_ref[...] = cut_scr[core]
    give_ref[...] = cut_scr[1 - core].astype(jnp.bfloat16)


def pair_kernel(keep_ref, got_ref, dq_ref, out_ref, same_ref):
    pieces = keep_ref.shape[0]
    out_ref[:pieces] = (keep_ref[...] + got_ref[...].astype(jnp.float32)).astype(jnp.bfloat16)


def total_kernel(parts_ref, out_ref):
    total = parts_ref[0].astype(jnp.float32)
    for d in range(1, parts_ref.shape[0]):
        total = total + parts_ref[d].astype(jnp.float32)
    total = total.astype(jnp.bfloat16)
    for d in range(out_ref.shape[0]):
        out_ref[d] = total


def unfold_kernel(core_ref, mine_ref, other_ref, out_ref):
    half = mine_ref.shape[2]
    rows = out_ref.shape[0] // 2
    for which, ref in ((core_ref[0], mine_ref), (1 - core_ref[0], other_ref)):
        for b in range(rows // 8):
            at = pl.ds(pl.multiple_of(which * rows + b * 8, 8), 8)
            for side in range(2):
                out_ref[at, side * half : (side + 1) * half] = ref[2 * b + side].astype(jnp.float32)


def params():
    return pltpu.CompilerParams(vmem_limit_bytes=VMEM_LIMIT)


def cost(us):
    return pl.CostEstimate(
        flops=int(us * 1e6 * 1150 / 2), bytes_accessed=int(us * 1e-6 * 3.6e12), transcendentals=0
    )


SMEM = pl.BlockSpec(memory_space=pltpu.SMEM)
VMEM = pl.BlockSpec(memory_space=pltpu.VMEM)
ANY = pl.BlockSpec(memory_space=pl.ANY)


def math_scratch(padded, ways):
    return [pltpu.VMEM((2 * padded, TILE), jnp.float32)] * ways + [
        pltpu.VMEM((padded, 2 * TILE), jnp.bfloat16)
    ] * ways


def far_call(plan, wire, first, many, both, kkt, own_acc, dkv, keys, us, length):
    owners, rows, _ = wire.shape
    images, all_heads, padded, _ = own_acc.shape
    more = () if dkv is None else (dkv,)
    back_rows = cdiv(many * length, 8) * 8
    most = (2 * owners * length) // TILE + images + WAYS - 1
    return pl.pallas_call(
        functools.partial(far_kernel, keys, padded, length, many),
        grid=(many,),
        in_specs=[
            SMEM,
            pl.BlockSpec((owners, rows, LANES), lambda h: (0, 0, 0)),
            pl.BlockSpec((images, 1, 2 * padded, LANES), lambda h: (0, first + h, 0, 0)),
            pl.BlockSpec((images, 1, LANES, padded), lambda h: (0, first + h, 0, 0)),
            pl.BlockSpec((images, 1, padded, LANES), lambda h: (0, first + h, 0, 0)),
        ]
        + [ANY] * len(more),
        out_specs=[
            pl.BlockSpec((images, 1, keys, LANES), lambda h: (0, first + h, 0, 0)),
            pl.BlockSpec((owners, back_rows, LANES), lambda h: (0, 0, 0)),
        ],
        out_shape=[
            jax.ShapeDtypeStruct((images, all_heads, keys, LANES), jnp.bfloat16),
            jax.ShapeDtypeStruct((owners, back_rows, LANES), jnp.bfloat16),
        ],
        scratch_shapes=[
            pltpu.VMEM((many, most * TILE + 64, LANES), jnp.float32),
            pltpu.VMEM((images, padded, LANES), jnp.float32),
        ]
        + math_scratch(padded, WAYS),
        input_output_aliases={5: 0} if more else {},
        compiler_params=params(),
        cost_estimate=cost(us),
        name="far" + str(first),
    )(plan, wire, both, kkt, own_acc, *more)


def exchange(x, groups=None):
    return lax.all_to_all(
        x, "dp", split_axis=0, concat_axis=0, axis_index_groups=groups, tiled=True
    )


def per_device(texts, query_weight, patch_key_value, grad_out, negatives):
    owners = lax.axis_size("dp")
    members = lax.axis_size("mp")
    member = lax.axis_index("mp")
    texts_here, length, depth = texts.shape
    images_here, heads, keys, _ = patch_key_value.shape
    width = query_weight.shape[0]
    captions = texts_here // images_here
    padded = cdiv(keys, 16) * 16
    count = texts_here * length
    bf16, f32, i32 = jnp.bfloat16, jnp.float32, jnp.int32
    early = heads - 1
    first_rows = cdiv(2 * early * length + 2, 8) * 8
    later_rows = cdiv(2 * length, 8) * 8

    flat_text = texts.transpose(1, 0, 2).reshape(count, depth)
    neg = negatives.T
    all_weight = lax.all_gather(query_weight, "mp", axis=0, tiled=True)
    start_col = member * width // LANES * LANES
    odd = ((member * width - start_col) // HEAD_SIZE).reshape(1).astype(i32)
    window = lax.dynamic_slice_in_dim(grad_out, start_col, 2 * LANES, 3)

    wire_first, query, rank = pl.pallas_call(
        functools.partial(pack_first_kernel, early, images_here),
        in_specs=[SMEM, SMEM, VMEM, VMEM, ANY],
        out_specs=[ANY, ANY, SMEM],
        out_shape=[
            jax.ShapeDtypeStruct((owners, first_rows, LANES), bf16),
            jax.ShapeDtypeStruct((heads, count, LANES), f32),
            jax.ShapeDtypeStruct(neg.shape, i32),
        ],
        scratch_shapes=[
            pltpu.VMEM((owners * first_rows, LANES), f32),
            pltpu.VMEM(window.shape, bf16),
            pltpu.VMEM((heads, count, LANES), f32),
            pltpu.VMEM((owners, first_rows, LANES), bf16),
            pltpu.SMEM((owners,), i32),
            pltpu.SemaphoreType.DMA((2 + PARTS,)),
        ],
        compiler_params=params(),
        cost_estimate=cost(5),
        name="pack_first",
    )(odd, neg, flat_text, query_weight, window)
    got_first = exchange(wire_first)

    own_acc, own_dq, both, kkt = pl.pallas_call(
        functools.partial(own_kernel, keys, padded, texts_here),
        grid=(images_here, heads),
        in_specs=[
            SMEM,
            pl.BlockSpec((1, count, LANES), lambda i, h: (h, 0, 0)),
            pl.BlockSpec((captions, 1, length, 2 * LANES), lambda i, h: (i, 0, 0, 0)),
            pl.BlockSpec((1, 1, keys, LANES), lambda i, h: (i, h, 0, 0)),
        ],
        out_specs=[
            pl.BlockSpec((1, 1, padded, LANES), lambda i, h: (i, h, 0, 0)),
            pl.BlockSpec((1, 1, TILE, LANES), lambda i, h: (i, h, 0, 0)),
            pl.BlockSpec((1, 1, 2 * padded, LANES), lambda i, h: (i, h, 0, 0)),
            pl.BlockSpec((1, 1, LANES, padded), lambda i, h: (i, h, 0, 0)),
        ],
        out_shape=[
            jax.ShapeDtypeStruct((images_here, heads, padded, LANES), f32),
            jax.ShapeDtypeStruct((images_here, heads, TILE, LANES), f32),
            jax.ShapeDtypeStruct((images_here, heads, 2 * padded, LANES), bf16),
            jax.ShapeDtypeStruct((images_here, heads, LANES, padded), bf16),
        ],
        scratch_shapes=[pltpu.VMEM((TILE, LANES), f32)] + math_scratch(padded, 1),
        compiler_params=params(),
        cost_estimate=cost(13),
        name="own",
    )(odd, query, window, patch_key_value)

    wire_later = pl.pallas_call(
        functools.partial(pack_later_kernel, early, heads - early, images_here),
        in_specs=[SMEM, SMEM, SMEM, VMEM, VMEM, ANY],
        out_specs=VMEM,
        out_shape=jax.ShapeDtypeStruct((owners, later_rows, LANES), bf16),
        scratch_shapes=[pltpu.VMEM((owners * later_rows, LANES), f32)],
        compiler_params=params(),
        cost_estimate=cost(4),
        name="pack_later",
    )(odd, neg, rank, query, window, own_acc)
    got_later = exchange(wire_later)

    tell = 2 * early * length
    plan = pl.pallas_call(
        functools.partial(plan_kernel, length, images_here, tell),
        in_specs=[ANY],
        out_specs=VMEM,
        out_shape=jax.ShapeDtypeStruct((owners + 8, LANES), i32),
        scratch_shapes=[
            pltpu.VMEM((owners, first_rows - tell // 16 * 16, LANES), bf16),
            pltpu.SemaphoreType.DMA,
        ],
        compiler_params=params(),
        cost_estimate=cost(2),
        name="plan",
    )(got_first)

    dkv, back_first = far_call(
        plan, got_first, 0, early, both, kkt, own_acc, None, keys, 22, length
    )
    home_first = exchange(back_first)
    dkv, back_later = far_call(
        plan, got_later, early, heads - early, both, kkt, own_acc, dkv, keys, 12, length
    )
    home_later = exchange(back_later)

    half = depth // 2
    cut = width // 8
    core = lax.rem(lax.axis_index("dp"), 2).reshape(1).astype(i32)
    chips = [list(range(c, owners, 2)) for c in range(2)]
    partner = [(d, d ^ 1) for d in range(owners)]
    dq_first, weight_first = pl.pallas_call(
        functools.partial(gather_two_kernel, length, images_here),
        grid=(1,),
        in_specs=[
            SMEM,
            SMEM,
            VMEM,
            pl.BlockSpec((images_here, early, TILE, LANES), lambda n: (0, 0, 0, 0)),
            VMEM,
        ],
        out_specs=[VMEM, VMEM],
        out_shape=[
            jax.ShapeDtypeStruct((members, count // members, LANES), bf16),
            jax.ShapeDtypeStruct((early * HEAD_SIZE, depth), f32),
        ],
        scratch_shapes=[pltpu.VMEM((early, count, LANES), f32)] * 2,
        compiler_params=params(),
        cost_estimate=cost(4),
        name="gather_two",
    )(neg, rank, flat_text, own_dq, home_first)
    def swap(dq):
        rows = []
        for r in range(members):
            block = lax.dynamic_index_in_dim(dq, lax.rem(member + r, members), 0, False)
            if r:
                block = lax.ppermute(block, "mp", [(i, (i + r) % members) for i in range(members)])
            rows.append(block)
        return rows

    def text_part(rows, skip, wide):
        total = None
        for r in range(members):
            source = lax.rem(member + members - r, members)
            weight = lax.dynamic_slice_in_dim(all_weight, source * width + skip, wide, 0)
            part = jnp.dot(rows[r][:, :wide], weight, preferred_element_type=f32)
            total = part if total is None else total + part
        return total

    rows_first = swap(dq_first)
    dq_later, keep, give = pl.pallas_call(
        functools.partial(gather_last_kernel, length, images_here),
        grid=(1,),
        in_specs=[
            SMEM,
            SMEM,
            SMEM,
            VMEM,
            pl.BlockSpec((images_here, 1, TILE, LANES), lambda n: (0, early, 0, 0)),
            VMEM,
            VMEM,
            ANY,
        ],
        out_specs=[VMEM, VMEM, VMEM],
        out_shape=[
            jax.ShapeDtypeStruct((members, count // members, LANES), bf16),
            jax.ShapeDtypeStruct((cut, 8, half), f32),
            jax.ShapeDtypeStruct((cut, 8, half), bf16),
        ],
        scratch_shapes=[pltpu.VMEM((1, count, LANES), f32)] * 2
        + [pltpu.VMEM((2, cut, 8, half), f32)],
        compiler_params=params(),
        cost_estimate=cost(3),
        name="gather_last",
    )(core, neg, rank, flat_text, own_dq, home_later, weight_first, rows_first[-1])

    got = lax.ppermute(give, "dp", partner)
    summed, dq_later = pl.pallas_call(
        pair_kernel,
        in_specs=[VMEM, VMEM, ANY],
        out_specs=[VMEM, ANY],
        out_shape=[
            jax.ShapeDtypeStruct((owners // 2, 8, half), bf16),
            jax.ShapeDtypeStruct(dq_later.shape, bf16),
        ],
        input_output_aliases={2: 1},
        compiler_params=params(),
        cost_estimate=cost(2),
        name="pair",
    )(keep, got, dq_later)
    parts = exchange(summed, chips)
    piece = pl.pallas_call(
        total_kernel,
        in_specs=[VMEM],
        out_specs=VMEM,
        out_shape=jax.ShapeDtypeStruct(parts.shape, bf16),
        compiler_params=params(),
        cost_estimate=cost(2),
        name="total",
    )(parts)
    pieces = exchange(piece, chips)[:cut]
    weight_grad = pl.pallas_call(
        unfold_kernel,
        in_specs=[SMEM, VMEM, VMEM],
        out_specs=VMEM,
        out_shape=jax.ShapeDtypeStruct((width, depth), f32),
        compiler_params=params(),
        cost_estimate=cost(2),
        name="unfold",
    )(core, pieces, lax.ppermute(pieces, "dp", partner))

    rows_later = swap(dq_later)
    text_grad = text_part(rows_first, 0, early * HEAD_SIZE)
    text_grad = text_grad + text_part(rows_later, early * HEAD_SIZE, (heads - early) * HEAD_SIZE)
    text_grad = text_grad.astype(bf16).reshape(texts_here // members, length, depth)
    return (text_grad, weight_grad, dkv)


def solution(mesh):
    in_specs = (
        P("dp", None, None),
        P("mp", None),
        P("dp", "mp", None, None),
        P("dp", None, None, None),
        P("dp", None),
    )
    out_specs = (P(("dp", "mp"), None, None), P("mp", None), P("dp", "mp", None, None))
    return jax.shard_map(
        per_device, mesh=mesh, in_specs=in_specs, out_specs=out_specs, check_vma=False
    )
```

```python
import functools

import jax
import jax.numpy as jnp
from jax import lax
from jax.experimental import pallas as pl
from jax.experimental.pallas import tpu as pltpu
from jax.sharding import PartitionSpec as P

HEAD_SIZE = 64
NEG = 3
LANES = 128
TILE = 256
WAYS = 4
PARTS = 4

VMEM_LIMIT = 60 * 1024 * 1024


def cdiv(a, b):
    return -(-a // b)


def lower_half(shape):
    return lax.broadcasted_iota(jnp.int32, shape, len(shape) - 1) < HEAD_SIZE


def request_slots(neg_ref, rank_ref, seen_ref, owners, images_here):
    negatives, texts_here = neg_ref.shape

    def clear(o, carry):
        seen_ref[o] = 0
        return carry

    lax.fori_loop(0, owners, clear, 0)

    def count(t, carry):
        for j in range(negatives):
            o = neg_ref[j, t] // images_here
            c = seen_ref[o]
            rank_ref[j, t] = c
            seen_ref[o] = c + 1
        return carry

    lax.fori_loop(0, texts_here, count, 0)


def joined(g, odd, q):
    g = g.astype(jnp.float32)
    g = jnp.where(odd == 1, g, pltpu.roll(g, HEAD_SIZE, 1))
    return jnp.where(lower_half(g.shape), q, g)


def project(text_ref, weight_ref, query_ref):
    q = lax.dot_general(
        text_ref[...], weight_ref[...], (((1,), (1,)), ((), ())), preferred_element_type=jnp.float32
    )
    q = q.astype(jnp.bfloat16).astype(jnp.float32) * HEAD_SIZE**-0.5
    for h in range(query_ref.shape[0]):
        if h % 2:
            a = (h - 1) * HEAD_SIZE
            query_ref[h] = pltpu.roll(q[:, a : a + LANES], HEAD_SIZE, 1)
        elif (h + 2) * HEAD_SIZE <= q.shape[1]:
            query_ref[h] = q[:, h * HEAD_SIZE : (h + 2) * HEAD_SIZE]
        else:
            query_ref[h, :, :HEAD_SIZE] = q[:, h * HEAD_SIZE :]
            query_ref[h, :, HEAD_SIZE:] = jnp.zeros((q.shape[0], HEAD_SIZE), jnp.float32)


def place_rows(
    first, heads, images_here, odd_ref, neg_ref, rank_ref, query_ref, grad_ref, wire_rows, scr
):
    texts_here, slots, length, _ = grad_ref.shape
    tells = wire_rows >= 2 * heads * length + 2
    if tells:
        for o in range(scr.shape[0] // wire_rows):
            scr[(o + 1) * wire_rows - 8 : (o + 1) * wire_rows, :] = jnp.full(
                (8, LANES), -1.0, jnp.float32
            )

    def one_text(t, carry):
        for h in range(heads):
            q = query_ref[first + h, pl.ds(t, length, stride=texts_here), :]
            place = odd_ref[0] + first + h
            col = pl.multiple_of((place // 2) * LANES, LANES)
            for j in range(slots - 1):
                n = neg_ref[j, t]
                r = rank_ref[j, t]
                o = n // images_here
                row = o * wire_rows + (r * heads + h) * length
                g = grad_ref[t, j + 1, :, pl.ds(col, LANES)]
                scr[pl.ds(row, length), :] = joined(g, lax.rem(place, 2), q)
                if h == 0 and tells:
                    tell = o * wire_rows + 2 * heads * length + r
                    image = (n - o * images_here).astype(jnp.float32)
                    scr[pl.ds(tell, 1), :] = jnp.full((1, LANES), image, jnp.float32)
        return carry

    lax.fori_loop(0, texts_here, one_text, 0, unroll=2)


def pack_first_kernel(
    heads,
    images_here,
    odd_ref,
    neg_ref,
    text_ref,
    weight_ref,
    grad_hbm,
    wire_hbm,
    query_hbm,
    rank_ref,
    scr,
    grad_scr,
    query_scr,
    wire_scr,
    seen_ref,
    sems,
):
    load = pltpu.make_async_copy(grad_hbm, grad_scr, sems.at[0])
    load.start()
    request_slots(neg_ref, rank_ref, seen_ref, wire_scr.shape[0], images_here)
    project(text_ref, weight_ref, query_scr)
    keep = pltpu.make_async_copy(query_scr, query_hbm, sems.at[1])
    keep.start()
    load.wait()
    place_rows(
        0, heads, images_here, odd_ref, neg_ref, rank_ref, query_scr, grad_scr, wire_scr.shape[1], scr
    )
    owners, rows, _ = wire_scr.shape
    part = owners // PARTS
    sends = []
    for p in range(PARTS):
        block = scr[p * part * rows : (p + 1) * part * rows, :]
        wire_scr[p * part : (p + 1) * part] = block.reshape(part, rows, LANES).astype(jnp.bfloat16)
        send = pltpu.make_async_copy(
            wire_scr.at[pl.ds(p * part, part)], wire_hbm.at[pl.ds(p * part, part)], sems.at[2 + p]
        )
        send.start()
        sends.append(send)
    keep.wait()
    for send in sends:
        send.wait()


def pack_later_kernel(
    first, heads, images_here, odd_ref, neg_ref, rank_ref, query_ref, grad_ref, after_ref, wire_ref, scr
):
    place_rows(
        first, heads, images_here, odd_ref, neg_ref, rank_ref, query_ref, grad_ref, wire_ref.shape[1], scr
    )
    wire_ref[...] = scr[...].reshape(wire_ref.shape).astype(jnp.bfloat16)


def load_memory(kv, keys, kv_ref, kkt_ref, padded):
    full = jnp.concatenate([kv, jnp.zeros((padded - keys, LANES), jnp.float32)], axis=0)
    low = lower_half(full.shape)
    k_only = jnp.where(low, full, 0.0)
    kv_ref[:padded, :] = k_only.astype(jnp.bfloat16)
    kv_ref[padded:, :] = jnp.where(low, 0.0, full).astype(jnp.bfloat16)
    twice = k_only + pltpu.roll(k_only, HEAD_SIZE, 1)
    kkt_ref[...] = twice.T.astype(jnp.bfloat16)


def tile_scores(qg, kv, s_scr):
    s_scr[...] = lax.dot_general(
        kv, qg, (((1,), (1,)), ((), ())), preferred_element_type=jnp.float32
    )


def tile_softmax(keys, padded, s_scr, pd_scr):
    tile = s_scr.shape[1]
    bounds = list(range(0, padded, 64)) + [padded]
    chunks = list(zip(bounds[:-1], bounds[1:]))
    top = jnp.full((8, tile), -jnp.inf, jnp.float32)
    for a, b in chunks:
        s = s_scr[a:b, :]
        if b > keys:
            row = lax.broadcasted_iota(jnp.int32, s.shape, 0) + a
            s = jnp.where(row < keys, s, -jnp.inf)
            s_scr[a:b, :] = s
        top = jnp.maximum(top, jnp.max(s.reshape((b - a) // 8, 8, tile), axis=0))
    top = jnp.max(top, axis=0, keepdims=True)
    total = jnp.zeros((8, tile), jnp.float32)
    center = jnp.zeros((8, tile), jnp.float32)
    for a, b in chunks:
        e = jnp.exp(s_scr[a:b, :] - top)
        s_scr[a:b, :] = e
        total = total + jnp.sum(e.reshape((b - a) // 8, 8, tile), axis=0)
        d = e * s_scr[padded + a : padded + b, :]
        center = center + jnp.sum(d.reshape((b - a) // 8, 8, tile), axis=0)
    inverse = 1.0 / jnp.sum(total, axis=0, keepdims=True)
    center = jnp.sum(center, axis=0, keepdims=True) * inverse
    for a, b in chunks:
        p = s_scr[a:b, :] * inverse
        pd_scr[a:b, tile:] = p.astype(jnp.bfloat16)
        ds = p * (s_scr[padded + a : padded + b, :] - center)
        pd_scr[a:b, :tile] = ds.astype(jnp.bfloat16)


def tile_outputs(qg, kkt, pd_scr):
    tile = qg.shape[0]
    low = lower_half(qg.shape)
    zero = jnp.zeros_like(qg)
    both = jnp.concatenate([jnp.where(low, qg, zero), jnp.where(low, zero, qg)], axis=0)
    dkv = jnp.dot(pd_scr[...], both, preferred_element_type=jnp.float32)
    dqt = jnp.dot(kkt, pd_scr[:, :tile], preferred_element_type=jnp.float32)
    return dqt.T * (HEAD_SIZE**-0.5), dkv


def own_kernel(
    keys, padded, texts_here, odd_ref, query_ref, grad_ref, kv_ref, acc_ref, dq_ref, both_ref, kkt_ref, own_scr, s_scr, pd_scr
):
    image, h = pl.program_id(0), pl.program_id(1)
    captions, _, length, _ = grad_ref.shape
    load_memory(kv_ref[0, 0].astype(jnp.float32), keys, both_ref.at[0, 0], kkt_ref.at[0, 0], padded)
    place = odd_ref[0] + h
    col = pl.multiple_of((place // 2) * LANES, LANES)
    own_scr[captions * length :, :] = jnp.zeros((TILE - captions * length, LANES), jnp.float32)
    for c in range(captions):
        q = query_ref[0, pl.ds(image * captions + c, length, stride=texts_here), :]
        g = grad_ref[c, 0, :, pl.ds(col, LANES)]
        own_scr[c * length : (c + 1) * length, :] = joined(g, lax.rem(place, 2), q)
    qg = own_scr[...].astype(jnp.bfloat16)
    tile_scores(qg, both_ref[0, 0], s_scr)
    tile_softmax(keys, padded, s_scr, pd_scr)
    dq, dkv = tile_outputs(qg, kkt_ref[0, 0], pd_scr)
    acc_ref[0, 0] = dkv
    dq_ref[0, 0] = dq


def plan_kernel(length, images, tell, wire_hbm, plan_ref, tail_scr, sem):
    senders, rows, _ = tail_scr.shape
    first = tell // 16 * 16
    copy = pltpu.make_async_copy(wire_hbm.at[:, pl.ds(first, rows), :], tail_scr, sem)
    copy.start()
    copy.wait()
    tail = tail_scr[...].astype(jnp.float32)
    id0, id1 = tail[:, tell - first, :], tail[:, tell - first + 1, :]
    lane = lax.broadcasted_iota(jnp.int32, (senders, LANES), 1)
    image = lane.astype(jnp.float32)
    hot0 = jnp.where(id0 == image, 1.0, 0.0)
    hot1 = jnp.where(id1 == image, 1.0, 0.0)
    both = hot0 + hot1
    row = lax.broadcasted_iota(jnp.int32, (senders, senders), 0)
    col = lax.broadcasted_iota(jnp.int32, (senders, senders), 1)
    before = jnp.where(col < row, 1.0, 0.0).astype(jnp.bfloat16)
    ahead = jnp.dot(before, both.astype(jnp.bfloat16), preferred_element_type=jnp.float32)
    number = jnp.sum(both, axis=0, keepdims=True).astype(jnp.int32)
    tiles = (number * length + (TILE - 1)) // TILE
    tiles = jnp.broadcast_to(tiles, (8, LANES))
    row = lax.broadcasted_iota(jnp.int32, (LANES, LANES), 0)
    col = lax.broadcasted_iota(jnp.int32, (LANES, LANES), 1)
    before = jnp.where(row < col, 1.0, 0.0).astype(jnp.bfloat16)
    first_tile = jnp.dot(
        tiles.astype(jnp.float32).astype(jnp.bfloat16), before, preferred_element_type=jnp.float32
    )
    at = first_tile[0:1] * TILE + ahead * length
    pos0 = jnp.sum(hot0 * at, axis=1, keepdims=True)
    pos1 = jnp.sum(hot1 * (at + hot0 * length), axis=1, keepdims=True)
    pos0 = jnp.where(id0 >= 0, pos0, -1.0)
    pos1 = jnp.where(id1 >= 0, pos1, -1.0)
    plan_ref[:senders, :] = jnp.where(lane == 0, pos0, pos1).astype(jnp.int32)
    low = lax.broadcasted_iota(jnp.int32, (8, LANES), 0)
    plan_ref[senders:, :] = jnp.where(low == 0, first_tile.astype(jnp.int32), tiles)


def far_kernel(
    keys,
    padded,
    length,
    heads,
    plan_ref,
    wire_ref,
    both_ref,
    kkt_ref,
    own_ref,
    *rest,
):
    h = pl.program_id(0)
    images = both_ref.shape[0]
    senders = wire_ref.shape[0]
    dkv_ref, back_ref, rows_scr, acc_scr = rest[-4 - 2 * WAYS : -2 * WAYS]
    pairs = rest[-2 * WAYS :]
    ways = WAYS
    s_scrs, pd_scrs = pairs[:ways], pairs[ways:]

    @pl.when(h == 0)
    def _():
        def clear(start):
            for g in range(heads):
                rows_scr[g, pl.ds(pl.multiple_of(start, TILE), TILE), :] = jnp.zeros(
                    (TILE, LANES), jnp.float32
                )

        for i in range(images):
            n = plan_ref[senders + 1, i]

            @pl.when(n > 0)
            def _():
                clear((plan_ref[senders, i] + n - 1) * TILE)

        end = plan_ref[senders, images - 1] + plan_ref[senders + 1, images - 1]
        for w in range(ways - 1):
            clear((end + w) * TILE)

        def place(s, carry):
            block = wire_ref[s].astype(jnp.float32)
            for r in range(2):
                pos = plan_ref[s, r]

                @pl.when(pos >= 0)
                def _():
                    for g in range(heads):
                        a = (r * heads + g) * length
                        rows_scr[g, pl.ds(pos, length), :] = block[a : a + length]

            return carry

        lax.fori_loop(0, senders, place, 0, unroll=4)

    for i in range(images):
        acc_scr[i] = own_ref[i, 0]
    edges = [plan_ref[senders, i] for i in range(1, images)]
    tiles = plan_ref[senders, images - 1] + plan_ref[senders + 1, images - 1]

    def step(k, carry):
        starts, images_of, rows = [], [], []
        for w in range(ways):
            n = k * ways + w
            image = jnp.int32(0)
            for e in edges:
                image = image + (n >= e).astype(jnp.int32)
            start = pl.multiple_of(n * TILE, TILE)
            qg = rows_scr[h, pl.ds(start, TILE), :].astype(jnp.bfloat16)
            starts.append(start)
            images_of.append(image)
            rows.append(qg)
            tile_scores(qg, both_ref[image, 0], s_scrs[w])
        for w in range(ways):
            tile_softmax(keys, padded, s_scrs[w], pd_scrs[w])
            dq, dkv = tile_outputs(rows[w], kkt_ref[images_of[w], 0], pd_scrs[w])
            acc_scr[images_of[w]] += dkv
            rows_scr[h, pl.ds(starts[w], TILE), :] = dq
        return carry

    lax.fori_loop(0, (tiles + ways - 1) // ways, step, 0)
    for i in range(images):
        dkv_ref[i, 0] = acc_scr[i, :keys, :].astype(jnp.bfloat16)

    @pl.when(h == heads - 1)
    def _():
        rows = back_ref.shape[1]
        low = lower_half((length, LANES))
        spare = rows - heads * length

        def give(s, carry):
            p0 = jnp.maximum(plan_ref[s, 0], 0)
            p1 = jnp.maximum(plan_ref[s, 1], 0)
            parts = []
            for g in range(heads):
                x0 = rows_scr[g, pl.ds(p0, length), :]
                x1 = rows_scr[g, pl.ds(p1, length), :]
                parts.append(jnp.where(low, x0, x1))
            if spare:
                parts.append(jnp.zeros((spare, LANES), jnp.float32))
            back_ref[s] = jnp.concatenate(parts, axis=0).astype(jnp.bfloat16)
            return carry

        lax.fori_loop(0, senders, give, 0, unroll=4)


def sum_requests(heads, length, images_here, neg_ref, rank_ref, own_ref, back_ref, sum_scr, text_scr, per):
    texts_here = sum_scr.shape[1] // length
    captions = texts_here // images_here

    def one(t, carry):
        image = t // captions
        totals = [
            own_ref[image, h, pl.ds((t - image * captions) * length, length), :]
            for h in range(heads)
        ]
        for j in range(NEG):
            block = back_ref[neg_ref[j, t] // images_here].astype(jnp.float32)
            block = jnp.where(rank_ref[j, t] == 1, pltpu.roll(block, HEAD_SIZE, 1), block)
            for h in range(heads):
                totals[h] = totals[h] + block[h * length : (h + 1) * length]
        for h in range(heads):
            sum_scr[h, pl.ds(t, length, stride=texts_here), :] = totals[h]
            at = t // per * (per * length) + lax.rem(t, per)
            text_scr[h, pl.ds(at, length, stride=per), :] = totals[h]
        return carry

    lax.fori_loop(0, texts_here, one, 0, unroll=2)


def gather_two_kernel(
    length, images_here, neg_ref, rank_ref, text_ref, own_ref, back_ref, dq_ref, weight_ref, sum_scr, text_scr
):
    per = dq_ref.shape[1] // length
    sum_requests(
        2, length, images_here, neg_ref, rank_ref, own_ref, back_ref, sum_scr, text_scr, per
    )
    members, mine, _ = dq_ref.shape

    def paired(x0, x1):
        x = jnp.where(lower_half(x0.shape), x0, pltpu.roll(x1, HEAD_SIZE, 1))
        return x.astype(jnp.bfloat16)

    for m in range(members):
        at = slice(m * mine, (m + 1) * mine)
        dq_ref[m] = paired(text_scr[0, at, :], text_scr[1, at, :])
    dq = paired(sum_scr[0], sum_scr[1])
    weight_ref[...] = lax.dot_general(
        dq, text_ref[...], (((0,), (0,)), ((), ())), preferred_element_type=jnp.float32
    )


def gather_last_kernel(
    length,
    images_here,
    core_ref,
    neg_ref,
    rank_ref,
    text_ref,
    own_ref,
    back_ref,
    head_ref,
    after_ref,
    dq_ref,
    keep_ref,
    give_ref,
    sum_scr,
    text_scr,
    cut_scr,
):
    per = dq_ref.shape[1] // length
    sum_requests(
        1, length, images_here, neg_ref, rank_ref, own_ref, back_ref, sum_scr, text_scr, per
    )
    members, mine, _ = dq_ref.shape
    for m in range(members):
        dq_ref[m] = text_scr[0, m * mine : (m + 1) * mine, :].astype(jnp.bfloat16)
    dq = sum_scr[0].astype(jnp.bfloat16)
    last = lax.dot_general(
        dq, text_ref[...], (((0,), (0,)), ((), ())), preferred_element_type=jnp.float32
    )
    half = cut_scr.shape[3]
    before = head_ref.shape[0] // 8
    blocks = before + HEAD_SIZE // 8
    for b in range(blocks):
        rows = head_ref[b * 8 : b * 8 + 8, :] if b < before else last[(b - before) * 8 : (b - before) * 8 + 8]
        for side in range(2):
            cut_scr[2 * b // blocks, 2 * b % blocks + side] = rows[:, side * half : (side + 1) * half]
    core = core_ref[0]
    keep_ref[...] = cut_scr[core]
    give_ref[...] = cut_scr[1 - core].astype(jnp.bfloat16)


def pair_kernel(keep_ref, got_ref, *rest):
    out_ref = rest[len(rest) // 2]
    pieces = keep_ref.shape[0]
    out_ref[:pieces] = (keep_ref[...] + got_ref[...].astype(jnp.float32)).astype(jnp.bfloat16)


def total_kernel(parts_ref, out_ref):
    total = parts_ref[0].astype(jnp.float32)
    for d in range(1, parts_ref.shape[0]):
        total = total + parts_ref[d].astype(jnp.float32)
    total = total.astype(jnp.bfloat16)
    for d in range(out_ref.shape[0]):
        out_ref[d] = total


def unfold_kernel(core_ref, mine_ref, other_ref, out_ref):
    half = mine_ref.shape[2]
    rows = out_ref.shape[0] // 2
    for which, ref in ((core_ref[0], mine_ref), (1 - core_ref[0], other_ref)):
        for b in range(rows // 8):
            at = pl.ds(pl.multiple_of(which * rows + b * 8, 8), 8)
            for side in range(2):
                out_ref[at, side * half : (side + 1) * half] = ref[2 * b + side].astype(jnp.float32)


def text_kernel(width, wides, member_ref, weight_ref, *refs):
    rows, out_ref = refs[:-1], refs[-1]
    members = len(rows) // len(wides)
    total = jnp.zeros(out_ref.shape, jnp.float32)
    for r in range(members):
        source = lax.rem(member_ref[0] + members - r, members)
        skip = 0
        for group, wide in enumerate(wides):
            at = pl.ds(pl.multiple_of(source * width + skip, HEAD_SIZE), wide)
            total = total + jnp.dot(
                rows[group * members + r][:, :wide],
                weight_ref[at, :],
                preferred_element_type=jnp.float32,
            )
            skip += wide
    out_ref[...] = total.astype(jnp.bfloat16)


def params():
    return pltpu.CompilerParams(vmem_limit_bytes=VMEM_LIMIT)


def cost(us):
    return pl.CostEstimate(
        flops=int(us * 1e6 * 1150 / 2), bytes_accessed=int(us * 1e-6 * 3.6e12), transcendentals=0
    )


SMEM = pl.BlockSpec(memory_space=pltpu.SMEM)
VMEM = pl.BlockSpec(memory_space=pltpu.VMEM)
ANY = pl.BlockSpec(memory_space=pl.ANY)


def math_scratch(padded, ways):
    return [pltpu.VMEM((2 * padded, TILE), jnp.float32)] * ways + [
        pltpu.VMEM((padded, 2 * TILE), jnp.bfloat16)
    ] * ways


def far_call(plan, wire, first, many, both, kkt, own_acc, dkv, keys, us, length):
    owners, rows, _ = wire.shape
    images, all_heads, padded, _ = own_acc.shape
    more = () if dkv is None else (dkv,)
    back_rows = cdiv(many * length, 8) * 8
    most = (2 * owners * length) // TILE + images + WAYS - 1
    return pl.pallas_call(
        functools.partial(far_kernel, keys, padded, length, many),
        grid=(many,),
        in_specs=[
            SMEM,
            pl.BlockSpec((owners, rows, LANES), lambda h: (0, 0, 0)),
            pl.BlockSpec((images, 1, 2 * padded, LANES), lambda h: (0, first + h, 0, 0)),
            pl.BlockSpec((images, 1, LANES, padded), lambda h: (0, first + h, 0, 0)),
            pl.BlockSpec((images, 1, padded, LANES), lambda h: (0, first + h, 0, 0)),
        ]
        + [ANY] * len(more),
        out_specs=[
            pl.BlockSpec((images, 1, keys, LANES), lambda h: (0, first + h, 0, 0)),
            pl.BlockSpec((owners, back_rows, LANES), lambda h: (0, 0, 0)),
        ],
        out_shape=[
            jax.ShapeDtypeStruct((images, all_heads, keys, LANES), jnp.bfloat16),
            jax.ShapeDtypeStruct((owners, back_rows, LANES), jnp.bfloat16),
        ],
        scratch_shapes=[
            pltpu.VMEM((many, most * TILE + 64, LANES), jnp.float32),
            pltpu.VMEM((images, padded, LANES), jnp.float32),
        ]
        + math_scratch(padded, WAYS),
        input_output_aliases={5: 0} if more else {},
        compiler_params=params(),
        cost_estimate=cost(us),
        name="far" + str(first),
    )(plan, wire, both, kkt, own_acc, *more)


def exchange(x, groups=None):
    return lax.all_to_all(
        x, "dp", split_axis=0, concat_axis=0, axis_index_groups=groups, tiled=True
    )


def per_device(texts, query_weight, patch_key_value, grad_out, negatives):
    owners = lax.axis_size("dp")
    members = lax.axis_size("mp")
    member = lax.axis_index("mp")
    texts_here, length, depth = texts.shape
    images_here, heads, keys, _ = patch_key_value.shape
    width = query_weight.shape[0]
    captions = texts_here // images_here
    padded = cdiv(keys, 16) * 16
    count = texts_here * length
    bf16, f32, i32 = jnp.bfloat16, jnp.float32, jnp.int32
    early = heads - 1
    first_rows = cdiv(2 * early * length + 2, 8) * 8
    later_rows = cdiv(2 * length, 8) * 8

    flat_text = texts.transpose(1, 0, 2).reshape(count, depth)
    neg = negatives.T
    all_weight = lax.all_gather(query_weight, "mp", axis=0, tiled=True)
    start_col = member * width // LANES * LANES
    odd = ((member * width - start_col) // HEAD_SIZE).reshape(1).astype(i32)
    window = lax.dynamic_slice_in_dim(grad_out, start_col, 2 * LANES, 3)

    wire_first, query, rank = pl.pallas_call(
        functools.partial(pack_first_kernel, early, images_here),
        in_specs=[SMEM, SMEM, VMEM, VMEM, ANY],
        out_specs=[ANY, ANY, SMEM],
        out_shape=[
            jax.ShapeDtypeStruct((owners, first_rows, LANES), bf16),
            jax.ShapeDtypeStruct((heads, count, LANES), f32),
            jax.ShapeDtypeStruct(neg.shape, i32),
        ],
        scratch_shapes=[
            pltpu.VMEM((owners * first_rows, LANES), f32),
            pltpu.VMEM(window.shape, bf16),
            pltpu.VMEM((heads, count, LANES), f32),
            pltpu.VMEM((owners, first_rows, LANES), bf16),
            pltpu.SMEM((owners,), i32),
            pltpu.SemaphoreType.DMA((2 + PARTS,)),
        ],
        compiler_params=params(),
        cost_estimate=cost(5),
        name="pack_first",
    )(odd, neg, flat_text, query_weight, window)
    got_first = exchange(wire_first)

    own_acc, own_dq, both, kkt = pl.pallas_call(
        functools.partial(own_kernel, keys, padded, texts_here),
        grid=(images_here, heads),
        in_specs=[
            SMEM,
            pl.BlockSpec((1, count, LANES), lambda i, h: (h, 0, 0)),
            pl.BlockSpec((captions, 1, length, 2 * LANES), lambda i, h: (i, 0, 0, 0)),
            pl.BlockSpec((1, 1, keys, LANES), lambda i, h: (i, h, 0, 0)),
        ],
        out_specs=[
            pl.BlockSpec((1, 1, padded, LANES), lambda i, h: (i, h, 0, 0)),
            pl.BlockSpec((1, 1, TILE, LANES), lambda i, h: (i, h, 0, 0)),
            pl.BlockSpec((1, 1, 2 * padded, LANES), lambda i, h: (i, h, 0, 0)),
            pl.BlockSpec((1, 1, LANES, padded), lambda i, h: (i, h, 0, 0)),
        ],
        out_shape=[
            jax.ShapeDtypeStruct((images_here, heads, padded, LANES), f32),
            jax.ShapeDtypeStruct((images_here, heads, TILE, LANES), f32),
            jax.ShapeDtypeStruct((images_here, heads, 2 * padded, LANES), bf16),
            jax.ShapeDtypeStruct((images_here, heads, LANES, padded), bf16),
        ],
        scratch_shapes=[pltpu.VMEM((TILE, LANES), f32)] + math_scratch(padded, 1),
        compiler_params=params(),
        cost_estimate=cost(13),
        name="own",
    )(odd, query, window, patch_key_value)

    wire_later = pl.pallas_call(
        functools.partial(pack_later_kernel, early, heads - early, images_here),
        in_specs=[SMEM, SMEM, SMEM, VMEM, VMEM, ANY],
        out_specs=VMEM,
        out_shape=jax.ShapeDtypeStruct((owners, later_rows, LANES), bf16),
        scratch_shapes=[pltpu.VMEM((owners * later_rows, LANES), f32)],
        compiler_params=params(),
        cost_estimate=cost(4),
        name="pack_later",
    )(odd, neg, rank, query, window, own_acc)
    got_later = exchange(wire_later)

    tell = 2 * early * length
    plan = pl.pallas_call(
        functools.partial(plan_kernel, length, images_here, tell),
        in_specs=[ANY],
        out_specs=VMEM,
        out_shape=jax.ShapeDtypeStruct((owners + 8, LANES), i32),
        scratch_shapes=[
            pltpu.VMEM((owners, first_rows - tell // 16 * 16, LANES), bf16),
            pltpu.SemaphoreType.DMA,
        ],
        compiler_params=params(),
        cost_estimate=cost(2),
        name="plan",
    )(got_first)

    dkv, back_first = far_call(
        plan, got_first, 0, early, both, kkt, own_acc, None, keys, 22, length
    )
    home_first = exchange(back_first)
    dkv, back_later = far_call(
        plan, got_later, early, heads - early, both, kkt, own_acc, dkv, keys, 12, length
    )
    home_later = exchange(back_later)

    half = depth // 2
    cut = width // 8
    core = lax.rem(lax.axis_index("dp"), 2).reshape(1).astype(i32)
    chips = [list(range(c, owners, 2)) for c in range(2)]
    partner = [(d, d ^ 1) for d in range(owners)]
    dq_first, weight_first = pl.pallas_call(
        functools.partial(gather_two_kernel, length, images_here),
        grid=(1,),
        in_specs=[
            SMEM,
            SMEM,
            VMEM,
            pl.BlockSpec((images_here, early, TILE, LANES), lambda n: (0, 0, 0, 0)),
            VMEM,
        ],
        out_specs=[VMEM, VMEM],
        out_shape=[
            jax.ShapeDtypeStruct((members, count // members, LANES), bf16),
            jax.ShapeDtypeStruct((early * HEAD_SIZE, depth), f32),
        ],
        scratch_shapes=[pltpu.VMEM((early, count, LANES), f32)] * 2,
        compiler_params=params(),
        cost_estimate=cost(4),
        name="gather_two",
    )(neg, rank, flat_text, own_dq, home_first)
    def swap(dq):
        rows = []
        for r in range(members):
            block = lax.dynamic_index_in_dim(dq, lax.rem(member + r, members), 0, False)
            if r:
                block = lax.ppermute(block, "mp", [(i, (i + r) % members) for i in range(members)])
            rows.append(block)
        return rows

    rows_first = swap(dq_first)
    dq_later, keep, give = pl.pallas_call(
        functools.partial(gather_last_kernel, length, images_here),
        grid=(1,),
        in_specs=[
            SMEM,
            SMEM,
            SMEM,
            VMEM,
            pl.BlockSpec((images_here, 1, TILE, LANES), lambda n: (0, early, 0, 0)),
            VMEM,
            VMEM,
            ANY,
        ],
        out_specs=[VMEM, VMEM, VMEM],
        out_shape=[
            jax.ShapeDtypeStruct((members, count // members, LANES), bf16),
            jax.ShapeDtypeStruct((cut, 8, half), f32),
            jax.ShapeDtypeStruct((cut, 8, half), bf16),
        ],
        scratch_shapes=[pltpu.VMEM((1, count, LANES), f32)] * 2
        + [pltpu.VMEM((2, cut, 8, half), f32)],
        compiler_params=params(),
        cost_estimate=cost(3),
        name="gather_last",
    )(core, neg, rank, flat_text, own_dq, home_later, weight_first, rows_first[-1])

    got = lax.ppermute(give, "dp", partner)
    later = [dq_later]
    summed, dq_later = pl.pallas_call(
        pair_kernel,
        in_specs=[VMEM, VMEM] + [ANY] * len(later),
        out_specs=[VMEM] + [ANY] * len(later),
        out_shape=[jax.ShapeDtypeStruct((owners // 2, 8, half), bf16)]
        + [jax.ShapeDtypeStruct(x.shape, x.dtype) for x in later],
        input_output_aliases={2 + n: 1 + n for n in range(len(later))},
        compiler_params=params(),
        cost_estimate=cost(2),
        name="pair",
    )(keep, got, *later)
    parts = exchange(summed, chips)
    piece = pl.pallas_call(
        total_kernel,
        in_specs=[VMEM],
        out_specs=VMEM,
        out_shape=jax.ShapeDtypeStruct(parts.shape, bf16),
        compiler_params=params(),
        cost_estimate=cost(2),
        name="total",
    )(parts)
    rows_later = swap(dq_later)
    mine = texts_here // members
    text_grad = pl.pallas_call(
        functools.partial(text_kernel, width, (early * HEAD_SIZE, (heads - early) * HEAD_SIZE)),
        in_specs=[SMEM] + [VMEM] * (1 + 2 * members),
        out_specs=VMEM,
        out_shape=jax.ShapeDtypeStruct((length * mine, depth), bf16),
        compiler_params=params(),
        cost_estimate=cost(3),
        name="text",
    )(member.reshape(1).astype(i32), all_weight, *rows_first, *rows_later)
    pieces, text_grad = pl.pallas_call(
        lambda *refs: None,
        in_specs=[ANY, ANY],
        out_specs=[ANY, ANY],
        out_shape=[
            jax.ShapeDtypeStruct(piece.shape, bf16),
            jax.ShapeDtypeStruct(text_grad.shape, bf16),
        ],
        input_output_aliases={0: 0, 1: 1},
        cost_estimate=cost(1),
        name="order",
    )(exchange(piece, chips), text_grad)
    text_grad = text_grad.reshape(length, mine, depth).transpose(1, 0, 2)
    weight_grad = pl.pallas_call(
        unfold_kernel,
        in_specs=[SMEM, VMEM, VMEM],
        out_specs=VMEM,
        out_shape=jax.ShapeDtypeStruct((width, depth), f32),
        compiler_params=params(),
        cost_estimate=cost(2),
        name="unfold",
    )(core, pieces, lax.ppermute(pieces, "dp", partner))

    return (text_grad, weight_grad, dkv)


def solution(mesh):
    in_specs = (
        P("dp", None, None),
        P("mp", None),
        P("dp", "mp", None, None),
        P("dp", None, None, None),
        P("dp", None),
    )
    out_specs = (P(("dp", "mp"), None, None), P("mp", None), P("dp", "mp", None, None))
    return jax.shard_map(
        per_device, mesh=mesh, in_specs=in_specs, out_specs=out_specs, check_vma=False
    )
```

```python
import functools

import jax
import jax.numpy as jnp
from jax import lax
from jax.experimental import pallas as pl
from jax.experimental.pallas import tpu as pltpu
from jax.sharding import PartitionSpec as P

HEAD_SIZE = 64
NEG = 3
LANES = 128
TILE = 256
WAYS = 4
PARTS = 4

VMEM_LIMIT = 60 * 1024 * 1024


def cdiv(a, b):
    return -(-a // b)


def lower_half(shape):
    return lax.broadcasted_iota(jnp.int32, shape, len(shape) - 1) < HEAD_SIZE


def request_slots(neg_ref, rank_ref, seen_ref, owners, images_here):
    negatives, texts_here = neg_ref.shape

    def clear(o, carry):
        seen_ref[o] = 0
        return carry

    lax.fori_loop(0, owners, clear, 0)

    def count(t, carry):
        for j in range(negatives):
            o = neg_ref[j, t] // images_here
            c = seen_ref[o]
            rank_ref[j, t] = c
            seen_ref[o] = c + 1
        return carry

    lax.fori_loop(0, texts_here, count, 0)


def joined(g, odd, q):
    g = g.astype(jnp.float32)
    g = jnp.where(odd == 1, g, pltpu.roll(g, HEAD_SIZE, 1))
    return jnp.where(lower_half(g.shape), q, g)


def project(text_ref, weight_ref, query_ref):
    q = lax.dot_general(
        text_ref[...], weight_ref[...], (((1,), (1,)), ((), ())), preferred_element_type=jnp.float32
    )
    q = q.astype(jnp.bfloat16).astype(jnp.float32) * HEAD_SIZE**-0.5
    for h in range(query_ref.shape[0]):
        if h % 2:
            a = (h - 1) * HEAD_SIZE
            query_ref[h] = pltpu.roll(q[:, a : a + LANES], HEAD_SIZE, 1)
        elif (h + 2) * HEAD_SIZE <= q.shape[1]:
            query_ref[h] = q[:, h * HEAD_SIZE : (h + 2) * HEAD_SIZE]
        else:
            query_ref[h, :, :HEAD_SIZE] = q[:, h * HEAD_SIZE :]
            query_ref[h, :, HEAD_SIZE:] = jnp.zeros((q.shape[0], HEAD_SIZE), jnp.float32)


def place_rows(
    first, heads, images_here, odd_ref, neg_ref, rank_ref, query_ref, grad_ref, wire_rows, scr
):
    texts_here, slots, length, _ = grad_ref.shape
    tells = wire_rows >= 2 * heads * length + 2
    if tells:
        for o in range(scr.shape[0] // wire_rows):
            scr[(o + 1) * wire_rows - 8 : (o + 1) * wire_rows, :] = jnp.full(
                (8, LANES), -1.0, jnp.float32
            )

    def one_text(t, carry):
        for h in range(heads):
            q = query_ref[first + h, pl.ds(t, length, stride=texts_here), :]
            place = odd_ref[0] + first + h
            col = pl.multiple_of((place // 2) * LANES, LANES)
            for j in range(slots - 1):
                n = neg_ref[j, t]
                r = rank_ref[j, t]
                o = n // images_here
                row = o * wire_rows + (r * heads + h) * length
                g = grad_ref[t, j + 1, :, pl.ds(col, LANES)]
                scr[pl.ds(row, length), :] = joined(g, lax.rem(place, 2), q)
                if h == 0 and tells:
                    tell = o * wire_rows + 2 * heads * length + r
                    image = (n - o * images_here).astype(jnp.float32)
                    scr[pl.ds(tell, 1), :] = jnp.full((1, LANES), image, jnp.float32)
        return carry

    lax.fori_loop(0, texts_here, one_text, 0, unroll=2)


def pack_first_kernel(
    heads,
    images_here,
    odd_ref,
    neg_ref,
    text_ref,
    weight_ref,
    grad_hbm,
    wire_hbm,
    query_hbm,
    rank_ref,
    scr,
    grad_scr,
    query_scr,
    wire_scr,
    seen_ref,
    sems,
):
    load = pltpu.make_async_copy(grad_hbm, grad_scr, sems.at[0])
    load.start()
    request_slots(neg_ref, rank_ref, seen_ref, wire_scr.shape[0], images_here)
    project(text_ref, weight_ref, query_scr)
    keep = pltpu.make_async_copy(query_scr, query_hbm, sems.at[1])
    keep.start()
    load.wait()
    place_rows(
        0, heads, images_here, odd_ref, neg_ref, rank_ref, query_scr, grad_scr, wire_scr.shape[1], scr
    )
    owners, rows, _ = wire_scr.shape
    part = owners // PARTS
    sends = []
    for p in range(PARTS):
        block = scr[p * part * rows : (p + 1) * part * rows, :]
        wire_scr[p * part : (p + 1) * part] = block.reshape(part, rows, LANES).astype(jnp.bfloat16)
        send = pltpu.make_async_copy(
            wire_scr.at[pl.ds(p * part, part)], wire_hbm.at[pl.ds(p * part, part)], sems.at[2 + p]
        )
        send.start()
        sends.append(send)
    keep.wait()
    for send in sends:
        send.wait()


def pack_later_kernel(
    first, heads, images_here, odd_ref, neg_ref, rank_ref, query_ref, grad_ref, after_ref, wire_ref, scr
):
    place_rows(
        first, heads, images_here, odd_ref, neg_ref, rank_ref, query_ref, grad_ref, wire_ref.shape[1], scr
    )
    wire_ref[...] = scr[...].reshape(wire_ref.shape).astype(jnp.bfloat16)


def load_memory(kv, keys, kv_ref, kkt_ref, padded):
    full = jnp.concatenate([kv, jnp.zeros((padded - keys, LANES), jnp.float32)], axis=0)
    low = lower_half(full.shape)
    k_only = jnp.where(low, full, 0.0)
    kv_ref[:padded, :] = k_only.astype(jnp.bfloat16)
    kv_ref[padded:, :] = jnp.where(low, 0.0, full).astype(jnp.bfloat16)
    twice = k_only + pltpu.roll(k_only, HEAD_SIZE, 1)
    kkt_ref[...] = twice.T.astype(jnp.bfloat16)


def tile_scores(qg, kv, s_scr):
    s_scr[...] = lax.dot_general(
        kv, qg, (((1,), (1,)), ((), ())), preferred_element_type=jnp.float32
    )


def tile_softmax(keys, padded, s_scr, pd_scr):
    tile = s_scr.shape[1]
    bounds = list(range(0, padded, 64)) + [padded]
    chunks = list(zip(bounds[:-1], bounds[1:]))
    top = jnp.full((8, tile), -jnp.inf, jnp.float32)
    for a, b in chunks:
        s = s_scr[a:b, :]
        if b > keys:
            row = lax.broadcasted_iota(jnp.int32, s.shape, 0) + a
            s = jnp.where(row < keys, s, -jnp.inf)
            s_scr[a:b, :] = s
        top = jnp.maximum(top, jnp.max(s.reshape((b - a) // 8, 8, tile), axis=0))
    top = jnp.max(top, axis=0, keepdims=True)
    total = jnp.zeros((8, tile), jnp.float32)
    center = jnp.zeros((8, tile), jnp.float32)
    for a, b in chunks:
        e = jnp.exp(s_scr[a:b, :] - top)
        s_scr[a:b, :] = e
        total = total + jnp.sum(e.reshape((b - a) // 8, 8, tile), axis=0)
        d = e * s_scr[padded + a : padded + b, :]
        center = center + jnp.sum(d.reshape((b - a) // 8, 8, tile), axis=0)
    inverse = 1.0 / jnp.sum(total, axis=0, keepdims=True)
    center = jnp.sum(center, axis=0, keepdims=True) * inverse
    for a, b in chunks:
        p = s_scr[a:b, :] * inverse
        pd_scr[a:b, tile:] = p.astype(jnp.bfloat16)
        ds = p * (s_scr[padded + a : padded + b, :] - center)
        pd_scr[a:b, :tile] = ds.astype(jnp.bfloat16)


def tile_outputs(qg, kkt, pd_scr):
    tile = qg.shape[0]
    low = lower_half(qg.shape)
    zero = jnp.zeros_like(qg)
    both = jnp.concatenate([jnp.where(low, qg, zero), jnp.where(low, zero, qg)], axis=0)
    dkv = jnp.dot(pd_scr[...], both, preferred_element_type=jnp.float32)
    dqt = jnp.dot(kkt, pd_scr[:, :tile], preferred_element_type=jnp.float32)
    return dqt.T * (HEAD_SIZE**-0.5), dkv


def own_kernel(
    keys, padded, texts_here, odd_ref, query_ref, grad_ref, kv_ref, acc_ref, dq_ref, both_ref, kkt_ref, own_scr, s_scr, pd_scr
):
    image, h = pl.program_id(0), pl.program_id(1)
    captions, _, length, _ = grad_ref.shape
    load_memory(kv_ref[0, 0].astype(jnp.float32), keys, both_ref.at[0, 0], kkt_ref.at[0, 0], padded)
    place = odd_ref[0] + h
    col = pl.multiple_of((place // 2) * LANES, LANES)
    own_scr[captions * length :, :] = jnp.zeros((TILE - captions * length, LANES), jnp.float32)
    for c in range(captions):
        q = query_ref[0, pl.ds(image * captions + c, length, stride=texts_here), :]
        g = grad_ref[c, 0, :, pl.ds(col, LANES)]
        own_scr[c * length : (c + 1) * length, :] = joined(g, lax.rem(place, 2), q)
    qg = own_scr[...].astype(jnp.bfloat16)
    tile_scores(qg, both_ref[0, 0], s_scr)
    tile_softmax(keys, padded, s_scr, pd_scr)
    dq, dkv = tile_outputs(qg, kkt_ref[0, 0], pd_scr)
    acc_ref[0, 0] = dkv
    dq_ref[0, 0] = dq


def plan_kernel(length, images, tell, wire_hbm, plan_ref, tail_scr, sem):
    senders, rows, _ = tail_scr.shape
    first = tell // 16 * 16
    copy = pltpu.make_async_copy(wire_hbm.at[:, pl.ds(first, rows), :], tail_scr, sem)
    copy.start()
    copy.wait()
    tail = tail_scr[...].astype(jnp.float32)
    id0, id1 = tail[:, tell - first, :], tail[:, tell - first + 1, :]
    lane = lax.broadcasted_iota(jnp.int32, (senders, LANES), 1)
    image = lane.astype(jnp.float32)
    hot0 = jnp.where(id0 == image, 1.0, 0.0)
    hot1 = jnp.where(id1 == image, 1.0, 0.0)
    both = hot0 + hot1
    row = lax.broadcasted_iota(jnp.int32, (senders, senders), 0)
    col = lax.broadcasted_iota(jnp.int32, (senders, senders), 1)
    before = jnp.where(col < row, 1.0, 0.0).astype(jnp.bfloat16)
    ahead = jnp.dot(before, both.astype(jnp.bfloat16), preferred_element_type=jnp.float32)
    number = jnp.sum(both, axis=0, keepdims=True).astype(jnp.int32)
    tiles = (number * length + (TILE - 1)) // TILE
    tiles = jnp.broadcast_to(tiles, (8, LANES))
    row = lax.broadcasted_iota(jnp.int32, (LANES, LANES), 0)
    col = lax.broadcasted_iota(jnp.int32, (LANES, LANES), 1)
    before = jnp.where(row < col, 1.0, 0.0).astype(jnp.bfloat16)
    first_tile = jnp.dot(
        tiles.astype(jnp.float32).astype(jnp.bfloat16), before, preferred_element_type=jnp.float32
    )
    at = first_tile[0:1] * TILE + ahead * length
    pos0 = jnp.sum(hot0 * at, axis=1, keepdims=True)
    pos1 = jnp.sum(hot1 * (at + hot0 * length), axis=1, keepdims=True)
    pos0 = jnp.where(id0 >= 0, pos0, -1.0)
    pos1 = jnp.where(id1 >= 0, pos1, -1.0)
    plan_ref[:senders, :] = jnp.where(lane == 0, pos0, pos1).astype(jnp.int32)
    low = lax.broadcasted_iota(jnp.int32, (8, LANES), 0)
    plan_ref[senders:, :] = jnp.where(low == 0, first_tile.astype(jnp.int32), tiles)


def far_kernel(
    keys,
    padded,
    length,
    heads,
    plan_ref,
    wire_ref,
    both_ref,
    kkt_ref,
    own_ref,
    *rest,
):
    h = pl.program_id(0)
    images = both_ref.shape[0]
    senders = wire_ref.shape[0]
    dkv_ref, back_ref, rows_scr, acc_scr = rest[-4 - 2 * WAYS : -2 * WAYS]
    pairs = rest[-2 * WAYS :]
    ways = WAYS
    s_scrs, pd_scrs = pairs[:ways], pairs[ways:]

    @pl.when(h == 0)
    def _():
        def clear(start):
            for g in range(heads):
                rows_scr[g, pl.ds(pl.multiple_of(start, TILE), TILE), :] = jnp.zeros(
                    (TILE, LANES), jnp.float32
                )

        for i in range(images):
            n = plan_ref[senders + 1, i]

            @pl.when(n > 0)
            def _():
                clear((plan_ref[senders, i] + n - 1) * TILE)

        end = plan_ref[senders, images - 1] + plan_ref[senders + 1, images - 1]
        for w in range(ways - 1):
            clear((end + w) * TILE)

        def place(s, carry):
            block = wire_ref[s].astype(jnp.float32)
            for r in range(2):
                pos = plan_ref[s, r]

                @pl.when(pos >= 0)
                def _():
                    for g in range(heads):
                        a = (r * heads + g) * length
                        rows_scr[g, pl.ds(pos, length), :] = block[a : a + length]

            return carry

        lax.fori_loop(0, senders, place, 0, unroll=4)

    for i in range(images):
        acc_scr[i] = own_ref[i, 0]
    edges = [plan_ref[senders, i] for i in range(1, images)]
    tiles = plan_ref[senders, images - 1] + plan_ref[senders + 1, images - 1]

    def step(k, carry):
        starts, images_of, rows = [], [], []
        for w in range(ways):
            n = k * ways + w
            image = jnp.int32(0)
            for e in edges:
                image = image + (n >= e).astype(jnp.int32)
            start = pl.multiple_of(n * TILE, TILE)
            qg = rows_scr[h, pl.ds(start, TILE), :].astype(jnp.bfloat16)
            starts.append(start)
            images_of.append(image)
            rows.append(qg)
            tile_scores(qg, both_ref[image, 0], s_scrs[w])
        for w in range(ways):
            tile_softmax(keys, padded, s_scrs[w], pd_scrs[w])
            dq, dkv = tile_outputs(rows[w], kkt_ref[images_of[w], 0], pd_scrs[w])
            acc_scr[images_of[w]] += dkv
            rows_scr[h, pl.ds(starts[w], TILE), :] = dq
        return carry

    lax.fori_loop(0, (tiles + ways - 1) // ways, step, 0)
    for i in range(images):
        dkv_ref[i, 0] = acc_scr[i, :keys, :].astype(jnp.bfloat16)

    @pl.when(h == heads - 1)
    def _():
        rows = back_ref.shape[1]
        low = lower_half((length, LANES))
        spare = rows - heads * length

        def give(s, carry):
            p0 = jnp.maximum(plan_ref[s, 0], 0)
            p1 = jnp.maximum(plan_ref[s, 1], 0)
            parts = []
            for g in range(heads):
                x0 = rows_scr[g, pl.ds(p0, length), :]
                x1 = rows_scr[g, pl.ds(p1, length), :]
                parts.append(jnp.where(low, x0, x1))
            if spare:
                parts.append(jnp.zeros((spare, LANES), jnp.float32))
            back_ref[s] = jnp.concatenate(parts, axis=0).astype(jnp.bfloat16)
            return carry

        lax.fori_loop(0, senders, give, 0, unroll=4)


def sum_requests(heads, length, images_here, neg_ref, rank_ref, own_ref, back_ref, sum_scr, text_scr, per):
    texts_here = sum_scr.shape[1] // length
    captions = texts_here // images_here

    def one(t, carry):
        image = t // captions
        totals = [
            own_ref[image, h, pl.ds((t - image * captions) * length, length), :]
            for h in range(heads)
        ]
        for j in range(NEG):
            block = back_ref[neg_ref[j, t] // images_here].astype(jnp.float32)
            block = jnp.where(rank_ref[j, t] == 1, pltpu.roll(block, HEAD_SIZE, 1), block)
            for h in range(heads):
                totals[h] = totals[h] + block[h * length : (h + 1) * length]
        for h in range(heads):
            sum_scr[h, pl.ds(t, length, stride=texts_here), :] = totals[h]
            at = t // per * (per * length) + lax.rem(t, per)
            text_scr[h, pl.ds(at, length, stride=per), :] = totals[h]
        return carry

    lax.fori_loop(0, texts_here, one, 0, unroll=2)


def gather_two_kernel(
    length, images_here, neg_ref, rank_ref, text_ref, own_ref, back_ref, dq_ref, weight_ref, sum_scr, text_scr
):
    per = dq_ref.shape[1] // length
    sum_requests(
        2, length, images_here, neg_ref, rank_ref, own_ref, back_ref, sum_scr, text_scr, per
    )
    members, mine, _ = dq_ref.shape

    def paired(x0, x1):
        x = jnp.where(lower_half(x0.shape), x0, pltpu.roll(x1, HEAD_SIZE, 1))
        return x.astype(jnp.bfloat16)

    for m in range(members):
        at = slice(m * mine, (m + 1) * mine)
        dq_ref[m] = paired(text_scr[0, at, :], text_scr[1, at, :])
    dq = paired(sum_scr[0], sum_scr[1])
    weight_ref[...] = lax.dot_general(
        dq, text_ref[...], (((0,), (0,)), ((), ())), preferred_element_type=jnp.float32
    )


def gather_last_kernel(
    length,
    images_here,
    core_ref,
    neg_ref,
    rank_ref,
    text_ref,
    own_ref,
    back_ref,
    head_ref,
    *rest,
):
    dq_ref, keep_ref, give_ref, _, sum_scr, text_scr, cut_scr = rest[-7:]
    per = dq_ref.shape[1] // length
    sum_requests(
        1, length, images_here, neg_ref, rank_ref, own_ref, back_ref, sum_scr, text_scr, per
    )
    members, mine, _ = dq_ref.shape
    for m in range(members):
        dq_ref[m] = text_scr[0, m * mine : (m + 1) * mine, :].astype(jnp.bfloat16)
    dq = sum_scr[0].astype(jnp.bfloat16)
    last = lax.dot_general(
        dq, text_ref[...], (((0,), (0,)), ((), ())), preferred_element_type=jnp.float32
    )
    half = cut_scr.shape[3]
    before = head_ref.shape[0] // 8
    blocks = before + HEAD_SIZE // 8
    for b in range(blocks):
        rows = head_ref[b * 8 : b * 8 + 8, :] if b < before else last[(b - before) * 8 : (b - before) * 8 + 8]
        for side in range(2):
            cut_scr[2 * b // blocks, 2 * b % blocks + side] = rows[:, side * half : (side + 1) * half]
    core = core_ref[0]
    keep_ref[...] = cut_scr[core]
    give_ref[...] = cut_scr[1 - core].astype(jnp.bfloat16)


def pair_kernel(keep_ref, got_ref, *rest):
    out_ref = rest[len(rest) // 2]
    pieces = keep_ref.shape[0]
    out_ref[:pieces] = (keep_ref[...] + got_ref[...].astype(jnp.float32)).astype(jnp.bfloat16)


def total_kernel(parts_ref, *rest):
    out_ref = rest[-1]
    total = parts_ref[0].astype(jnp.float32)
    for d in range(1, parts_ref.shape[0]):
        total = total + parts_ref[d].astype(jnp.float32)
    total = total.astype(jnp.bfloat16)
    for d in range(out_ref.shape[0]):
        out_ref[d] = total


def unfold_kernel(core_ref, mine_ref, other_ref, out_ref):
    half = mine_ref.shape[2]
    rows = out_ref.shape[0] // 2
    for which, ref in ((core_ref[0], mine_ref), (1 - core_ref[0], other_ref)):
        for b in range(rows // 8):
            at = pl.ds(pl.multiple_of(which * rows + b * 8, 8), 8)
            for side in range(2):
                out_ref[at, side * half : (side + 1) * half] = ref[2 * b + side].astype(jnp.float32)


def text_kernel(width, wides, member_ref, weight_ref, *refs):
    rows, out_ref = refs[:-1], refs[-1]
    members = len(rows) // len(wides)
    total = jnp.zeros(out_ref.shape, jnp.float32)
    for r in range(members):
        source = lax.rem(member_ref[0] + members - r, members)
        skip = 0
        for group, wide in enumerate(wides):
            at = pl.ds(pl.multiple_of(source * width + skip, HEAD_SIZE), wide)
            total = total + jnp.dot(
                rows[group * members + r][:, :wide],
                weight_ref[at, :],
                preferred_element_type=jnp.float32,
            )
            skip += wide
    out_ref[...] = total.astype(jnp.bfloat16)


def params():
    return pltpu.CompilerParams(vmem_limit_bytes=VMEM_LIMIT)


def cost(us):
    return pl.CostEstimate(
        flops=int(us * 1e6 * 1150 / 2), bytes_accessed=int(us * 1e-6 * 3.6e12), transcendentals=0
    )


SMEM = pl.BlockSpec(memory_space=pltpu.SMEM)
VMEM = pl.BlockSpec(memory_space=pltpu.VMEM)
ANY = pl.BlockSpec(memory_space=pl.ANY)


def math_scratch(padded, ways):
    return [pltpu.VMEM((2 * padded, TILE), jnp.float32)] * ways + [
        pltpu.VMEM((padded, 2 * TILE), jnp.bfloat16)
    ] * ways


def far_call(plan, wire, first, many, both, kkt, own_acc, dkv, keys, us, length):
    owners, rows, _ = wire.shape
    images, all_heads, padded, _ = own_acc.shape
    more = () if dkv is None else (dkv,)
    back_rows = cdiv(many * length, 8) * 8
    most = (2 * owners * length) // TILE + images + WAYS - 1
    return pl.pallas_call(
        functools.partial(far_kernel, keys, padded, length, many),
        grid=(many,),
        in_specs=[
            SMEM,
            pl.BlockSpec((owners, rows, LANES), lambda h: (0, 0, 0)),
            pl.BlockSpec((images, 1, 2 * padded, LANES), lambda h: (0, first + h, 0, 0)),
            pl.BlockSpec((images, 1, LANES, padded), lambda h: (0, first + h, 0, 0)),
            pl.BlockSpec((images, 1, padded, LANES), lambda h: (0, first + h, 0, 0)),
        ]
        + [ANY] * len(more),
        out_specs=[
            pl.BlockSpec((images, 1, keys, LANES), lambda h: (0, first + h, 0, 0)),
            pl.BlockSpec((owners, back_rows, LANES), lambda h: (0, 0, 0)),
        ],
        out_shape=[
            jax.ShapeDtypeStruct((images, all_heads, keys, LANES), jnp.bfloat16),
            jax.ShapeDtypeStruct((owners, back_rows, LANES), jnp.bfloat16),
        ],
        scratch_shapes=[
            pltpu.VMEM((many, most * TILE + 64, LANES), jnp.float32),
            pltpu.VMEM((images, padded, LANES), jnp.float32),
        ]
        + math_scratch(padded, WAYS),
        input_output_aliases={5: 0} if more else {},
        compiler_params=params(),
        cost_estimate=cost(us),
        name="far" + str(first),
    )(plan, wire, both, kkt, own_acc, *more)


def exchange(x, groups=None):
    return lax.all_to_all(
        x, "dp", split_axis=0, concat_axis=0, axis_index_groups=groups, tiled=True
    )


def per_device(texts, query_weight, patch_key_value, grad_out, negatives):
    owners = lax.axis_size("dp")
    members = lax.axis_size("mp")
    member = lax.axis_index("mp")
    texts_here, length, depth = texts.shape
    images_here, heads, keys, _ = patch_key_value.shape
    width = query_weight.shape[0]
    captions = texts_here // images_here
    padded = cdiv(keys, 16) * 16
    count = texts_here * length
    bf16, f32, i32 = jnp.bfloat16, jnp.float32, jnp.int32
    early = heads - 1
    first_rows = cdiv(2 * early * length + 2, 8) * 8
    later_rows = cdiv(2 * length, 8) * 8

    flat_text = texts.transpose(1, 0, 2).reshape(count, depth)
    neg = negatives.T
    all_weight = lax.all_gather(query_weight, "mp", axis=0, tiled=True)
    start_col = member * width // LANES * LANES
    odd = ((member * width - start_col) // HEAD_SIZE).reshape(1).astype(i32)
    window = lax.dynamic_slice_in_dim(grad_out, start_col, 2 * LANES, 3)

    wire_first, query, rank = pl.pallas_call(
        functools.partial(pack_first_kernel, early, images_here),
        in_specs=[SMEM, SMEM, VMEM, VMEM, ANY],
        out_specs=[ANY, ANY, SMEM],
        out_shape=[
            jax.ShapeDtypeStruct((owners, first_rows, LANES), bf16),
            jax.ShapeDtypeStruct((heads, count, LANES), f32),
            jax.ShapeDtypeStruct(neg.shape, i32),
        ],
        scratch_shapes=[
            pltpu.VMEM((owners * first_rows, LANES), f32),
            pltpu.VMEM(window.shape, bf16),
            pltpu.VMEM((heads, count, LANES), f32),
            pltpu.VMEM((owners, first_rows, LANES), bf16),
            pltpu.SMEM((owners,), i32),
            pltpu.SemaphoreType.DMA((2 + PARTS,)),
        ],
        compiler_params=params(),
        cost_estimate=cost(5),
        name="pack_first",
    )(odd, neg, flat_text, query_weight, window)
    got_first = exchange(wire_first)

    own_acc, own_dq, both, kkt = pl.pallas_call(
        functools.partial(own_kernel, keys, padded, texts_here),
        grid=(images_here, heads),
        in_specs=[
            SMEM,
            pl.BlockSpec((1, count, LANES), lambda i, h: (h, 0, 0)),
            pl.BlockSpec((captions, 1, length, 2 * LANES), lambda i, h: (i, 0, 0, 0)),
            pl.BlockSpec((1, 1, keys, LANES), lambda i, h: (i, h, 0, 0)),
        ],
        out_specs=[
            pl.BlockSpec((1, 1, padded, LANES), lambda i, h: (i, h, 0, 0)),
            pl.BlockSpec((1, 1, TILE, LANES), lambda i, h: (i, h, 0, 0)),
            pl.BlockSpec((1, 1, 2 * padded, LANES), lambda i, h: (i, h, 0, 0)),
            pl.BlockSpec((1, 1, LANES, padded), lambda i, h: (i, h, 0, 0)),
        ],
        out_shape=[
            jax.ShapeDtypeStruct((images_here, heads, padded, LANES), f32),
            jax.ShapeDtypeStruct((images_here, heads, TILE, LANES), f32),
            jax.ShapeDtypeStruct((images_here, heads, 2 * padded, LANES), bf16),
            jax.ShapeDtypeStruct((images_here, heads, LANES, padded), bf16),
        ],
        scratch_shapes=[pltpu.VMEM((TILE, LANES), f32)] + math_scratch(padded, 1),
        compiler_params=params(),
        cost_estimate=cost(13),
        name="own",
    )(odd, query, window, patch_key_value)

    wire_later = pl.pallas_call(
        functools.partial(pack_later_kernel, early, heads - early, images_here),
        in_specs=[SMEM, SMEM, SMEM, VMEM, VMEM, ANY],
        out_specs=VMEM,
        out_shape=jax.ShapeDtypeStruct((owners, later_rows, LANES), bf16),
        scratch_shapes=[pltpu.VMEM((owners * later_rows, LANES), f32)],
        compiler_params=params(),
        cost_estimate=cost(4),
        name="pack_later",
    )(odd, neg, rank, query, window, own_acc)
    got_later = exchange(wire_later)

    tell = 2 * early * length
    plan = pl.pallas_call(
        functools.partial(plan_kernel, length, images_here, tell),
        in_specs=[ANY],
        out_specs=VMEM,
        out_shape=jax.ShapeDtypeStruct((owners + 8, LANES), i32),
        scratch_shapes=[
            pltpu.VMEM((owners, first_rows - tell // 16 * 16, LANES), bf16),
            pltpu.SemaphoreType.DMA,
        ],
        compiler_params=params(),
        cost_estimate=cost(2),
        name="plan",
    )(got_first)

    dkv, back_first = far_call(
        plan, got_first, 0, early, both, kkt, own_acc, None, keys, 22, length
    )
    home_first = exchange(back_first)
    dkv, back_later = far_call(
        plan, got_later, early, heads - early, both, kkt, own_acc, dkv, keys, 12, length
    )
    home_later = exchange(back_later)

    half = depth // 2
    cut = width // 8
    core = lax.rem(lax.axis_index("dp"), 2).reshape(1).astype(i32)
    chips = [list(range(c, owners, 2)) for c in range(2)]
    partner = [(d, d ^ 1) for d in range(owners)]
    dq_first, weight_first = pl.pallas_call(
        functools.partial(gather_two_kernel, length, images_here),
        grid=(1,),
        in_specs=[
            SMEM,
            SMEM,
            VMEM,
            pl.BlockSpec((images_here, early, TILE, LANES), lambda n: (0, 0, 0, 0)),
            VMEM,
        ],
        out_specs=[VMEM, VMEM],
        out_shape=[
            jax.ShapeDtypeStruct((members, count // members, LANES), bf16),
            jax.ShapeDtypeStruct((early * HEAD_SIZE, depth), f32),
        ],
        scratch_shapes=[pltpu.VMEM((early, count, LANES), f32)] * 2,
        compiler_params=params(),
        cost_estimate=cost(4),
        name="gather_two",
    )(neg, rank, flat_text, own_dq, home_first)
    def swap(dq):
        rows = []
        for r in range(members):
            block = lax.dynamic_index_in_dim(dq, lax.rem(member + r, members), 0, False)
            if r:
                block = lax.ppermute(block, "mp", [(i, (i + r) % members) for i in range(members)])
            rows.append(block)
        return rows

    rows_first = swap(dq_first)
    dkv = dkv.transpose(1, 2, 0, 3)
    dq_later, keep, give, dkv = pl.pallas_call(
        functools.partial(gather_last_kernel, length, images_here),
        grid=(1,),
        in_specs=[
            SMEM,
            SMEM,
            SMEM,
            VMEM,
            pl.BlockSpec((images_here, 1, TILE, LANES), lambda n: (0, early, 0, 0)),
            VMEM,
            VMEM,
        ]
        + [ANY] * members,
        out_specs=[VMEM, VMEM, VMEM, ANY],
        out_shape=[
            jax.ShapeDtypeStruct((members, count // members, LANES), bf16),
            jax.ShapeDtypeStruct((cut, 8, half), f32),
            jax.ShapeDtypeStruct((cut, 8, half), bf16),
            jax.ShapeDtypeStruct(dkv.shape, bf16),
        ],
        input_output_aliases={6 + members: 3},
        scratch_shapes=[pltpu.VMEM((1, count, LANES), f32)] * 2
        + [pltpu.VMEM((2, cut, 8, half), f32)],
        compiler_params=params(),
        cost_estimate=cost(3),
        name="gather_last",
    )(core, neg, rank, flat_text, own_dq, home_later, weight_first, *rows_first[1:], dkv)
    dkv = dkv.transpose(2, 0, 1, 3)

    got = lax.ppermute(give, "dp", partner)
    later = [dq_later]
    summed, dq_later = pl.pallas_call(
        pair_kernel,
        in_specs=[VMEM, VMEM] + [ANY] * len(later),
        out_specs=[VMEM] + [ANY] * len(later),
        out_shape=[jax.ShapeDtypeStruct((owners // 2, 8, half), bf16)]
        + [jax.ShapeDtypeStruct(x.shape, x.dtype) for x in later],
        input_output_aliases={2 + n: 1 + n for n in range(len(later))},
        compiler_params=params(),
        cost_estimate=cost(2),
        name="pair",
    )(keep, got, *later)
    parts = exchange(summed, chips)
    rows_later = swap(dq_later)
    piece = pl.pallas_call(
        total_kernel,
        in_specs=[VMEM] + [ANY] * (members - 1),
        out_specs=VMEM,
        out_shape=jax.ShapeDtypeStruct(parts.shape, bf16),
        compiler_params=params(),
        cost_estimate=cost(2),
        name="total",
    )(parts, *rows_later[1:])
    mine = texts_here // members
    text_grad = pl.pallas_call(
        functools.partial(text_kernel, width, (early * HEAD_SIZE, (heads - early) * HEAD_SIZE)),
        in_specs=[SMEM] + [VMEM] * (1 + 2 * members),
        out_specs=VMEM,
        out_shape=jax.ShapeDtypeStruct((length * mine, depth), bf16),
        compiler_params=params(),
        cost_estimate=cost(3),
        name="text",
    )(member.reshape(1).astype(i32), all_weight, *rows_first, *rows_later)
    text_grad = text_grad.reshape(length, mine, depth)
    pieces, text_grad = pl.pallas_call(
        lambda *refs: None,
        in_specs=[ANY, ANY],
        out_specs=[ANY, ANY],
        out_shape=[
            jax.ShapeDtypeStruct(piece.shape, bf16),
            jax.ShapeDtypeStruct(text_grad.shape, bf16),
        ],
        input_output_aliases={0: 0, 1: 1},
        cost_estimate=cost(1),
        name="order",
    )(exchange(piece, chips), text_grad)
    text_grad = text_grad.transpose(1, 0, 2)
    weight_grad = pl.pallas_call(
        unfold_kernel,
        in_specs=[SMEM, VMEM, VMEM],
        out_specs=VMEM,
        out_shape=jax.ShapeDtypeStruct((width, depth), f32),
        compiler_params=params(),
        cost_estimate=cost(2),
        name="unfold",
    )(core, pieces, lax.ppermute(pieces, "dp", partner))

    return (text_grad, weight_grad, dkv)


def solution(mesh):
    in_specs = (
        P("dp", None, None),
        P("mp", None),
        P("dp", "mp", None, None),
        P("dp", None, None, None),
        P("dp", None),
    )
    out_specs = (P(("dp", "mp"), None, None), P("mp", None), P("dp", "mp", None, None))
    return jax.shard_map(
        per_device, mesh=mesh, in_specs=in_specs, out_specs=out_specs, check_vma=False
    )
```

```python
import functools

import jax
import jax.numpy as jnp
from jax import lax
from jax.experimental import pallas as pl
from jax.experimental.pallas import tpu as pltpu
from jax.sharding import PartitionSpec as P

HEAD_SIZE = 64
NEG = 3
LANES = 128
TILE = 256
WAYS = 4
PARTS = 4

VMEM_LIMIT = 60 * 1024 * 1024
SMALL_LIMIT = 16 * 1024 * 1024


def cdiv(a, b):
    return -(-a // b)


def lower_half(shape):
    return lax.broadcasted_iota(jnp.int32, shape, len(shape) - 1) < HEAD_SIZE


def request_slots(neg_ref, rank_ref, seen_ref, owners, images_here):
    negatives, texts_here = neg_ref.shape

    def clear(o, carry):
        seen_ref[o] = 0
        return carry

    lax.fori_loop(0, owners, clear, 0)

    def count(t, carry):
        for j in range(negatives):
            o = neg_ref[j, t] // images_here
            c = seen_ref[o]
            rank_ref[j, t] = c
            seen_ref[o] = c + 1
        return carry

    lax.fori_loop(0, texts_here, count, 0)


def joined(g, odd, q):
    g = g.astype(jnp.float32)
    g = jnp.where(odd == 1, g, pltpu.roll(g, HEAD_SIZE, 1))
    return jnp.where(lower_half(g.shape), q, g)


def project(text_ref, weight_ref, query_ref):
    q = lax.dot_general(
        text_ref[...], weight_ref[...], (((1,), (1,)), ((), ())), preferred_element_type=jnp.float32
    )
    q = q.astype(jnp.bfloat16).astype(jnp.float32) * HEAD_SIZE**-0.5
    for h in range(query_ref.shape[0]):
        if h % 2:
            a = (h - 1) * HEAD_SIZE
            query_ref[h] = pltpu.roll(q[:, a : a + LANES], HEAD_SIZE, 1)
        elif (h + 2) * HEAD_SIZE <= q.shape[1]:
            query_ref[h] = q[:, h * HEAD_SIZE : (h + 2) * HEAD_SIZE]
        else:
            query_ref[h, :, :HEAD_SIZE] = q[:, h * HEAD_SIZE :]
            query_ref[h, :, HEAD_SIZE:] = jnp.zeros((q.shape[0], HEAD_SIZE), jnp.float32)


def place_rows(
    first, heads, images_here, odd_ref, neg_ref, rank_ref, query_ref, grad_ref, wire_rows, scr
):
    texts_here, slots, length, _ = grad_ref.shape
    tells = wire_rows >= 2 * heads * length + 2
    if tells:
        for o in range(scr.shape[0] // wire_rows):
            scr[(o + 1) * wire_rows - 8 : (o + 1) * wire_rows, :] = jnp.full(
                (8, LANES), -1.0, jnp.float32
            )

    def one_text(t, carry):
        for h in range(heads):
            q = query_ref[first + h, pl.ds(t, length, stride=texts_here), :]
            place = odd_ref[0] + first + h
            col = pl.multiple_of((place // 2) * LANES, LANES)
            for j in range(slots - 1):
                n = neg_ref[j, t]
                r = rank_ref[j, t]
                o = n // images_here
                row = o * wire_rows + (r * heads + h) * length
                g = grad_ref[t, j + 1, :, pl.ds(col, LANES)]
                scr[pl.ds(row, length), :] = joined(g, lax.rem(place, 2), q)
                if h == 0 and tells:
                    tell = o * wire_rows + 2 * heads * length + r
                    image = (n - o * images_here).astype(jnp.float32)
                    scr[pl.ds(tell, 1), :] = jnp.full((1, LANES), image, jnp.float32)
        return carry

    lax.fori_loop(0, texts_here, one_text, 0, unroll=2)


def pack_first_kernel(
    heads,
    images_here,
    odd_ref,
    neg_ref,
    text_ref,
    weight_ref,
    grad_hbm,
    wire_hbm,
    query_hbm,
    rank_ref,
    scr,
    grad_scr,
    query_scr,
    wire_scr,
    seen_ref,
    sems,
):
    load = pltpu.make_async_copy(grad_hbm, grad_scr, sems.at[0])
    load.start()
    request_slots(neg_ref, rank_ref, seen_ref, wire_scr.shape[0], images_here)
    project(text_ref, weight_ref, query_scr)
    keep = pltpu.make_async_copy(query_scr, query_hbm, sems.at[1])
    keep.start()
    load.wait()
    place_rows(
        0, heads, images_here, odd_ref, neg_ref, rank_ref, query_scr, grad_scr, wire_scr.shape[1], scr
    )
    owners, rows, _ = wire_scr.shape
    part = owners // PARTS
    sends = []
    for p in range(PARTS):
        block = scr[p * part * rows : (p + 1) * part * rows, :]
        wire_scr[p * part : (p + 1) * part] = block.reshape(part, rows, LANES).astype(jnp.bfloat16)
        send = pltpu.make_async_copy(
            wire_scr.at[pl.ds(p * part, part)], wire_hbm.at[pl.ds(p * part, part)], sems.at[2 + p]
        )
        send.start()
        sends.append(send)
    keep.wait()
    for send in sends:
        send.wait()


def pack_later_kernel(
    first, heads, images_here, odd_ref, neg_ref, rank_ref, query_ref, grad_ref, after_ref, wire_ref, scr
):
    place_rows(
        first, heads, images_here, odd_ref, neg_ref, rank_ref, query_ref, grad_ref, wire_ref.shape[1], scr
    )
    wire_ref[...] = scr[...].reshape(wire_ref.shape).astype(jnp.bfloat16)


def load_memory(kv, keys, kv_ref, kkt_ref, padded):
    full = jnp.concatenate([kv, jnp.zeros((padded - keys, LANES), jnp.float32)], axis=0)
    low = lower_half(full.shape)
    k_only = jnp.where(low, full, 0.0)
    kv_ref[:padded, :] = k_only.astype(jnp.bfloat16)
    kv_ref[padded:, :] = jnp.where(low, 0.0, full).astype(jnp.bfloat16)
    twice = k_only + pltpu.roll(k_only, HEAD_SIZE, 1)
    kkt_ref[...] = twice.T.astype(jnp.bfloat16)


def tile_scores(qg, kv, s_scr):
    s_scr[...] = lax.dot_general(
        kv, qg, (((1,), (1,)), ((), ())), preferred_element_type=jnp.float32
    )


def tile_softmax(keys, padded, s_scr, pd_scr):
    tile = s_scr.shape[1]
    bounds = list(range(0, padded, 64)) + [padded]
    chunks = list(zip(bounds[:-1], bounds[1:]))
    top = jnp.full((8, tile), -jnp.inf, jnp.float32)
    for a, b in chunks:
        s = s_scr[a:b, :]
        if b > keys:
            row = lax.broadcasted_iota(jnp.int32, s.shape, 0) + a
            s = jnp.where(row < keys, s, -jnp.inf)
            s_scr[a:b, :] = s
        top = jnp.maximum(top, jnp.max(s.reshape((b - a) // 8, 8, tile), axis=0))
    top = jnp.max(top, axis=0, keepdims=True)
    total = jnp.zeros((8, tile), jnp.float32)
    center = jnp.zeros((8, tile), jnp.float32)
    for a, b in chunks:
        e = jnp.exp(s_scr[a:b, :] - top)
        s_scr[a:b, :] = e
        total = total + jnp.sum(e.reshape((b - a) // 8, 8, tile), axis=0)
        d = e * s_scr[padded + a : padded + b, :]
        center = center + jnp.sum(d.reshape((b - a) // 8, 8, tile), axis=0)
    inverse = 1.0 / jnp.sum(total, axis=0, keepdims=True)
    center = jnp.sum(center, axis=0, keepdims=True) * inverse
    for a, b in chunks:
        p = s_scr[a:b, :] * inverse
        pd_scr[a:b, tile:] = p.astype(jnp.bfloat16)
        ds = p * (s_scr[padded + a : padded + b, :] - center)
        pd_scr[a:b, :tile] = ds.astype(jnp.bfloat16)


def tile_outputs(qg, kkt, pd_scr):
    tile = qg.shape[0]
    low = lower_half(qg.shape)
    zero = jnp.zeros_like(qg)
    both = jnp.concatenate([jnp.where(low, qg, zero), jnp.where(low, zero, qg)], axis=0)
    dkv = jnp.dot(pd_scr[...], both, preferred_element_type=jnp.float32)
    dqt = jnp.dot(kkt, pd_scr[:, :tile], preferred_element_type=jnp.float32)
    return dqt.T * (HEAD_SIZE**-0.5), dkv


def own_kernel(
    keys, padded, texts_here, odd_ref, query_ref, grad_ref, kv_ref, acc_ref, dq_ref, both_ref, kkt_ref, own_scr, s_scr, pd_scr
):
    image, h = pl.program_id(0), pl.program_id(1)
    captions, _, length, _ = grad_ref.shape
    load_memory(kv_ref[0, 0].astype(jnp.float32), keys, both_ref.at[0, 0], kkt_ref.at[0, 0], padded)
    place = odd_ref[0] + h
    col = pl.multiple_of((place // 2) * LANES, LANES)
    own_scr[captions * length :, :] = jnp.zeros((TILE - captions * length, LANES), jnp.float32)
    for c in range(captions):
        q = query_ref[0, pl.ds(image * captions + c, length, stride=texts_here), :]
        g = grad_ref[c, 0, :, pl.ds(col, LANES)]
        own_scr[c * length : (c + 1) * length, :] = joined(g, lax.rem(place, 2), q)
    qg = own_scr[...].astype(jnp.bfloat16)
    tile_scores(qg, both_ref[0, 0], s_scr)
    tile_softmax(keys, padded, s_scr, pd_scr)
    dq, dkv = tile_outputs(qg, kkt_ref[0, 0], pd_scr)
    acc_ref[0, 0] = dkv
    dq_ref[0, 0] = dq


def plan_kernel(length, images, tell, wire_hbm, plan_ref, tail_scr, sem):
    senders, rows, _ = tail_scr.shape
    first = tell // 16 * 16
    copy = pltpu.make_async_copy(wire_hbm.at[:, pl.ds(first, rows), :], tail_scr, sem)
    copy.start()
    copy.wait()
    tail = tail_scr[...].astype(jnp.float32)
    id0, id1 = tail[:, tell - first, :], tail[:, tell - first + 1, :]
    lane = lax.broadcasted_iota(jnp.int32, (senders, LANES), 1)
    image = lane.astype(jnp.float32)
    hot0 = jnp.where(id0 == image, 1.0, 0.0)
    hot1 = jnp.where(id1 == image, 1.0, 0.0)
    both = hot0 + hot1
    row = lax.broadcasted_iota(jnp.int32, (senders, senders), 0)
    col = lax.broadcasted_iota(jnp.int32, (senders, senders), 1)
    before = jnp.where(col < row, 1.0, 0.0).astype(jnp.bfloat16)
    ahead = jnp.dot(before, both.astype(jnp.bfloat16), preferred_element_type=jnp.float32)
    number = jnp.sum(both, axis=0, keepdims=True).astype(jnp.int32)
    tiles = (number * length + (TILE - 1)) // TILE
    tiles = jnp.broadcast_to(tiles, (8, LANES))
    row = lax.broadcasted_iota(jnp.int32, (LANES, LANES), 0)
    col = lax.broadcasted_iota(jnp.int32, (LANES, LANES), 1)
    before = jnp.where(row < col, 1.0, 0.0).astype(jnp.bfloat16)
    first_tile = jnp.dot(
        tiles.astype(jnp.float32).astype(jnp.bfloat16), before, preferred_element_type=jnp.float32
    )
    at = first_tile[0:1] * TILE + ahead * length
    pos0 = jnp.sum(hot0 * at, axis=1, keepdims=True)
    pos1 = jnp.sum(hot1 * (at + hot0 * length), axis=1, keepdims=True)
    pos0 = jnp.where(id0 >= 0, pos0, -1.0)
    pos1 = jnp.where(id1 >= 0, pos1, -1.0)
    plan_ref[:senders, :] = jnp.where(lane == 0, pos0, pos1).astype(jnp.int32)
    low = lax.broadcasted_iota(jnp.int32, (8, LANES), 0)
    plan_ref[senders:, :] = jnp.where(low == 0, first_tile.astype(jnp.int32), tiles)


def far_kernel(
    keys,
    padded,
    length,
    heads,
    plan_ref,
    wire_ref,
    both_ref,
    kkt_ref,
    own_ref,
    *rest,
):
    h = pl.program_id(0)
    images = both_ref.shape[0]
    senders = wire_ref.shape[0]
    dkv_ref, back_ref, rows_scr, acc_scr = rest[-4 - 2 * WAYS : -2 * WAYS]
    pairs = rest[-2 * WAYS :]
    ways = WAYS
    s_scrs, pd_scrs = pairs[:ways], pairs[ways:]

    @pl.when(h == 0)
    def _():
        def clear(start):
            for g in range(heads):
                rows_scr[g, pl.ds(pl.multiple_of(start, TILE), TILE), :] = jnp.zeros(
                    (TILE, LANES), jnp.float32
                )

        for i in range(images):
            n = plan_ref[senders + 1, i]

            @pl.when(n > 0)
            def _():
                clear((plan_ref[senders, i] + n - 1) * TILE)

        end = plan_ref[senders, images - 1] + plan_ref[senders + 1, images - 1]
        for w in range(ways - 1):
            clear((end + w) * TILE)

        def place(s, carry):
            block = wire_ref[s].astype(jnp.float32)
            for r in range(2):
                pos = plan_ref[s, r]

                @pl.when(pos >= 0)
                def _():
                    for g in range(heads):
                        a = (r * heads + g) * length
                        rows_scr[g, pl.ds(pos, length), :] = block[a : a + length]

            return carry

        lax.fori_loop(0, senders, place, 0, unroll=4)

    for i in range(images):
        acc_scr[i] = own_ref[i, 0]
    edges = [plan_ref[senders, i] for i in range(1, images)]
    tiles = plan_ref[senders, images - 1] + plan_ref[senders + 1, images - 1]

    def step(k, carry):
        starts, images_of, rows = [], [], []
        for w in range(ways):
            n = k * ways + w
            image = jnp.int32(0)
            for e in edges:
                image = image + (n >= e).astype(jnp.int32)
            start = pl.multiple_of(n * TILE, TILE)
            qg = rows_scr[h, pl.ds(start, TILE), :].astype(jnp.bfloat16)
            starts.append(start)
            images_of.append(image)
            rows.append(qg)
            tile_scores(qg, both_ref[image, 0], s_scrs[w])
        for w in range(ways):
            tile_softmax(keys, padded, s_scrs[w], pd_scrs[w])
            dq, dkv = tile_outputs(rows[w], kkt_ref[images_of[w], 0], pd_scrs[w])
            acc_scr[images_of[w]] += dkv
            rows_scr[h, pl.ds(starts[w], TILE), :] = dq
        return carry

    lax.fori_loop(0, (tiles + ways - 1) // ways, step, 0)
    for i in range(images):
        dkv_ref[i, 0] = acc_scr[i, :keys, :].astype(jnp.bfloat16)

    @pl.when(h == heads - 1)
    def _():
        rows = back_ref.shape[1]
        low = lower_half((length, LANES))
        spare = rows - heads * length

        def give(s, carry):
            p0 = jnp.maximum(plan_ref[s, 0], 0)
            p1 = jnp.maximum(plan_ref[s, 1], 0)
            parts = []
            for g in range(heads):
                x0 = rows_scr[g, pl.ds(p0, length), :]
                x1 = rows_scr[g, pl.ds(p1, length), :]
                parts.append(jnp.where(low, x0, x1))
            if spare:
                parts.append(jnp.zeros((spare, LANES), jnp.float32))
            back_ref[s] = jnp.concatenate(parts, axis=0).astype(jnp.bfloat16)
            return carry

        lax.fori_loop(0, senders, give, 0, unroll=4)


def sum_requests(heads, length, images_here, neg_ref, rank_ref, own_ref, back_ref, sum_scr, text_scr, per):
    texts_here = sum_scr.shape[1] // length
    captions = texts_here // images_here

    def one(t, carry):
        image = t // captions
        totals = [
            own_ref[image, h, pl.ds((t - image * captions) * length, length), :]
            for h in range(heads)
        ]
        for j in range(NEG):
            block = back_ref[neg_ref[j, t] // images_here].astype(jnp.float32)
            block = jnp.where(rank_ref[j, t] == 1, pltpu.roll(block, HEAD_SIZE, 1), block)
            for h in range(heads):
                totals[h] = totals[h] + block[h * length : (h + 1) * length]
        for h in range(heads):
            sum_scr[h, pl.ds(t, length, stride=texts_here), :] = totals[h]
            at = t // per * (per * length) + lax.rem(t, per)
            text_scr[h, pl.ds(at, length, stride=per), :] = totals[h]
        return carry

    lax.fori_loop(0, texts_here, one, 0, unroll=2)


def by_distance(member, members, mine, r):
    return pl.ds(lax.rem(member + r, members) * mine, mine)


def paired(x0, x1):
    x = jnp.where(lower_half(x0.shape), x0, pltpu.roll(x1, HEAD_SIZE, 1))
    return x.astype(jnp.bfloat16)


def gather_two_kernel(
    length, images_here, member_ref, neg_ref, rank_ref, text_ref, own_ref, back_ref, *rest
):
    dq_refs, (weight_ref, sum_scr, text_scr) = rest[:-3], rest[-3:]
    mine = dq_refs[0].shape[0]
    sum_requests(
        2, length, images_here, neg_ref, rank_ref, own_ref, back_ref, sum_scr, text_scr, mine // length
    )
    for r, dq_ref in enumerate(dq_refs):
        at = by_distance(member_ref[0], len(dq_refs), mine, r)
        dq_ref[...] = paired(text_scr[0, at, :], text_scr[1, at, :])
    dq = paired(sum_scr[0], sum_scr[1])
    weight_ref[...] = lax.dot_general(
        dq, text_ref[...], (((0,), (0,)), ((), ())), preferred_element_type=jnp.float32
    )


def gather_last_kernel(
    length,
    images_here,
    place_ref,
    neg_ref,
    rank_ref,
    text_ref,
    own_ref,
    back_ref,
    head_ref,
    *rest,
):
    keep_ref, give_ref, _, sum_scr, text_scr, cut_scr = rest[-6:]
    members = len(rest) // 2 - 3
    dq_refs = rest[-6 - members : -6]
    mine = dq_refs[0].shape[0]
    sum_requests(
        1, length, images_here, neg_ref, rank_ref, own_ref, back_ref, sum_scr, text_scr, mine // length
    )
    for r, dq_ref in enumerate(dq_refs):
        at = by_distance(place_ref[0], members, mine, r)
        dq_ref[...] = text_scr[0, at, :].astype(jnp.bfloat16)
    dq = sum_scr[0].astype(jnp.bfloat16)
    last = lax.dot_general(
        dq, text_ref[...], (((0,), (0,)), ((), ())), preferred_element_type=jnp.float32
    )
    half = cut_scr.shape[3]
    before = head_ref.shape[0] // 8
    blocks = before + HEAD_SIZE // 8
    for b in range(blocks):
        rows = head_ref[b * 8 : b * 8 + 8, :] if b < before else last[(b - before) * 8 : (b - before) * 8 + 8]
        for side in range(2):
            cut_scr[2 * b // blocks, 2 * b % blocks + side] = rows[:, side * half : (side + 1) * half]
    core = place_ref[1]
    keep_ref[...] = cut_scr[core]
    give_ref[...] = cut_scr[1 - core].astype(jnp.bfloat16)


def pair_kernel(keep_ref, got_ref, *rest):
    out_ref = rest[len(rest) // 2]
    pieces = keep_ref.shape[0]
    out_ref[:pieces] = (keep_ref[...] + got_ref[...].astype(jnp.float32)).astype(jnp.bfloat16)


def total_kernel(parts_ref, *rest):
    out_ref = rest[-1]
    total = parts_ref[0].astype(jnp.float32)
    for d in range(1, parts_ref.shape[0]):
        total = total + parts_ref[d].astype(jnp.float32)
    total = total.astype(jnp.bfloat16)
    for d in range(out_ref.shape[0]):
        out_ref[d] = total


def unfold_kernel(core_ref, mine_ref, other_ref, out_ref):
    half = mine_ref.shape[2]
    rows = out_ref.shape[0] // 2
    for which, ref in ((core_ref[0], mine_ref), (1 - core_ref[0], other_ref)):
        for b in range(rows // 8):
            at = pl.ds(pl.multiple_of(which * rows + b * 8, 8), 8)
            for side in range(2):
                out_ref[at, side * half : (side + 1) * half] = ref[2 * b + side].astype(jnp.float32)


def text_kernel(width, wides, member_ref, weight_ref, *refs):
    rows, out_ref = refs[:-1], refs[-1]
    members = len(rows) // len(wides)
    total = jnp.zeros(out_ref.shape, jnp.float32)
    for r in range(members):
        source = lax.rem(member_ref[0] + members - r, members)
        skip = 0
        for group, wide in enumerate(wides):
            at = pl.ds(pl.multiple_of(source * width + skip, HEAD_SIZE), wide)
            total = total + jnp.dot(
                rows[group * members + r][:, :wide],
                weight_ref[at, :],
                preferred_element_type=jnp.float32,
            )
            skip += wide
    out_ref[...] = total.astype(jnp.bfloat16)


def params(limit=VMEM_LIMIT):
    return pltpu.CompilerParams(vmem_limit_bytes=limit)


def cost(us):
    return pl.CostEstimate(
        flops=int(us * 1e6 * 1150 / 2), bytes_accessed=int(us * 1e-6 * 3.6e12), transcendentals=0
    )


SMEM = pl.BlockSpec(memory_space=pltpu.SMEM)
VMEM = pl.BlockSpec(memory_space=pltpu.VMEM)
ANY = pl.BlockSpec(memory_space=pl.ANY)


def math_scratch(padded, ways):
    return [pltpu.VMEM((2 * padded, TILE), jnp.float32)] * ways + [
        pltpu.VMEM((padded, 2 * TILE), jnp.bfloat16)
    ] * ways


def far_call(plan, wire, first, many, both, kkt, own_acc, dkv, keys, us, length):
    owners, rows, _ = wire.shape
    images, all_heads, padded, _ = own_acc.shape
    more = () if dkv is None else (dkv,)
    back_rows = cdiv(many * length, 8) * 8
    most = (2 * owners * length) // TILE + images + WAYS - 1
    return pl.pallas_call(
        functools.partial(far_kernel, keys, padded, length, many),
        grid=(many,),
        in_specs=[
            SMEM,
            pl.BlockSpec((owners, rows, LANES), lambda h: (0, 0, 0)),
            pl.BlockSpec((images, 1, 2 * padded, LANES), lambda h: (0, first + h, 0, 0)),
            pl.BlockSpec((images, 1, LANES, padded), lambda h: (0, first + h, 0, 0)),
            pl.BlockSpec((images, 1, padded, LANES), lambda h: (0, first + h, 0, 0)),
        ]
        + [ANY] * len(more),
        out_specs=[
            pl.BlockSpec((images, 1, keys, LANES), lambda h: (0, first + h, 0, 0)),
            pl.BlockSpec((owners, back_rows, LANES), lambda h: (0, 0, 0)),
        ],
        out_shape=[
            jax.ShapeDtypeStruct((images, all_heads, keys, LANES), jnp.bfloat16),
            jax.ShapeDtypeStruct((owners, back_rows, LANES), jnp.bfloat16),
        ],
        scratch_shapes=[
            pltpu.VMEM((many, most * TILE + 64, LANES), jnp.float32),
            pltpu.VMEM((images, padded, LANES), jnp.float32),
        ]
        + math_scratch(padded, WAYS),
        input_output_aliases={5: 0} if more else {},
        compiler_params=params(),
        cost_estimate=cost(us),
        name="far" + str(first),
    )(plan, wire, both, kkt, own_acc, *more)


def exchange(x, groups=None):
    return lax.all_to_all(
        x, "dp", split_axis=0, concat_axis=0, axis_index_groups=groups, tiled=True
    )


def per_device(texts, query_weight, patch_key_value, grad_out, negatives):
    owners = lax.axis_size("dp")
    members = lax.axis_size("mp")
    member = lax.axis_index("mp")
    texts_here, length, depth = texts.shape
    images_here, heads, keys, _ = patch_key_value.shape
    width = query_weight.shape[0]
    captions = texts_here // images_here
    padded = cdiv(keys, 16) * 16
    count = texts_here * length
    bf16, f32, i32 = jnp.bfloat16, jnp.float32, jnp.int32
    early = heads - 1
    first_rows = cdiv(2 * early * length + 2, 8) * 8
    later_rows = cdiv(2 * length, 8) * 8

    flat_text = texts.transpose(1, 0, 2).reshape(count, depth)
    neg = negatives.T
    all_weight = lax.all_gather(query_weight, "mp", axis=0, tiled=True)
    start_col = member * width // LANES * LANES
    odd = ((member * width - start_col) // HEAD_SIZE).reshape(1).astype(i32)
    window = lax.dynamic_slice_in_dim(grad_out, start_col, 2 * LANES, 3)

    wire_first, query, rank = pl.pallas_call(
        functools.partial(pack_first_kernel, early, images_here),
        in_specs=[SMEM, SMEM, VMEM, VMEM, ANY],
        out_specs=[ANY, ANY, SMEM],
        out_shape=[
            jax.ShapeDtypeStruct((owners, first_rows, LANES), bf16),
            jax.ShapeDtypeStruct((heads, count, LANES), f32),
            jax.ShapeDtypeStruct(neg.shape, i32),
        ],
        scratch_shapes=[
            pltpu.VMEM((owners * first_rows, LANES), f32),
            pltpu.VMEM(window.shape, bf16),
            pltpu.VMEM((heads, count, LANES), f32),
            pltpu.VMEM((owners, first_rows, LANES), bf16),
            pltpu.SMEM((owners,), i32),
            pltpu.SemaphoreType.DMA((2 + PARTS,)),
        ],
        compiler_params=params(),
        cost_estimate=cost(5),
        name="pack_first",
    )(odd, neg, flat_text, query_weight, window)
    got_first = exchange(wire_first)

    own_acc, own_dq, both, kkt = pl.pallas_call(
        functools.partial(own_kernel, keys, padded, texts_here),
        grid=(images_here, heads),
        in_specs=[
            SMEM,
            pl.BlockSpec((1, count, LANES), lambda i, h: (h, 0, 0)),
            pl.BlockSpec((captions, 1, length, 2 * LANES), lambda i, h: (i, 0, 0, 0)),
            pl.BlockSpec((1, 1, keys, LANES), lambda i, h: (i, h, 0, 0)),
        ],
        out_specs=[
            pl.BlockSpec((1, 1, padded, LANES), lambda i, h: (i, h, 0, 0)),
            pl.BlockSpec((1, 1, TILE, LANES), lambda i, h: (i, h, 0, 0)),
            pl.BlockSpec((1, 1, 2 * padded, LANES), lambda i, h: (i, h, 0, 0)),
            pl.BlockSpec((1, 1, LANES, padded), lambda i, h: (i, h, 0, 0)),
        ],
        out_shape=[
            jax.ShapeDtypeStruct((images_here, heads, padded, LANES), f32),
            jax.ShapeDtypeStruct((images_here, heads, TILE, LANES), f32),
            jax.ShapeDtypeStruct((images_here, heads, 2 * padded, LANES), bf16),
            jax.ShapeDtypeStruct((images_here, heads, LANES, padded), bf16),
        ],
        scratch_shapes=[pltpu.VMEM((TILE, LANES), f32)] + math_scratch(padded, 1),
        compiler_params=params(),
        cost_estimate=cost(13),
        name="own",
    )(odd, query, window, patch_key_value)

    wire_later = pl.pallas_call(
        functools.partial(pack_later_kernel, early, heads - early, images_here),
        in_specs=[SMEM, SMEM, SMEM, VMEM, VMEM, ANY],
        out_specs=VMEM,
        out_shape=jax.ShapeDtypeStruct((owners, later_rows, LANES), bf16),
        scratch_shapes=[pltpu.VMEM((owners * later_rows, LANES), f32)],
        compiler_params=params(),
        cost_estimate=cost(4),
        name="pack_later",
    )(odd, neg, rank, query, window, own_acc)
    got_later = exchange(wire_later)

    tell = 2 * early * length
    plan = pl.pallas_call(
        functools.partial(plan_kernel, length, images_here, tell),
        in_specs=[ANY],
        out_specs=VMEM,
        out_shape=jax.ShapeDtypeStruct((owners + 8, LANES), i32),
        scratch_shapes=[
            pltpu.VMEM((owners, first_rows - tell // 16 * 16, LANES), bf16),
            pltpu.SemaphoreType.DMA,
        ],
        compiler_params=params(),
        cost_estimate=cost(2),
        name="plan",
    )(got_first)

    dkv, back_first = far_call(
        plan, got_first, 0, early, both, kkt, own_acc, None, keys, 22, length
    )
    home_first = exchange(back_first)
    dkv, back_later = far_call(
        plan, got_later, early, heads - early, both, kkt, own_acc, dkv, keys, 12, length
    )
    home_later = exchange(back_later)

    half = depth // 2
    cut = width // 8
    core = lax.rem(lax.axis_index("dp"), 2).reshape(1).astype(i32)
    place = jnp.concatenate([member.reshape(1).astype(i32), core])
    chips = [list(range(c, owners, 2)) for c in range(2)]
    partner = [(d, d ^ 1) for d in range(owners)]
    mine = texts_here // members
    block = jax.ShapeDtypeStruct((mine * length, LANES), bf16)
    *dq_first, weight_first = pl.pallas_call(
        functools.partial(gather_two_kernel, length, images_here),
        grid=(1,),
        in_specs=[
            SMEM,
            SMEM,
            SMEM,
            VMEM,
            pl.BlockSpec((images_here, early, TILE, LANES), lambda n: (0, 0, 0, 0)),
            VMEM,
        ],
        out_specs=[VMEM] * (members + 1),
        out_shape=[block] * members
        + [jax.ShapeDtypeStruct((early * HEAD_SIZE, depth), f32)],
        scratch_shapes=[pltpu.VMEM((early, count, LANES), f32)] * 2,
        compiler_params=params(),
        cost_estimate=cost(4),
        name="gather_two",
    )(place, neg, rank, flat_text, own_dq, home_first)
    def swap(dq):
        rows = [dq[0]]
        for r in range(1, members):
            pairs = [(i, (i + r) % members) for i in range(members)]
            rows.append(lax.ppermute(dq[r], "mp", pairs))
        return rows

    rows_first = swap(dq_first)
    dkv = dkv.transpose(1, 2, 0, 3)
    *dq_later, keep, give, dkv = pl.pallas_call(
        functools.partial(gather_last_kernel, length, images_here),
        grid=(1,),
        in_specs=[
            SMEM,
            SMEM,
            SMEM,
            VMEM,
            pl.BlockSpec((images_here, 1, TILE, LANES), lambda n: (0, early, 0, 0)),
            VMEM,
            VMEM,
        ]
        + [ANY] * members,
        out_specs=[VMEM] * (members + 2) + [ANY],
        out_shape=[block] * members
        + [
            jax.ShapeDtypeStruct((cut, 8, half), f32),
            jax.ShapeDtypeStruct((cut, 8, half), bf16),
            jax.ShapeDtypeStruct(dkv.shape, bf16),
        ],
        input_output_aliases={6 + members: members + 2},
        scratch_shapes=[pltpu.VMEM((1, count, LANES), f32)] * 2
        + [pltpu.VMEM((2, cut, 8, half), f32)],
        compiler_params=params(),
        cost_estimate=cost(3),
        name="gather_last",
    )(place, neg, rank, flat_text, own_dq, home_later, weight_first, *rows_first[1:], dkv)
    dkv = dkv.transpose(2, 0, 1, 3)

    got = lax.ppermute(give, "dp", partner)
    summed, *dq_later = pl.pallas_call(
        pair_kernel,
        in_specs=[VMEM, VMEM] + [ANY] * members,
        out_specs=[VMEM] + [ANY] * members,
        out_shape=[jax.ShapeDtypeStruct((owners // 2, 8, half), bf16)]
        + [block] * members,
        input_output_aliases={2 + n: 1 + n for n in range(members)},
        compiler_params=params(SMALL_LIMIT),
        cost_estimate=cost(2),
        name="pair",
    )(keep, got, *dq_later)
    parts = exchange(summed, chips)
    rows_later = swap(dq_later)
    piece = pl.pallas_call(
        total_kernel,
        in_specs=[VMEM] + [ANY] * (members - 1),
        out_specs=VMEM,
        out_shape=jax.ShapeDtypeStruct(parts.shape, bf16),
        compiler_params=params(),
        cost_estimate=cost(2),
        name="total",
    )(parts, *rows_later[1:])
    text_grad = pl.pallas_call(
        functools.partial(text_kernel, width, (early * HEAD_SIZE, (heads - early) * HEAD_SIZE)),
        in_specs=[SMEM] + [VMEM] * (1 + 2 * members),
        out_specs=VMEM,
        out_shape=jax.ShapeDtypeStruct((length * mine, depth), bf16),
        compiler_params=params(),
        cost_estimate=cost(3),
        name="text",
    )(member.reshape(1).astype(i32), all_weight, *rows_first, *rows_later)
    text_grad = text_grad.reshape(length, mine, depth)
    pieces, text_grad = pl.pallas_call(
        lambda *refs: None,
        in_specs=[ANY, ANY],
        out_specs=[ANY, ANY],
        out_shape=[
            jax.ShapeDtypeStruct(piece.shape, bf16),
            jax.ShapeDtypeStruct(text_grad.shape, bf16),
        ],
        input_output_aliases={0: 0, 1: 1},
        cost_estimate=cost(1),
        name="order",
    )(exchange(piece, chips), text_grad)
    text_grad = text_grad.transpose(1, 0, 2)
    weight_grad = pl.pallas_call(
        unfold_kernel,
        in_specs=[SMEM, VMEM, VMEM],
        out_specs=VMEM,
        out_shape=jax.ShapeDtypeStruct((width, depth), f32),
        compiler_params=params(SMALL_LIMIT),
        cost_estimate=cost(2),
        name="unfold",
    )(core, pieces, lax.ppermute(pieces, "dp", partner))

    return (text_grad, weight_grad, dkv)


def solution(mesh):
    in_specs = (
        P("dp", None, None),
        P("mp", None),
        P("dp", "mp", None, None),
        P("dp", None, None, None),
        P("dp", None),
    )
    out_specs = (P(("dp", "mp"), None, None), P("mp", None), P("dp", "mp", None, None))
    return jax.shard_map(
        per_device, mesh=mesh, in_specs=in_specs, out_specs=out_specs, check_vma=False
    )
```

```python
import functools

import jax
import jax.numpy as jnp
from jax import lax
from jax.experimental import pallas as pl
from jax.experimental.pallas import tpu as pltpu
from jax.sharding import PartitionSpec as P

HEAD_SIZE = 64
NEG = 3
LANES = 128
TILE = 256
WAYS = 4
PARTS = 4

VMEM_LIMIT = 60 * 1024 * 1024
SMALL_LIMIT = 16 * 1024 * 1024


def cdiv(a, b):
    return -(-a // b)


def lower_half(shape):
    return lax.broadcasted_iota(jnp.int32, shape, len(shape) - 1) < HEAD_SIZE


def request_slots(neg_ref, rank_ref, seen_ref, owners, images_here):
    negatives, texts_here = neg_ref.shape

    def clear(o, carry):
        seen_ref[o] = 0
        return carry

    lax.fori_loop(0, owners, clear, 0)

    def count(t, carry):
        for j in range(negatives):
            o = neg_ref[j, t] // images_here
            c = seen_ref[o]
            rank_ref[j, t] = c
            seen_ref[o] = c + 1
        return carry

    lax.fori_loop(0, texts_here, count, 0)


def joined(g, odd, q):
    g = g.astype(jnp.float32)
    g = jnp.where(odd == 1, g, pltpu.roll(g, HEAD_SIZE, 1))
    return jnp.where(lower_half(g.shape), q, g)


def project(text_ref, weight_ref, query_ref):
    q = lax.dot_general(
        text_ref[...], weight_ref[...], (((1,), (1,)), ((), ())), preferred_element_type=jnp.float32
    )
    q = q.astype(jnp.bfloat16).astype(jnp.float32) * HEAD_SIZE**-0.5
    for h in range(query_ref.shape[0]):
        if h % 2:
            a = (h - 1) * HEAD_SIZE
            query_ref[h] = pltpu.roll(q[:, a : a + LANES], HEAD_SIZE, 1)
        elif (h + 2) * HEAD_SIZE <= q.shape[1]:
            query_ref[h] = q[:, h * HEAD_SIZE : (h + 2) * HEAD_SIZE]
        else:
            query_ref[h, :, :HEAD_SIZE] = q[:, h * HEAD_SIZE :]
            query_ref[h, :, HEAD_SIZE:] = jnp.zeros((q.shape[0], HEAD_SIZE), jnp.float32)


def place_rows(
    first, heads, images_here, odd_ref, neg_ref, rank_ref, query_ref, grad_ref, wire_rows, scr
):
    texts_here, slots, length, _ = grad_ref.shape
    tells = wire_rows >= 2 * heads * length + 2
    if tells:
        for o in range(scr.shape[0] // wire_rows):
            scr[(o + 1) * wire_rows - 8 : (o + 1) * wire_rows, :] = jnp.full(
                (8, LANES), -1.0, jnp.float32
            )

    def one_text(t, carry):
        for h in range(heads):
            q = query_ref[first + h, pl.ds(t, length, stride=texts_here), :]
            place = odd_ref[0] + first + h
            col = pl.multiple_of((place // 2) * LANES, LANES)
            for j in range(slots - 1):
                n = neg_ref[j, t]
                r = rank_ref[j, t]
                o = n // images_here
                row = o * wire_rows + (r * heads + h) * length
                g = grad_ref[t, j + 1, :, pl.ds(col, LANES)]
                scr[pl.ds(row, length), :] = joined(g, lax.rem(place, 2), q)
                if h == 0 and tells:
                    tell = o * wire_rows + 2 * heads * length + r
                    image = (n - o * images_here).astype(jnp.float32)
                    scr[pl.ds(tell, 1), :] = jnp.full((1, LANES), image, jnp.float32)
        return carry

    lax.fori_loop(0, texts_here, one_text, 0, unroll=2)


def pack_first_kernel(
    heads,
    images_here,
    odd_ref,
    neg_ref,
    text_ref,
    weight_ref,
    grad_hbm,
    wire_hbm,
    query_hbm,
    rank_ref,
    scr,
    grad_scr,
    query_scr,
    wire_scr,
    seen_ref,
    sems,
):
    load = pltpu.make_async_copy(grad_hbm, grad_scr, sems.at[0])
    load.start()
    request_slots(neg_ref, rank_ref, seen_ref, wire_scr.shape[0], images_here)
    project(text_ref, weight_ref, query_scr)
    keep = pltpu.make_async_copy(query_scr, query_hbm, sems.at[1])
    keep.start()
    load.wait()
    place_rows(
        0, heads, images_here, odd_ref, neg_ref, rank_ref, query_scr, grad_scr, wire_scr.shape[1], scr
    )
    owners, rows, _ = wire_scr.shape
    part = owners // PARTS
    sends = []
    for p in range(PARTS):
        block = scr[p * part * rows : (p + 1) * part * rows, :]
        wire_scr[p * part : (p + 1) * part] = block.reshape(part, rows, LANES).astype(jnp.bfloat16)
        send = pltpu.make_async_copy(
            wire_scr.at[pl.ds(p * part, part)], wire_hbm.at[pl.ds(p * part, part)], sems.at[2 + p]
        )
        send.start()
        sends.append(send)
    keep.wait()
    for send in sends:
        send.wait()


def pack_later_kernel(
    first, heads, images_here, odd_ref, neg_ref, rank_ref, query_ref, grad_ref, after_ref, wire_ref, scr
):
    place_rows(
        first, heads, images_here, odd_ref, neg_ref, rank_ref, query_ref, grad_ref, wire_ref.shape[1], scr
    )
    wire_ref[...] = scr[...].reshape(wire_ref.shape).astype(jnp.bfloat16)


def load_memory(kv, keys, kv_ref, kkt_ref, padded):
    full = jnp.concatenate([kv, jnp.zeros((padded - keys, LANES), jnp.float32)], axis=0)
    low = lower_half(full.shape)
    k_only = jnp.where(low, full, 0.0)
    kv_ref[:padded, :] = k_only.astype(jnp.bfloat16)
    kv_ref[padded:, :] = jnp.where(low, 0.0, full).astype(jnp.bfloat16)
    twice = k_only + pltpu.roll(k_only, HEAD_SIZE, 1)
    kkt_ref[...] = twice.T.astype(jnp.bfloat16)


def tile_scores(qg, kv, s_scr):
    s_scr[...] = lax.dot_general(
        kv, qg, (((1,), (1,)), ((), ())), preferred_element_type=jnp.float32
    )


def tile_softmax(keys, padded, s_scr, pd_scr):
    tile = s_scr.shape[1]
    bounds = list(range(0, padded, 64)) + [padded]
    chunks = list(zip(bounds[:-1], bounds[1:]))
    top = jnp.full((8, tile), -jnp.inf, jnp.float32)
    for a, b in chunks:
        s = s_scr[a:b, :]
        if b > keys:
            row = lax.broadcasted_iota(jnp.int32, s.shape, 0) + a
            s = jnp.where(row < keys, s, -jnp.inf)
            s_scr[a:b, :] = s
        top = jnp.maximum(top, jnp.max(s.reshape((b - a) // 8, 8, tile), axis=0))
    top = jnp.max(top, axis=0, keepdims=True)
    total = jnp.zeros((8, tile), jnp.float32)
    center = jnp.zeros((8, tile), jnp.float32)
    for a, b in chunks:
        e = jnp.exp(s_scr[a:b, :] - top)
        s_scr[a:b, :] = e
        total = total + jnp.sum(e.reshape((b - a) // 8, 8, tile), axis=0)
        d = e * s_scr[padded + a : padded + b, :]
        center = center + jnp.sum(d.reshape((b - a) // 8, 8, tile), axis=0)
    inverse = 1.0 / jnp.sum(total, axis=0, keepdims=True)
    center = jnp.sum(center, axis=0, keepdims=True) * inverse
    for a, b in chunks:
        p = s_scr[a:b, :] * inverse
        pd_scr[a:b, tile:] = p.astype(jnp.bfloat16)
        ds = p * (s_scr[padded + a : padded + b, :] - center)
        pd_scr[a:b, :tile] = ds.astype(jnp.bfloat16)


def tile_outputs(qg, kkt, pd_scr):
    tile = qg.shape[0]
    low = lower_half(qg.shape)
    zero = jnp.zeros_like(qg)
    both = jnp.concatenate([jnp.where(low, qg, zero), jnp.where(low, zero, qg)], axis=0)
    dkv = jnp.dot(pd_scr[...], both, preferred_element_type=jnp.float32)
    dqt = jnp.dot(kkt, pd_scr[:, :tile], preferred_element_type=jnp.float32)
    return dqt.T * (HEAD_SIZE**-0.5), dkv


def own_kernel(
    keys, padded, texts_here, odd_ref, query_ref, grad_ref, kv_ref, acc_ref, dq_ref, both_ref, kkt_ref, own_scr, s_scr, pd_scr
):
    image, h = pl.program_id(0), pl.program_id(1)
    captions, _, length, _ = grad_ref.shape
    load_memory(kv_ref[0, 0].astype(jnp.float32), keys, both_ref.at[0, 0], kkt_ref.at[0, 0], padded)
    place = odd_ref[0] + h
    col = pl.multiple_of((place // 2) * LANES, LANES)
    own_scr[captions * length :, :] = jnp.zeros((TILE - captions * length, LANES), jnp.float32)
    for c in range(captions):
        q = query_ref[0, pl.ds(image * captions + c, length, stride=texts_here), :]
        g = grad_ref[c, 0, :, pl.ds(col, LANES)]
        own_scr[c * length : (c + 1) * length, :] = joined(g, lax.rem(place, 2), q)
    qg = own_scr[...].astype(jnp.bfloat16)
    tile_scores(qg, both_ref[0, 0], s_scr)
    tile_softmax(keys, padded, s_scr, pd_scr)
    dq, dkv = tile_outputs(qg, kkt_ref[0, 0], pd_scr)
    acc_ref[0, 0] = dkv
    dq_ref[0, 0] = dq


def plan_kernel(length, images, tell, wire_hbm, plan_ref, tail_scr, sem):
    senders, rows, _ = tail_scr.shape
    first = tell // 16 * 16
    copy = pltpu.make_async_copy(wire_hbm.at[:, pl.ds(first, rows), :], tail_scr, sem)
    copy.start()
    copy.wait()
    tail = tail_scr[...].astype(jnp.float32)
    id0, id1 = tail[:, tell - first, :], tail[:, tell - first + 1, :]
    lane = lax.broadcasted_iota(jnp.int32, (senders, LANES), 1)
    image = lane.astype(jnp.float32)
    hot0 = jnp.where(id0 == image, 1.0, 0.0)
    hot1 = jnp.where(id1 == image, 1.0, 0.0)
    both = hot0 + hot1
    row = lax.broadcasted_iota(jnp.int32, (senders, senders), 0)
    col = lax.broadcasted_iota(jnp.int32, (senders, senders), 1)
    before = jnp.where(col < row, 1.0, 0.0).astype(jnp.bfloat16)
    ahead = jnp.dot(before, both.astype(jnp.bfloat16), preferred_element_type=jnp.float32)
    number = jnp.sum(both, axis=0, keepdims=True).astype(jnp.int32)
    tiles = (number * length + (TILE - 1)) // TILE
    tiles = jnp.broadcast_to(tiles, (8, LANES))
    row = lax.broadcasted_iota(jnp.int32, (LANES, LANES), 0)
    col = lax.broadcasted_iota(jnp.int32, (LANES, LANES), 1)
    before = jnp.where(row < col, 1.0, 0.0).astype(jnp.bfloat16)
    first_tile = jnp.dot(
        tiles.astype(jnp.float32).astype(jnp.bfloat16), before, preferred_element_type=jnp.float32
    )
    at = first_tile[0:1] * TILE + ahead * length
    pos0 = jnp.sum(hot0 * at, axis=1, keepdims=True)
    pos1 = jnp.sum(hot1 * (at + hot0 * length), axis=1, keepdims=True)
    pos0 = jnp.where(id0 >= 0, pos0, -1.0)
    pos1 = jnp.where(id1 >= 0, pos1, -1.0)
    plan_ref[:senders, :] = jnp.where(lane == 0, pos0, pos1).astype(jnp.int32)
    low = lax.broadcasted_iota(jnp.int32, (8, LANES), 0)
    plan_ref[senders:, :] = jnp.where(low == 0, first_tile.astype(jnp.int32), tiles)


def far_kernel(
    keys,
    padded,
    length,
    heads,
    plan_ref,
    wire_ref,
    both_ref,
    kkt_ref,
    own_ref,
    *rest,
):
    h = pl.program_id(0)
    images = both_ref.shape[0]
    senders = wire_ref.shape[0]
    dkv_ref, back_ref, rows_scr, acc_scr = rest[-4 - 2 * WAYS : -2 * WAYS]
    pairs = rest[-2 * WAYS :]
    ways = WAYS
    s_scrs, pd_scrs = pairs[:ways], pairs[ways:]

    @pl.when(h == 0)
    def _():
        def clear(start):
            for g in range(heads):
                rows_scr[g, pl.ds(pl.multiple_of(start, TILE), TILE), :] = jnp.zeros(
                    (TILE, LANES), jnp.float32
                )

        for i in range(images):
            n = plan_ref[senders + 1, i]

            @pl.when(n > 0)
            def _():
                clear((plan_ref[senders, i] + n - 1) * TILE)

        end = plan_ref[senders, images - 1] + plan_ref[senders + 1, images - 1]
        for w in range(ways - 1):
            clear((end + w) * TILE)

        def place(s, carry):
            block = wire_ref[s].astype(jnp.float32)
            for r in range(2):
                pos = plan_ref[s, r]

                @pl.when(pos >= 0)
                def _():
                    for g in range(heads):
                        a = (r * heads + g) * length
                        rows_scr[g, pl.ds(pos, length), :] = block[a : a + length]

            return carry

        lax.fori_loop(0, senders, place, 0, unroll=4)

    for i in range(images):
        acc_scr[i] = own_ref[i, 0]
    edges = [plan_ref[senders, i] for i in range(1, images)]
    tiles = plan_ref[senders, images - 1] + plan_ref[senders + 1, images - 1]

    def step(k, carry):
        starts, images_of, rows = [], [], []
        for w in range(ways):
            n = k * ways + w
            image = jnp.int32(0)
            for e in edges:
                image = image + (n >= e).astype(jnp.int32)
            start = pl.multiple_of(n * TILE, TILE)
            qg = rows_scr[h, pl.ds(start, TILE), :].astype(jnp.bfloat16)
            starts.append(start)
            images_of.append(image)
            rows.append(qg)
            tile_scores(qg, both_ref[image, 0], s_scrs[w])
        for w in range(ways):
            tile_softmax(keys, padded, s_scrs[w], pd_scrs[w])
            dq, dkv = tile_outputs(rows[w], kkt_ref[images_of[w], 0], pd_scrs[w])
            acc_scr[images_of[w]] += dkv
            rows_scr[h, pl.ds(starts[w], TILE), :] = dq
        return carry

    lax.fori_loop(0, (tiles + ways - 1) // ways, step, 0)
    for i in range(images):
        dkv_ref[i, 0] = acc_scr[i, :keys, :].astype(jnp.bfloat16)

    @pl.when(h == heads - 1)
    def _():
        rows = back_ref.shape[1]
        low = lower_half((length, LANES))
        spare = rows - heads * length

        def give(s, carry):
            p0 = jnp.maximum(plan_ref[s, 0], 0)
            p1 = jnp.maximum(plan_ref[s, 1], 0)
            parts = []
            for g in range(heads):
                x0 = rows_scr[g, pl.ds(p0, length), :]
                x1 = rows_scr[g, pl.ds(p1, length), :]
                parts.append(jnp.where(low, x0, x1))
            if spare:
                parts.append(jnp.zeros((spare, LANES), jnp.float32))
            back_ref[s] = jnp.concatenate(parts, axis=0).astype(jnp.bfloat16)
            return carry

        lax.fori_loop(0, senders, give, 0, unroll=4)


def sum_requests(heads, length, images_here, neg_ref, rank_ref, own_ref, back_ref, sum_scr, text_scr, per):
    texts_here = sum_scr.shape[1] // length
    captions = texts_here // images_here

    def one(t, carry):
        image = t // captions
        totals = [
            own_ref[image, h, pl.ds((t - image * captions) * length, length), :]
            for h in range(heads)
        ]
        for j in range(NEG):
            block = back_ref[neg_ref[j, t] // images_here].astype(jnp.float32)
            block = jnp.where(rank_ref[j, t] == 1, pltpu.roll(block, HEAD_SIZE, 1), block)
            for h in range(heads):
                totals[h] = totals[h] + block[h * length : (h + 1) * length]
        for h in range(heads):
            sum_scr[h, pl.ds(t, length, stride=texts_here), :] = totals[h]
            at = t // per * (per * length) + lax.rem(t, per)
            text_scr[h, pl.ds(at, length, stride=per), :] = totals[h]
        return carry

    lax.fori_loop(0, texts_here, one, 0, unroll=2)


def by_distance(member, members, mine, r):
    return pl.ds(lax.rem(member + r, members) * mine, mine)


def paired(x0, x1):
    x = jnp.where(lower_half(x0.shape), x0, pltpu.roll(x1, HEAD_SIZE, 1))
    return x.astype(jnp.bfloat16)


def gather_two_kernel(
    length, images_here, member_ref, neg_ref, rank_ref, text_ref, own_ref, back_ref, *rest
):
    dq_refs, (weight_ref, sum_scr, text_scr) = rest[:-3], rest[-3:]
    mine = dq_refs[0].shape[0]
    sum_requests(
        2, length, images_here, neg_ref, rank_ref, own_ref, back_ref, sum_scr, text_scr, mine // length
    )
    for r, dq_ref in enumerate(dq_refs):
        at = by_distance(member_ref[0], len(dq_refs), mine, r)
        dq_ref[...] = paired(text_scr[0, at, :], text_scr[1, at, :])
    dq = paired(sum_scr[0], sum_scr[1])
    weight_ref[...] = lax.dot_general(
        dq, text_ref[...], (((0,), (0,)), ((), ())), preferred_element_type=jnp.float32
    )


def gather_last_kernel(
    length,
    images_here,
    place_ref,
    neg_ref,
    rank_ref,
    text_ref,
    own_ref,
    back_ref,
    head_ref,
    *rest,
):
    keep_ref, give_ref, _, sum_scr, text_scr, cut_scr = rest[-6:]
    members = len(rest) // 2 - 3
    dq_refs = rest[-6 - members : -6]
    mine = dq_refs[0].shape[0]
    sum_requests(
        1, length, images_here, neg_ref, rank_ref, own_ref, back_ref, sum_scr, text_scr, mine // length
    )
    for r, dq_ref in enumerate(dq_refs):
        at = by_distance(place_ref[0], members, mine, r)
        dq_ref[...] = text_scr[0, at, :].astype(jnp.bfloat16)
    dq = sum_scr[0].astype(jnp.bfloat16)
    last = lax.dot_general(
        dq, text_ref[...], (((0,), (0,)), ((), ())), preferred_element_type=jnp.float32
    )
    half = cut_scr.shape[3]
    before = head_ref.shape[0] // 8
    blocks = before + HEAD_SIZE // 8
    for b in range(blocks):
        rows = head_ref[b * 8 : b * 8 + 8, :] if b < before else last[(b - before) * 8 : (b - before) * 8 + 8]
        for side in range(2):
            cut_scr[2 * b // blocks, 2 * b % blocks + side] = rows[:, side * half : (side + 1) * half]
    core = place_ref[1]
    keep_ref[...] = cut_scr[core]
    give_ref[...] = cut_scr[1 - core].astype(jnp.bfloat16)


def pair_kernel(keep_ref, got_ref, *rest):
    out_ref = rest[len(rest) // 2]
    pieces = keep_ref.shape[0]
    out_ref[:pieces] = (keep_ref[...] + got_ref[...].astype(jnp.float32)).astype(jnp.bfloat16)


def total_kernel(parts_ref, *rest):
    out_ref = rest[-1]
    total = parts_ref[0].astype(jnp.float32)
    for d in range(1, parts_ref.shape[0]):
        total = total + parts_ref[d].astype(jnp.float32)
    total = total.astype(jnp.bfloat16)
    for d in range(out_ref.shape[0]):
        out_ref[d] = total


def unfold_kernel(core_ref, mine_ref, other_ref, out_ref):
    half = mine_ref.shape[2]
    rows = out_ref.shape[0] // 2
    for which, ref in ((core_ref[0], mine_ref), (1 - core_ref[0], other_ref)):
        for b in range(rows // 8):
            at = pl.ds(pl.multiple_of(which * rows + b * 8, 8), 8)
            for side in range(2):
                out_ref[at, side * half : (side + 1) * half] = ref[2 * b + side].astype(jnp.float32)


def text_kernel(width, wides, member_ref, weight_ref, *refs):
    rows, out_ref = refs[:-1], refs[-1]
    members = len(rows) // len(wides)
    total = jnp.zeros(out_ref.shape, jnp.float32)
    for r in range(members):
        source = lax.rem(member_ref[0] + members - r, members)
        skip = 0
        for group, wide in enumerate(wides):
            at = pl.ds(pl.multiple_of(source * width + skip, HEAD_SIZE), wide)
            total = total + jnp.dot(
                rows[group * members + r][:, :wide],
                weight_ref[at, :],
                preferred_element_type=jnp.float32,
            )
            skip += wide
    out_ref[...] = total.astype(jnp.bfloat16)


def params(limit=VMEM_LIMIT):
    return pltpu.CompilerParams(vmem_limit_bytes=limit)


def cost(us):
    return pl.CostEstimate(
        flops=int(us * 1e6 * 1150 / 2), bytes_accessed=int(us * 1e-6 * 3.6e12), transcendentals=0
    )


SMEM = pl.BlockSpec(memory_space=pltpu.SMEM)
VMEM = pl.BlockSpec(memory_space=pltpu.VMEM)
ANY = pl.BlockSpec(memory_space=pl.ANY)


def math_scratch(padded, ways):
    return [pltpu.VMEM((2 * padded, TILE), jnp.float32)] * ways + [
        pltpu.VMEM((padded, 2 * TILE), jnp.bfloat16)
    ] * ways


def far_call(plan, wire, first, many, both, kkt, own_acc, dkv, keys, us, length):
    owners, rows, _ = wire.shape
    images, all_heads, padded, _ = own_acc.shape
    more = () if dkv is None else (dkv,)
    back_rows = cdiv(many * length, 8) * 8
    most = (2 * owners * length) // TILE + images + WAYS - 1
    return pl.pallas_call(
        functools.partial(far_kernel, keys, padded, length, many),
        grid=(many,),
        in_specs=[
            SMEM,
            pl.BlockSpec((owners, rows, LANES), lambda h: (0, 0, 0)),
            pl.BlockSpec((images, 1, 2 * padded, LANES), lambda h: (0, first + h, 0, 0)),
            pl.BlockSpec((images, 1, LANES, padded), lambda h: (0, first + h, 0, 0)),
            pl.BlockSpec((images, 1, padded, LANES), lambda h: (0, first + h, 0, 0)),
        ]
        + [ANY] * len(more),
        out_specs=[
            pl.BlockSpec((images, 1, keys, LANES), lambda h: (0, first + h, 0, 0)),
            pl.BlockSpec((owners, back_rows, LANES), lambda h: (0, 0, 0)),
        ],
        out_shape=[
            jax.ShapeDtypeStruct((images, all_heads, keys, LANES), jnp.bfloat16),
            jax.ShapeDtypeStruct((owners, back_rows, LANES), jnp.bfloat16),
        ],
        scratch_shapes=[
            pltpu.VMEM((many, most * TILE + 64, LANES), jnp.float32),
            pltpu.VMEM((images, padded, LANES), jnp.float32),
        ]
        + math_scratch(padded, WAYS),
        input_output_aliases={5: 0} if more else {},
        compiler_params=params(),
        cost_estimate=cost(us),
        name="far" + str(first),
    )(plan, wire, both, kkt, own_acc, *more)


def exchange(x, groups=None):
    return lax.all_to_all(
        x, "dp", split_axis=0, concat_axis=0, axis_index_groups=groups, tiled=True
    )


def per_device(texts, query_weight, patch_key_value, grad_out, negatives):
    owners = lax.axis_size("dp")
    members = lax.axis_size("mp")
    member = lax.axis_index("mp")
    texts_here, length, depth = texts.shape
    images_here, heads, keys, _ = patch_key_value.shape
    width = query_weight.shape[0]
    captions = texts_here // images_here
    padded = cdiv(keys, 16) * 16
    count = texts_here * length
    bf16, f32, i32 = jnp.bfloat16, jnp.float32, jnp.int32
    early = heads - 1
    first_rows = cdiv(2 * early * length + 2, 8) * 8
    later_rows = cdiv(2 * length, 8) * 8

    flat_text = texts.transpose(1, 0, 2).reshape(count, depth)
    neg = negatives.T
    all_weight = lax.all_gather(query_weight, "mp", axis=0, tiled=True)
    start_col = member * width // LANES * LANES
    odd = ((member * width - start_col) // HEAD_SIZE).reshape(1).astype(i32)
    window = lax.dynamic_slice_in_dim(grad_out, start_col, 2 * LANES, 3)

    wire_first, query, rank = pl.pallas_call(
        functools.partial(pack_first_kernel, early, images_here),
        in_specs=[SMEM, SMEM, VMEM, VMEM, ANY],
        out_specs=[ANY, ANY, SMEM],
        out_shape=[
            jax.ShapeDtypeStruct((owners, first_rows, LANES), bf16),
            jax.ShapeDtypeStruct((heads, count, LANES), f32),
            jax.ShapeDtypeStruct(neg.shape, i32),
        ],
        scratch_shapes=[
            pltpu.VMEM((owners * first_rows, LANES), f32),
            pltpu.VMEM(window.shape, bf16),
            pltpu.VMEM((heads, count, LANES), f32),
            pltpu.VMEM((owners, first_rows, LANES), bf16),
            pltpu.SMEM((owners,), i32),
            pltpu.SemaphoreType.DMA((2 + PARTS,)),
        ],
        compiler_params=params(),
        cost_estimate=cost(5),
        name="pack_first",
    )(odd, neg, flat_text, query_weight, window)
    got_first = exchange(wire_first)

    own_acc, own_dq, both, kkt = pl.pallas_call(
        functools.partial(own_kernel, keys, padded, texts_here),
        grid=(images_here, heads),
        in_specs=[
            SMEM,
            pl.BlockSpec((1, count, LANES), lambda i, h: (h, 0, 0)),
            pl.BlockSpec((captions, 1, length, 2 * LANES), lambda i, h: (i, 0, 0, 0)),
            pl.BlockSpec((1, 1, keys, LANES), lambda i, h: (i, h, 0, 0)),
        ],
        out_specs=[
            pl.BlockSpec((1, 1, padded, LANES), lambda i, h: (i, h, 0, 0)),
            pl.BlockSpec((1, 1, TILE, LANES), lambda i, h: (i, h, 0, 0)),
            pl.BlockSpec((1, 1, 2 * padded, LANES), lambda i, h: (i, h, 0, 0)),
            pl.BlockSpec((1, 1, LANES, padded), lambda i, h: (i, h, 0, 0)),
        ],
        out_shape=[
            jax.ShapeDtypeStruct((images_here, heads, padded, LANES), f32),
            jax.ShapeDtypeStruct((images_here, heads, TILE, LANES), f32),
            jax.ShapeDtypeStruct((images_here, heads, 2 * padded, LANES), bf16),
            jax.ShapeDtypeStruct((images_here, heads, LANES, padded), bf16),
        ],
        scratch_shapes=[pltpu.VMEM((TILE, LANES), f32)] + math_scratch(padded, 1),
        compiler_params=params(),
        cost_estimate=cost(13),
        name="own",
    )(odd, query, window, patch_key_value)

    wire_later = pl.pallas_call(
        functools.partial(pack_later_kernel, early, heads - early, images_here),
        in_specs=[SMEM, SMEM, SMEM, VMEM, VMEM, ANY],
        out_specs=VMEM,
        out_shape=jax.ShapeDtypeStruct((owners, later_rows, LANES), bf16),
        scratch_shapes=[pltpu.VMEM((owners * later_rows, LANES), f32)],
        compiler_params=params(),
        cost_estimate=cost(4),
        name="pack_later",
    )(odd, neg, rank, query, window, own_acc)
    got_later = exchange(wire_later)

    tell = 2 * early * length
    plan = pl.pallas_call(
        functools.partial(plan_kernel, length, images_here, tell),
        in_specs=[ANY],
        out_specs=VMEM,
        out_shape=jax.ShapeDtypeStruct((owners + 8, LANES), i32),
        scratch_shapes=[
            pltpu.VMEM((owners, first_rows - tell // 16 * 16, LANES), bf16),
            pltpu.SemaphoreType.DMA,
        ],
        compiler_params=params(),
        cost_estimate=cost(2),
        name="plan",
    )(got_first)

    dkv, back_first = far_call(
        plan, got_first, 0, early, both, kkt, own_acc, None, keys, 22, length
    )
    home_first = exchange(back_first)
    dkv, back_later = far_call(
        plan, got_later, early, heads - early, both, kkt, own_acc, dkv, keys, 12, length
    )
    home_later = exchange(back_later)

    half = depth // 2
    cut = width // 8
    core = lax.rem(lax.axis_index("dp"), 2).reshape(1).astype(i32)
    place = jnp.concatenate([member.reshape(1).astype(i32), core])
    chips = [list(range(c, owners, 2)) for c in range(2)]
    partner = [(d, d ^ 1) for d in range(owners)]
    mine = texts_here // members
    block = jax.ShapeDtypeStruct((mine * length, LANES), bf16)
    *dq_first, weight_first = pl.pallas_call(
        functools.partial(gather_two_kernel, length, images_here),
        grid=(1,),
        in_specs=[
            SMEM,
            SMEM,
            SMEM,
            VMEM,
            pl.BlockSpec((images_here, early, TILE, LANES), lambda n: (0, 0, 0, 0)),
            VMEM,
        ],
        out_specs=[VMEM] * (members + 1),
        out_shape=[block] * members
        + [jax.ShapeDtypeStruct((early * HEAD_SIZE, depth), f32)],
        scratch_shapes=[pltpu.VMEM((early, count, LANES), f32)] * 2,
        compiler_params=params(),
        cost_estimate=cost(4),
        name="gather_two",
    )(place, neg, rank, flat_text, own_dq, home_first)
    def swap(dq):
        rows = [dq[0]]
        for r in range(1, members):
            pairs = [(i, (i + r) % members) for i in range(members)]
            rows.append(lax.ppermute(dq[r], "mp", pairs))
        return rows

    rows_first = swap(dq_first)
    dkv = dkv.transpose(1, 2, 0, 3)
    *dq_later, keep, give, dkv = pl.pallas_call(
        functools.partial(gather_last_kernel, length, images_here),
        grid=(1,),
        in_specs=[
            SMEM,
            SMEM,
            SMEM,
            VMEM,
            pl.BlockSpec((images_here, 1, TILE, LANES), lambda n: (0, early, 0, 0)),
            VMEM,
            VMEM,
        ]
        + [ANY] * members,
        out_specs=[VMEM] * (members + 2) + [ANY],
        out_shape=[block] * members
        + [
            jax.ShapeDtypeStruct((cut, 8, half), f32),
            jax.ShapeDtypeStruct((cut, 8, half), bf16),
            jax.ShapeDtypeStruct(dkv.shape, bf16),
        ],
        input_output_aliases={6 + members: members + 2},
        scratch_shapes=[pltpu.VMEM((1, count, LANES), f32)] * 2
        + [pltpu.VMEM((2, cut, 8, half), f32)],
        compiler_params=params(),
        cost_estimate=cost(3),
        name="gather_last",
    )(place, neg, rank, flat_text, own_dq, home_later, weight_first, *rows_first[1:], dkv)
    dkv = dkv.transpose(2, 0, 1, 3)

    got = lax.ppermute(give, "dp", partner)
    summed, *dq_later = pl.pallas_call(
        pair_kernel,
        in_specs=[VMEM, VMEM] + [ANY] * members,
        out_specs=[VMEM] + [ANY] * members,
        out_shape=[jax.ShapeDtypeStruct((owners // 2, 8, half), bf16)]
        + [block] * members,
        input_output_aliases={2 + n: 1 + n for n in range(members)},
        compiler_params=params(),
        cost_estimate=cost(2),
        name="pair",
    )(keep, got, *dq_later)
    parts = exchange(summed, chips)
    rows_later = swap(dq_later)
    piece = pl.pallas_call(
        total_kernel,
        in_specs=[VMEM] + [ANY] * (members - 1),
        out_specs=VMEM,
        out_shape=jax.ShapeDtypeStruct(parts.shape, bf16),
        compiler_params=params(),
        cost_estimate=cost(2),
        name="total",
    )(parts, *rows_later[1:])
    text_grad = pl.pallas_call(
        functools.partial(text_kernel, width, (early * HEAD_SIZE, (heads - early) * HEAD_SIZE)),
        in_specs=[SMEM] + [VMEM] * (1 + 2 * members),
        out_specs=VMEM,
        out_shape=jax.ShapeDtypeStruct((length * mine, depth), bf16),
        compiler_params=params(),
        cost_estimate=cost(3),
        name="text",
    )(member.reshape(1).astype(i32), all_weight, *rows_first, *rows_later)
    text_grad = text_grad.reshape(length, mine, depth)
    pieces, text_grad = pl.pallas_call(
        lambda *refs: None,
        in_specs=[ANY, ANY],
        out_specs=[ANY, ANY],
        out_shape=[
            jax.ShapeDtypeStruct(piece.shape, bf16),
            jax.ShapeDtypeStruct(text_grad.shape, bf16),
        ],
        input_output_aliases={0: 0, 1: 1},
        cost_estimate=cost(1),
        name="order",
    )(exchange(piece, chips), text_grad)
    text_grad = text_grad.transpose(1, 0, 2)
    weight_grad = pl.pallas_call(
        unfold_kernel,
        in_specs=[SMEM, VMEM, VMEM],
        out_specs=VMEM,
        out_shape=jax.ShapeDtypeStruct((width, depth), f32),
        compiler_params=params(SMALL_LIMIT),
        cost_estimate=cost(2),
        name="unfold",
    )(core, pieces, lax.ppermute(pieces, "dp", partner))

    return (text_grad, weight_grad, dkv)


def solution(mesh):
    in_specs = (
        P("dp", None, None),
        P("mp", None),
        P("dp", "mp", None, None),
        P("dp", None, None, None),
        P("dp", None),
    )
    out_specs = (P(("dp", "mp"), None, None), P("mp", None), P("dp", "mp", None, None))
    return jax.shard_map(
        per_device, mesh=mesh, in_specs=in_specs, out_specs=out_specs, check_vma=False
    )
```
